32 devices in a mesh: dp: 8 (over z, y), mp: 4 (over x, core).
Axes of the slice: x: 2, y: 2, z: 4, core: 2. Of those that a mesh axis runs over, the one named last changes fastest.
Arguments:
- stream: float32 [16384, 512], P('dp', 'mp'), may hold values from -6 to 6
- cotangent: float32 [16384, 512], P('dp', 'mp'), may hold values from -6 to 6
- start_offsets: int32 [8], P('dp'), may hold values from 0 to 2047, as said below
- norm_gain: float32 [2, 512], P(None, 'mp'), may hold values from 0.5 to 1.5
- norm_shift: float32 [2, 512], P(None, 'mp'), may hold values from -3 to 3
- input_map: bfloat16 [2, 512, 512], replicated, may hold values from -0.25 to 0.25
- decay_log: float32 [2, 256], replicated, may hold values from -9 to -2.5
- phase_log: float32 [2, 256], replicated, may hold values from -3 to 0.5
- scale_log: float32 [2, 256], replicated, may hold values from -4.7 to -0.4
- output_map: bfloat16 [2, 512, 512], P(None, None, 'mp'), may hold values from -0.25 to 0.25
- skip_gain: float32 [2, 512], P(None, 'mp'), may hold values from -4 to 4
- value_weight: bfloat16 [2, 512, 512], P(None, None, 'mp'), may hold values from -0.25 to 0.25
- gate_weight: bfloat16 [2, 512, 512], P(None, None, 'mp'), may hold values from -0.25 to 0.25
- value_bias: float32 [2, 512], P(None, 'mp'), may hold values from -3 to 3
- gate_bias: float32 [2, 512], P(None, 'mp'), may hold values from -3 to 3
Outputs:
- result: float32 [16384, 512], P('dp', 'mp')
- stream_grad: float32 [16384, 512], P('dp', 'mp')
- gain_grad: float32 [2, 512], P(None, 'mp')
- shift_grad: float32 [2, 512], P(None, 'mp')
- input_map_grad: float32 [2, 512, 512], replicated
- decay_grad: float32 [2, 256], replicated
- phase_grad: float32 [2, 256], replicated
- scale_grad: float32 [2, 256], replicated
- output_map_grad: float32 [2, 512, 512], P(None, None, 'mp')
- skip_grad: float32 [2, 512], P(None, 'mp')
- value_weight_grad: float32 [2, 512, 512], P(None, None, 'mp')
- gate_weight_grad: float32 [2, 512, 512], P(None, None, 'mp')
- value_bias_grad: float32 [2, 512], P(None, 'mp')
- gate_bias_grad: float32 [2, 512], P(None, 'mp')
The draws below stay inside these ranges and needn't reach their ends.
Inputs may be any that keep to these rules, and one draw needn't show every extreme that they name: `start_offsets`: only the first and the last token block have a nonzero entry, each of 1 to 2047, and one of the two is 2047; so one sequence runs from the first token block to the last.
All inputs are finite; a program needn't handle non-finite values.
Results may differ from the reference program's by a relative error of at most 0.019.
Values may be sent and summed in bfloat16 or wider, within the bound.
No kernel may reach another device: no remote copies, remote signals or barrier semaphores. Data moves between devices by JAX's collectives and lax.ppermute only.
A program may use at most 192 MiB of HBM per device.

```python
import jax
import jax.numpy as jnp
from jax import lax

D_MODEL = 512
STATES = 256
TOK_DEV = 2048
STRETCH = 64
LAYERS = 2
BLOCKS = 8
TOKENS = 16384


def decay_values(key):
    return jax.random.uniform(key, (LAYERS, STATES), jnp.float32, -9.0, -2.5)


def draw_decay_log(key, part):
    shared = decay_values(key)
    return shared


def draw_scale_log(key, part):
    shared = decay_values(key)
    key = jax.random.fold_in(key, 2)
    jitter = jax.random.uniform(key, (LAYERS, STATES), jnp.float32, -0.5, 0.5)
    radius_sq = jnp.exp(-2.0 * jnp.exp(shared))
    return 0.5 * jnp.log(1.0 - radius_sq) + jitter


def draw_start_offsets(key, part):
    key = jax.random.fold_in(key, 3)
    key_pick, key_other = jax.random.split(key)
    pick_first = jax.random.randint(key_pick, (), 0, 2)
    other_offset = jax.random.randint(key_other, (), 1, TOK_DEV)
    top_offset = jnp.int32(TOK_DEV - 1)
    first_offset = jnp.where(pick_first == 1, top_offset, other_offset)
    last_offset = jnp.where(pick_first == 1, other_offset, top_offset)
    block_index = jnp.arange(BLOCKS)
    return jnp.where(block_index == 0, first_offset, jnp.where(block_index == BLOCKS - 1, last_offset, 0)).astype(jnp.int32)


def block_levels(stream_key, dims, pieces, least, high):
    level, own = 1.0, jax.random.fold_in(stream_key, 6)
    for position, blocks in pieces:
        heights = jnp.exp(jax.random.uniform(jax.random.fold_in(own, position), (blocks,), jnp.float32, least / len(pieces), high / len(pieces)))
        level = level * jnp.repeat(heights, dims[position] // blocks).reshape([-1 if axis == position else 1 for axis in range(len(dims))])
    return level


def scatter_about(own_key, shape, scale, reach, pieces=(), held_as=jnp.bfloat16):
    array = scale * jax.random.normal(own_key, shape, jnp.float32)
    if pieces:
        array = array * block_levels(own_key, shape, pieces, -0.22, 0.18)
    return jnp.clip(array, -reach, reach).astype(held_as)


def setup_inputs(seed: int = 0) -> dict:
    splits = jax.random.split(jax.random.key(seed), 16)
    stream = scatter_about(splits[0], (TOKENS, D_MODEL), 1.0, 6.0, ((0, 8), (1, 4)), jnp.float32)
    cotangent = scatter_about(splits[1], (TOKENS, D_MODEL), 1.0, 6.0, ((0, 8), (1, 4)), jnp.float32)
    start_offsets = draw_start_offsets(jax.random.fold_in(splits[15], 71), 0)
    norm_gain = jnp.clip(1.0 + 0.1 * jax.random.normal(splits[3], (LAYERS, D_MODEL), jnp.float32), 0.5, 1.5)
    norm_shift = scatter_about(splits[4], (LAYERS, D_MODEL), 0.5, 3.0, ((1, 4),), jnp.float32)
    input_map = scatter_about(splits[5], (LAYERS, D_MODEL, 2 * STATES), D_MODEL ** -0.5, 0.25)
    decay_log = draw_decay_log(jax.random.fold_in(splits[15], 71), 0)
    phase_log = jnp.clip(jax.random.uniform(splits[7], (LAYERS, STATES), jnp.float32, -3.0, 0.5), -3.0, 0.5)
    scale_log = draw_scale_log(jax.random.fold_in(splits[15], 71), 0)
    output_map = scatter_about(splits[9], (LAYERS, 2 * STATES, D_MODEL), (2 * STATES) ** -0.5, 0.25, ((2, 4),))
    skip_gain = scatter_about(splits[10], (LAYERS, D_MODEL), 1.0, 4.0, ((1, 4),), jnp.float32)
    value_weight = scatter_about(splits[11], (LAYERS, D_MODEL, D_MODEL), D_MODEL ** -0.5, 0.25, ((2, 4),))
    gate_weight = scatter_about(splits[12], (LAYERS, D_MODEL, D_MODEL), D_MODEL ** -0.5, 0.25, ((2, 4),))
    value_bias = scatter_about(splits[13], (LAYERS, D_MODEL), 0.5, 3.0, ((1, 4),), jnp.float32)
    gate_bias = scatter_about(splits[14], (LAYERS, D_MODEL), 0.5, 3.0, ((1, 4),), jnp.float32)
    return dict(stream=stream, cotangent=cotangent, start_offsets=start_offsets, norm_gain=norm_gain, norm_shift=norm_shift, input_map=input_map, decay_log=decay_log, phase_log=phase_log, scale_log=scale_log, output_map=output_map, skip_gain=skip_gain, value_weight=value_weight, gate_weight=gate_weight, value_bias=value_bias, gate_bias=gate_bias)


epsilon = 1e-05

@jax.custom_vjp
def low(v):
    return lax.optimization_barrier(v.astype(jnp.bfloat16)).astype(jnp.float32)

@jax.custom_vjp
def low_back(v):
    return v

def low_keep(v):
    return (low(v), None)

def low_pass(kept, grad):
    return (grad,)

def back_keep(v):
    return (v, None)

def back_low(kept, grad):
    return (low(grad),)
low.defvjp(low_keep, low_pass)
low_back.defvjp(back_keep, back_low)

def matmul(left, right):
    return jnp.dot(left, right, precision=lax.Precision.HIGHEST, preferred_element_type=jnp.float32)

def recurrence(drive_re, drive_im, gates, rate_re, rate_im):
    rows_total = drive_re.shape[0]
    steps_total = rows_total // STRETCH

    def stretch_step(carried, inputs):
        part_re, part_im, part_gate = inputs

        def row_step(state, row_values):
            state_re, state_im = state
            row_re, row_im, row_gate = row_values
            mult_re = rate_re * row_gate
            mult_im = rate_im * row_gate
            new_re = mult_re * state_re - mult_im * state_im + row_re
            new_im = mult_re * state_im + mult_im * state_re + row_im
            return ((new_re, new_im), (new_re, new_im))
        return lax.scan(row_step, carried, (part_re, part_im, part_gate))
    initial = (jnp.zeros(rate_re.shape, jnp.float32), jnp.zeros(rate_re.shape, jnp.float32))
    inputs = (drive_re.reshape(steps_total, STRETCH, -1), drive_im.reshape(steps_total, STRETCH, -1), gates.reshape(steps_total, STRETCH))
    _, (out_re, out_im) = lax.scan(jax.checkpoint(stretch_step), initial, inputs)
    return (out_re.reshape(rows_total, -1), out_im.reshape(rows_total, -1))

def reference(stream, cotangent, start_offsets, norm_gain, norm_shift, input_map, decay_log, phase_log, scale_log, output_map, skip_gain, value_weight, gate_weight, value_bias, gate_bias):
    positions = jnp.arange(TOKENS, dtype=jnp.int32)
    within = positions % TOK_DEV
    offsets_rows = jnp.repeat(start_offsets.astype(jnp.int32), TOK_DEV)
    begin_flags = (within == offsets_rows) & (offsets_rows > 0) | (positions == 0)
    begins = begin_flags.astype(jnp.float32)
    finishes = jnp.concatenate([begins[1:], jnp.ones((1,), jnp.float32)])
    forward_gates = 1.0 - begins
    backward_gates = jnp.flip(1.0 - finishes, 0)
    params = (norm_gain, norm_shift, input_map.astype(jnp.float32), decay_log, phase_log, scale_log, output_map.astype(jnp.float32), skip_gain, value_weight.astype(jnp.float32), gate_weight.astype(jnp.float32), value_bias, gate_bias)

    def forward(stream_in, weights):
        gains, shifts, in_maps, decays, phases, scales, out_maps, skips, value_maps, gate_maps, value_shift, gate_shift = weights
        hidden = stream_in
        for layer_index in range(LAYERS):
            mean_val = lax.optimization_barrier(jnp.mean(hidden, axis=0))
            second = lax.optimization_barrier(jnp.mean(hidden * hidden, axis=0)) - mean_val * mean_val
            normed = (hidden - mean_val) * lax.rsqrt(second + epsilon)
            scaled = normed * gains[layer_index] + shifts[layer_index]
            driven = low_back(matmul(low(scaled), in_maps[layer_index]))
            radius = jnp.exp(-jnp.exp(decays[layer_index]))
            angle_val = jnp.exp(phases[layer_index])
            rate_re = radius * jnp.cos(angle_val)
            rate_im = radius * jnp.sin(angle_val)
            factor = jnp.exp(scales[layer_index])
            drive_re = factor * driven[:, :STATES]
            drive_im = factor * driven[:, STATES:]
            if layer_index % 2 == 1:
                state_re, state_im = recurrence(jnp.flip(drive_re, 0), jnp.flip(drive_im, 0), backward_gates, rate_re, rate_im)
                state_re = jnp.flip(state_re, 0)
                state_im = jnp.flip(state_im, 0)
            else:
                state_re, state_im = recurrence(drive_re, drive_im, forward_gates, rate_re, rate_im)
            states = low(jnp.concatenate([state_re, state_im], axis=1))
            mixed_val = low_back(matmul(states, out_maps[layer_index])) + skips[layer_index] * scaled
            sent = low(jax.nn.gelu(mixed_val))
            values = low_back(matmul(sent, value_maps[layer_index])) + value_shift[layer_index]
            gated = low_back(matmul(sent, gate_maps[layer_index])) + gate_shift[layer_index]
            hidden = hidden + values * jax.nn.sigmoid(gated)
        return hidden
    result, pullback = jax.vjp(forward, stream, params)
    stream_grad, grads = pullback(cotangent)
    return (result, stream_grad, grads[0], grads[1], grads[2], grads[3], grads[4], grads[5], grads[6], grads[7], grads[8], grads[9], grads[10], grads[11])
```

```python
import functools

import jax
import jax.numpy as jnp
from jax import lax
from jax.experimental import pallas as pl
from jax.experimental.pallas import tpu as pltpu
from jax.sharding import PartitionSpec as P

epsilon = 1e-05
LANES = 128
SUB = 8
ROOT = 0.7978845608028654
CUBE = 0.044715
AXES = ("dp", "mp")
F32 = jnp.float32
BF16 = jnp.bfloat16
NT = (((1,), (1,)), ((), ()))
TN = (((0,), (0,)), ((), ()))
GAIN, SHIFT, SKIP, VBIAS, GBIAS = range(5)
PARAMS = 5


def params():
    return pltpu.CompilerParams(vmem_limit_bytes=48 * 1024 * 1024)


def call(body, outs, scratch, *args, scalars=0):
    specs = [pl.BlockSpec(memory_space=pltpu.SMEM)] * scalars + [
        pl.BlockSpec(memory_space=pltpu.VMEM)
    ] * (len(args) - scalars)
    return pl.pallas_call(
        body,
        out_shape=outs,
        in_specs=specs,
        out_specs=[pl.BlockSpec(memory_space=pltpu.VMEM)] * len(outs),
        scratch_shapes=scratch,
        compiler_params=params(),
    )(*args)


def cat(ref, rows):
    return jnp.concatenate([ref[j, rows, :] for j in range(ref.shape[0])], axis=1)


def put(ref, rows, val):
    for j in range(ref.shape[0]):
        ref[j, rows, :] = val[:, j * LANES : (j + 1) * LANES].astype(ref.dtype)


def rowcat(ref, r):
    return jnp.concatenate([ref[j, r : r + 1, :] for j in range(ref.shape[0])], axis=1)


def lanes(rows):
    return jnp.concatenate([rows[j : j + 1, :] for j in range(rows.shape[0])], axis=1)


def dot(a, b):
    return jnp.dot(a, b, preferred_element_type=F32)


def dot_nt(a, b):
    return lax.dot_general(a, b, NT, preferred_element_type=F32)


def dot_tn(a, b):
    return lax.dot_general(a, b, TN, preferred_element_type=F32)


def chunks(rows, count):
    size = rows // count
    return [slice(i * size, (i + 1) * size) for i in range(count)]


def sweep(src, dst, table, init, reset, reverse, conj, extra=None):
    halves = src.shape[0] // 2
    span = src.shape[1] // SUB
    rate_re = [jnp.broadcast_to(table[h : h + 1, :], (SUB, LANES)) for h in range(halves)]
    rate_im = [
        jnp.broadcast_to(table[halves + h : halves + h + 1, :], (SUB, LANES))
        for h in range(halves)
    ]
    if conj:
        rate_im = [-r for r in rate_im]
    base = lax.broadcasted_iota(jnp.int32, (SUB, LANES), 0) * span - reset

    def body(step, carry):
        j = span - 1 - step if reverse else step
        state, sums = carry
        drop = base == -j
        at = pl.ds(j, SUB, stride=span)
        new_re, new_im = [], []
        for h in range(halves):
            a = jnp.where(drop, 0.0, rate_re[h])
            b = jnp.where(drop, 0.0, rate_im[h])
            re, im = state[h], state[halves + h]
            new_re.append((src[h, at, :] + a * re) - b * im)
            new_im.append((src[halves + h, at, :] + a * im) + b * re)
        state = tuple(new_re + new_im)
        if dst is not None:
            for k in range(2 * halves):
                dst[k, at, :] = state[k]
        if extra is not None:
            sums = extra(at, state, sums)
        return state, sums

    sums = ()
    if extra is not None:
        sums = tuple(jnp.zeros((SUB, LANES), F32) for _ in range(4 * halves))
    return lax.fori_loop(0, span, body, (init, sums), unroll=8)


def zeros_state(halves):
    return tuple(jnp.zeros((SUB, LANES), F32) for _ in range(2 * halves))


def chain_segments(ends, first, table, reset, span, reverse, conj):
    halves = len(ends) // 2
    power_re = [table[4 + h : 5 + h, :] for h in range(halves)]
    power_im = [table[6 + h : 7 + h, :] for h in range(halves)]
    if conj:
        power_im = [-r for r in power_im]
    state = list(first)
    incoming = [[None] * SUB for _ in ends]
    order = range(SUB - 1, -1, -1) if reverse else range(SUB)
    for k in order:
        inside = (reset >= k * span) & (reset < (k + 1) * span)
        keep = jnp.where(inside, 0.0, 1.0)
        new = [None] * len(ends)
        for h in range(halves):
            re, im = state[h], state[halves + h]
            incoming[h][k], incoming[halves + h][k] = re, im
            new[h] = keep * (power_re[h] * re - power_im[h] * im) + ends[h][k : k + 1, :]
            new[halves + h] = (
                keep * (power_re[h] * im + power_im[h] * re) + ends[halves + h][k : k + 1, :]
            )
        state = new
    return [jnp.concatenate(rows, axis=0) for rows in incoming], state


def zero_rows(halves):
    return [jnp.zeros((1, LANES), F32) for _ in range(2 * halves)]


def emit_ends(out, ends_out, ends, table, reset, span, reverse, conj):
    halves = len(ends) // 2
    _, last = chain_segments(ends, zero_rows(halves), table, reset, span, reverse, conj)
    tile = jnp.concatenate(last, axis=0)
    out[...] = jnp.broadcast_to(tile[None], out.shape)
    for k in range(2 * halves):
        ends_out[k, :, :] = ends[k]


def carried_in(gathered, moments, table, me, reverse, conj):
    count = gathered.shape[0]
    power_re = table[8:10, :]
    power_im = table[10:12, :]
    if conj:
        power_im = -power_im
    flag = 3 if reverse else 2

    def body(i, state):
        d = count - 1 - i if reverse else i
        re, im = state
        keep = moments[d, flag : flag + 1, :]
        tile = gathered[d]
        return (
            keep * (power_re * re - power_im * im) + tile[0:2, :],
            keep * (power_re * im + power_im * re) + tile[2:4, :],
        )

    zero = jnp.zeros((2, LANES), F32)
    re, im = lax.fori_loop(0, count - 1 - me if reverse else me, body, (zero, zero))
    return [re[0:1, :], re[1:2, :], im[0:1, :], im[1:2, :]]


def local_resets(offset, mp, rows):
    shift = jnp.where(offset > 0, offset - mp * rows, -(1 << 20))
    return shift, shift - 1


def first_kernel(rows, scal, stream, plist, decay, phase, scale, packed, moments, table):
    offset, mp = scal[0], scal[1]
    total = stream.shape[0]
    parts = packed.shape[0]
    size = 64

    def body(i, carry):
        one, two = carry
        x = stream[pl.ds(i * size, size), :]
        for g in range(0, size, SUB):
            piece = x[g : g + SUB, :]
            one = one + piece
            two = two + piece * piece
        packed[(i * size) // rows, pl.ds((i * size) % rows, size), :] = x
        return one, two

    zero = jnp.zeros((SUB, LANES), F32)
    one, two = lax.fori_loop(0, total // size, body, (zero, zero))
    for j in range(parts):
        packed[j, rows : rows + plist.shape[0], :] = plist[...]
    fwd, bwd = local_resets(offset, mp, rows)
    keep_f = jnp.where((fwd >= 0) & (fwd < rows), 0.0, 1.0)
    keep_b = jnp.where((bwd >= 0) & (bwd < rows), 0.0, 1.0)
    tile = jnp.concatenate(
        [
            jnp.sum(one, axis=0, keepdims=True),
            jnp.sum(two, axis=0, keepdims=True),
            jnp.full((1, LANES), keep_f, F32),
            jnp.full((1, LANES), keep_b, F32),
        ],
        axis=0,
    )
    moments[...] = jnp.broadcast_to(tile[None], moments.shape)
    span = rows // SUB
    for layer in range(decay.shape[0]):
        for h in range(2):
            cols = slice(h * LANES, (h + 1) * LANES)
            radius = jnp.exp(-jnp.exp(decay[layer : layer + 1, cols]))
            angle = jnp.exp(phase[layer : layer + 1, cols])
            re, im = radius * jnp.cos(angle), radius * jnp.sin(angle)
            table[layer, h : h + 1, :] = re
            table[layer, 2 + h : 3 + h, :] = im
            length = 1
            while length < rows:
                re, im = re * re - im * im, 2.0 * re * im
                length *= 2
                if length == span:
                    table[layer, 4 + h : 5 + h, :] = re
                    table[layer, 6 + h : 7 + h, :] = im
            table[layer, 8 + h : 9 + h, :] = re
            table[layer, 10 + h : 11 + h, :] = im
            table[layer, 12 + h : 13 + h, :] = jnp.exp(scale[layer : layer + 1, cols])
            table[layer, 14 + h : 15 + h, :] = jnp.zeros((1, LANES), F32)


def norm_rows(mean, second, gain, shift):
    inverse = lax.rsqrt(second - mean * mean + epsilon)
    factor = inverse * gain
    return inverse, factor, shift - mean * factor


def drive_body(layer, total_tokens, scal, h, mom, prm, prm_base, table, weight, drive, norms, out, ends_out):
    offset, mp = scal[0], scal[1]
    rows = drive.shape[1]
    reverse = layer % 2 == 1
    if layer == 0:
        groups = prm.shape[0]
        sums = [mom[j, 0:2, :] for j in range(groups)]
        for d in range(groups, mom.shape[0]):
            sums[d % groups] = sums[d % groups] + mom[d, 0:2, :]
        both = jnp.concatenate(sums, axis=1) * (1.0 / total_tokens)
        mean, second = both[0:1, :], both[1:2, :]
    else:
        tile = mom[0]
        for d in range(1, mom.shape[0]):
            tile = tile + mom[d]
        tile = tile * (1.0 / total_tokens)
        half = tile.shape[0] // 2
        mean, second = lanes(tile[:half]), lanes(tile[half:])
    base = prm_base + layer * PARAMS
    inverse, factor, bias = norm_rows(
        mean, second, rowcat(prm, base + GAIN), rowcat(prm, base + SHIFT)
    )
    norms[...] = jnp.concatenate(
        [factor, bias, inverse, mean] + [jnp.zeros_like(mean)] * 4, axis=0
    )
    gamma = lanes(table[layer, 12:14, :])
    gamma = jnp.concatenate([gamma, gamma], axis=1)
    for at in chunks(rows, 2):
        low = (cat(h, at) * factor + bias).astype(BF16)
        put(drive, at, dot(low, weight[layer]) * gamma)
    fwd, bwd = local_resets(offset, mp, rows)
    reset = bwd if reverse else fwd
    ends, _ = sweep(drive, None, table[layer], zeros_state(2), reset, reverse, False)
    emit_ends(out, ends_out, ends, table[layer], reset, rows // SUB, reverse, False)


def drive_first(layer, total_tokens, scal, h, mom, table, weight, drive, norms, out, ends, prm_out):
    rows = drive.shape[1]
    drive_body(layer, total_tokens, scal, h, mom, h, rows, table, weight, drive, norms, out, ends)
    for j in range(prm_out.shape[0]):
        prm_out[j, :, :] = h[j, rows : rows + prm_out.shape[1], :]


def drive_next(layer, total_tokens, scal, h, mom, prm, table, weight, drive, norms, out, ends):
    drive_body(layer, total_tokens, scal, h, mom, prm, 0, table, weight, drive, norms, out, ends)


def resume(scal, rows, gathered, mom, tab, ends, reverse, conj):
    offset, mp, me = scal[0], scal[1], scal[2]
    fwd, bwd = local_resets(offset, mp, rows)
    reset = bwd if reverse else fwd
    first = carried_in(gathered, mom, tab, me, reverse, conj)
    incoming, _ = chain_segments(
        [ends[k] for k in range(4)], first, tab, reset, rows // SUB, reverse, conj
    )
    return tuple(incoming), reset


def mix_chunk(layer, at, h, norms, states, c_map, v_map, g_map, prm):
    base = layer * PARAMS
    x = cat(h, at)
    scaled = x * norms[0:1, :] + norms[1:2, :]
    states_low = cat(states, at).astype(BF16)
    mixed = dot(states_low, c_map) + rowcat(prm, base + SKIP) * scaled
    square = mixed * mixed
    wave = jnp.tanh(ROOT * mixed * (1.0 + CUBE * square))
    half = 0.5 * (1.0 + wave)
    sent_low = (mixed * half).astype(BF16)
    slope = half + 0.5 * mixed * (1.0 - wave * wave) * (ROOT * (1.0 + 3.0 * CUBE * square))
    value = dot(sent_low, v_map) + rowcat(prm, base + VBIAS)
    gate = dot(sent_low, g_map) + rowcat(prm, base + GBIAS)
    sig = 0.5 + 0.5 * jnp.tanh(0.5 * gate)
    gated = value * sig
    return x, scaled, states_low, sent_low, slope, sig, gated


def back_chunk(layer, at, g, sig, gain_part, sent_low, states_low, scaled, slope, c_map, v_map, g_map, refs, sums):
    dv_ref, dg_ref, dm_ref, dmlow_ref, ds = refs
    dvalue = g * sig
    dgate = g * gain_part
    dv_low, dg_low = dvalue.astype(BF16), dgate.astype(BF16)
    dmixed = (dot_nt(dv_low, v_map) + dot_nt(dg_low, g_map)) * slope
    dm_low = dmixed.astype(BF16)
    put(ds, at, dot_nt(dm_low, c_map))
    dv_ref[at, :] = dv_low
    dg_ref[at, :] = dg_low
    dmlow_ref[at, :] = dm_low
    put(dm_ref, at, dmixed)
    add = lambda v: jnp.sum(v, axis=0, keepdims=True)
    return [
        s + n for s, n in zip(sums, [add(dvalue), add(dgate), add(dmixed * scaled)], strict=True)
    ]


def weight_grads(pack, sent, states, dv, dg, dm, sums):
    width = sent.shape[1]
    parts = pack.shape[0]
    for first, left, right in ((0, sent, dv), (1, sent, dg), (2, states, dm)):
        grad = dot_tn(left[...], right[...])
        put(pack, slice(first * width, (first + 1) * width), grad)
    top = 3 * width
    for j in range(parts):
        cols = slice(j * LANES, (j + 1) * LANES)
        rows = [s[:, cols] for s in sums] + [jnp.zeros((16 - len(sums), LANES), F32)]
        pack[j, top : top + 16, :] = jnp.concatenate(rows, axis=0).astype(pack.dtype)


def add_chunk(mom, one, two):
    tile = jnp.concatenate(
        [one[:, j * LANES : (j + 1) * LANES] for j in range(one.shape[1] // LANES)]
        + [two[:, j * LANES : (j + 1) * LANES] for j in range(two.shape[1] // LANES)],
        axis=0,
    )
    mom[...] = jnp.broadcast_to(tile[None], mom.shape)


def mix_first(layer, scal, gathered, mom, table, ends, h, norms, drive, prm, c4, v4, g4,
              states, sent, slope_out, sig_out, part_out, new_h, new_mom):
    rows = drive.shape[1]
    reverse = layer % 2 == 1
    tab = table[layer]
    init, reset = resume(scal, rows, gathered, mom, tab, ends, reverse, False)
    sweep(drive, states, tab, init, reset, reverse, False)
    c_map, v_map, g_map = cat(c4, slice(None)), cat(v4, slice(None)), cat(g4, slice(None))
    one = two = 0.0
    for at in chunks(rows, 2):
        x, scaled, states_low, sent_low, slope, sig, gated = mix_chunk(
            layer, at, h, norms, states, c_map, v_map, g_map, prm
        )
        sent[at, :] = sent_low
        put(slope_out, at, slope)
        put(sig_out, at, sig)
        put(part_out, at, gated * (1.0 - sig))
        new = x + gated
        put(new_h, at, new)
        one = one + jnp.sum(new, axis=0, keepdims=True)
        two = two + jnp.sum(new * new, axis=0, keepdims=True)
    add_chunk(new_mom, one, two)


def turn(layer, scal, gathered, mom, table, ends, h, norms, drive, prm, c4, v4, g4, cot,
         states, new_h, ds, dm, pack, out, ends_out, sent, slow, dv, dg, dml):
    rows = drive.shape[1]
    reverse = layer % 2 == 1
    tab = table[layer]
    init, reset = resume(scal, rows, gathered, mom, tab, ends, reverse, False)
    sweep(drive, states, tab, init, reset, reverse, False)
    c_map, v_map, g_map = cat(c4, slice(None)), cat(v4, slice(None)), cat(g4, slice(None))
    sums = [0.0, 0.0, 0.0]
    for at in chunks(rows, 2):
        x, scaled, states_low, sent_low, slope, sig, gated = mix_chunk(
            layer, at, h, norms, states, c_map, v_map, g_map, prm
        )
        sent[at, :] = sent_low
        slow[at, :] = states_low
        put(new_h, at, x + gated)
        sums = back_chunk(layer, at, cat(cot, at), sig, gated * (1.0 - sig), sent_low, states_low,
                          scaled, slope, c_map, v_map, g_map, (dv, dg, dm, dml, ds), sums)
    adjoint_start(layer, scal, tab, ds, out, ends_out)
    weight_grads(pack, sent, slow, dv, dg, dml, sums)


def adjoint_start(layer, scal, tab, ds, out, ends_out):
    rows = ds.shape[1]
    reverse = layer % 2 == 0
    fwd, bwd = local_resets(scal[0], scal[1], rows)
    reset = bwd if reverse else fwd
    ends, _ = sweep(ds, None, tab, zeros_state(2), reset, reverse, True)
    emit_ends(out, ends_out, ends, tab, reset, rows // SUB, reverse, True)


def corrected(total_tokens, layer, u, normed, norms, back, prm):
    tile = back[0]
    for d in range(1, back.shape[0]):
        tile = tile + back[d]
    half = tile.shape[0] // 2
    factor = norms[0:1, :] * (1.0 / total_tokens)
    return u - factor * lanes(tile[:half]) - normed * (factor * lanes(tile[half:]))


def back_first(layer, total_tokens, scal, back, u, h1, norms1, h, norms, sent, states, slope, sig, part,
               prm, table, c4, v4, g4, g_out, ds, dm, pack, out, ends_out, slow, dv, dg, dml):
    rows = ds.shape[1]
    tab = table[layer]
    tile = back[0]
    for d in range(1, back.shape[0]):
        tile = tile + back[d]
    half = tile.shape[0] // 2
    factor = norms1[0:1, :] * (1.0 / total_tokens)
    m_one, m_two = factor * lanes(tile[:half]), factor * lanes(tile[half:])
    inverse1, mean1 = norms1[2:3, :], norms1[3:4, :]
    c_map, v_map, g_map = cat(c4, slice(None)), cat(v4, slice(None)), cat(g4, slice(None))
    sums = [0.0, 0.0, 0.0]
    for at in chunks(rows, 2):
        normed1 = (cat(h1, at) - mean1) * inverse1
        g = cat(u, at) - m_one - normed1 * m_two
        put(g_out, at, g)
        scaled = cat(h, at) * norms[0:1, :] + norms[1:2, :]
        states_low = cat(states, at).astype(BF16)
        slow[at, :] = states_low
        sums = back_chunk(layer, at, g, cat(sig, at), cat(part, at), sent[at, :], states_low, scaled,
                          cat(slope, at), c_map, v_map, g_map, (dv, dg, dm, dml, ds), sums)
    adjoint_start(layer, scal, tab, ds, out, ends_out)
    weight_grads(pack, sent, slow, dv, dg, dml, sums)


def back_second(layer, scal, gathered, mom, table, ends, ds, drive, states, h, norms, dm, g, prm, weight,
                u_out, back, pack, adj, slow, dlow):
    rows = ds.shape[1]
    reverse = layer % 2 == 0
    tab = table[layer]
    init, reset = resume(scal, rows, gathered, mom, tab, ends, reverse, True)

    def extra(at, a, sums):
        new = []
        for h_ in range(2):
            re, im = a[h_], a[2 + h_]
            for ref in (states, drive):
                sre, sim = ref[h_, at, :], ref[2 + h_, at, :]
                new.append(re * sre + im * sim)
                new.append(im * sre - re * sim)
        return tuple(s + n for s, n in zip(sums, new, strict=True))

    _, sums = sweep(ds, adj, tab, init, reset, reverse, True, extra)
    flat = [jnp.sum(s, axis=0, keepdims=True) for s in sums]
    gamma = lanes(tab[12:14, :])
    gamma = jnp.concatenate([gamma, gamma], axis=1)
    base = layer * PARAMS
    gain, skip = rowcat(prm, base + GAIN), rowcat(prm, base + SKIP)
    factor, bias, inverse, mean = (norms[i : i + 1, :] for i in range(4))
    one = two = 0.0
    for at in chunks(rows, 2):
        x = cat(h, at)
        normed = (x - mean) * inverse
        slow[at, :] = (x * factor + bias).astype(BF16)
        low = (cat(adj, at) * gamma).astype(BF16)
        dlow[at, :] = low
        dscaled = dot_nt(low, weight[layer]) + cat(dm, at) * skip
        put(u_out, at, cat(g, at) + factor * dscaled)
        one = one + jnp.sum(dscaled, axis=0, keepdims=True)
        two = two + jnp.sum(dscaled * normed, axis=0, keepdims=True)
    add_chunk(back, one, two)
    put(pack, slice(0, slow.shape[1]), dot_tn(slow[...], dlow[...]))
    top = slow.shape[1]
    rows_out = []
    for h_ in range(2):
        x_re, x_im, y_re, y_im = flat[4 * h_ : 4 * h_ + 4]
        rows_out += [x_re - y_re, x_im - y_im, y_re]
    tile = jnp.concatenate(rows_out + [jnp.zeros((16 - 6, LANES), F32)], axis=0).astype(pack.dtype)
    for j in range(pack.shape[0]):
        pack[j, top : top + 16, :] = tile


def last_kernel(total_tokens, groups, scal, u, stream, norms, back, out, sums_out):
    mp = scal[1]
    tile = back[0]
    for d in range(1, back.shape[0]):
        tile = tile + back[d]
    half = tile.shape[0] // 2
    one = two = factor = inverse = mean = jnp.zeros((1, LANES), F32)
    for j in range(groups):
        mine = jnp.where(mp == j, 1.0, 0.0)
        cols = slice(j * LANES, (j + 1) * LANES)
        one = one + mine * tile[j : j + 1, :]
        two = two + mine * tile[half + j : half + j + 1, :]
        factor = factor + mine * norms[0:1, cols]
        inverse = inverse + mine * norms[2:3, cols]
        mean = mean + mine * norms[3:4, cols]
    scaled = factor * (1.0 / total_tokens)
    m_one, m_two = scaled * one, scaled * two
    size = 128

    def body(i, carry):
        at = pl.ds(i * size, size)
        normed = (stream[at, :] - mean) * inverse
        out[at, :] = u[at, :] - m_one - normed * m_two
        return carry

    lax.fori_loop(0, out.shape[0] // size, body, 0)
    sums_out[...] = jnp.concatenate([one, two] + [jnp.zeros((6, LANES), F32)], axis=0)


def shape(dims, dtype=F32):
    return jax.ShapeDtypeStruct(tuple(dims), dtype)


def every(x):
    return lax.all_to_all(x, AXES, 0, 0)


def across(x):
    return lax.all_to_all(x, "mp", 0, 0)


def reduced(pack, count_dp):
    parts, rows, width = pack.shape
    own = jnp.sum(across(pack).astype(F32), axis=0)
    unit = 16 * count_dp
    padded = -(-rows // unit) * unit
    own = jnp.pad(own, ((0, padded - rows), (0, 0))).astype(BF16)
    pieces = lax.all_to_all(own.reshape(count_dp, padded // count_dp, width), "dp", 0, 0)
    mine = jnp.sum(pieces.astype(F32), axis=0).astype(BF16)
    full = lax.all_to_all(jnp.broadcast_to(mine[None], (count_dp,) + mine.shape), "dp", 0, 0)
    return full.reshape(padded, width)[:rows]


def on_device(
    stream,
    cotangent,
    start_offsets,
    norm_gain,
    norm_shift,
    input_map,
    decay_log,
    phase_log,
    scale_log,
    output_map,
    skip_gain,
    value_weight,
    gate_weight,
    value_bias,
    gate_bias,
):
    block, width = stream.shape
    layers = input_map.shape[0]
    count_dp, parts = lax.axis_size("dp"), lax.axis_size("mp")
    devices = count_dp * parts
    tokens = block * count_dp
    rows = block // parts
    features = width * parts
    assert width == LANES and features == 4 * LANES and layers == 2
    mp = lax.axis_index("mp")
    me = lax.axis_index("dp") * parts + mp
    scal = jnp.stack([start_offsets[0], mp, me]).astype(jnp.int32)

    plist = jnp.concatenate(
        [
            a[layer : layer + 1]
            for layer in range(layers)
            for a in (norm_gain, norm_shift, skip_gain, value_bias, gate_bias)
        ]
        + [jnp.zeros((16 - PARAMS * layers, width), F32)],
        axis=0,
    )
    blocks = (parts, rows, width)
    tall = (parts, rows + 16, width)
    ends_shape = shape((4, SUB, LANES))
    every_shape = shape((devices, 4, LANES))
    sums_shape = shape((devices, 2 * parts, LANES))
    norm_shape = shape((8, features))

    packed, mom_out, table = call(
        functools.partial(first_kernel, rows),
        [shape(tall), every_shape, shape((layers, 16, LANES))],
        [],
        scal, stream, plist, decay_log, phase_log, scale_log,
        scalars=1,
    )
    h0 = across(packed)
    mom0 = every(mom_out)
    cot = across(cotangent.reshape(blocks))
    maps = []
    for layer in range(layers):
        own = jnp.stack([output_map[layer], value_weight[layer], gate_weight[layer]])
        got = across(jnp.broadcast_to(own[None], (parts,) + own.shape))
        maps.append([got[:, k] for k in range(3)])

    drive0, norms0, ends_all, ends0, prm = call(
        functools.partial(drive_first, 0, tokens),
        [shape(blocks), norm_shape, every_shape, ends_shape, shape((parts, 16, width))],
        [],
        scal, h0, mom0, table, input_map,
        scalars=1,
    )
    got = every(ends_all)
    states0, sent0, slope0, sig0, part0, h1, mom_out = call(
        functools.partial(mix_first, 0),
        [shape(blocks), shape((rows, features), BF16), shape(blocks), shape(blocks), shape(blocks),
         shape(blocks), sums_shape],
        [],
        scal, got, mom0, table, ends0, h0, norms0, drive0, prm, *maps[0],
        scalars=1,
    )
    mom1 = every(mom_out)
    drive1, norms1, ends_all, ends1 = call(
        functools.partial(drive_next, 1, tokens),
        [shape(blocks), norm_shape, every_shape, ends_shape],
        [],
        scal, h1, mom1, prm, table, input_map,
        scalars=1,
    )
    got = every(ends_all)
    low = pltpu.VMEM((rows, features), BF16)
    pack_shape = shape((parts, 3 * features + 16, width), BF16)
    states1, h2, ds1, dm1, pack1, ends_all, back_ends1 = call(
        functools.partial(turn, 1),
        [shape(blocks), shape(blocks), shape(blocks), shape(blocks), pack_shape, every_shape, ends_shape],
        [low] * 5,
        scal, got, mom0, table, ends1, h1, norms1, drive1, prm, *maps[1], cot,
        scalars=1,
    )
    result = across(h2).reshape(block, width)
    got = every(ends_all)
    in_pack_shape = shape((parts, features + 16, width), BF16)
    u1, back_out, in_pack1 = call(
        functools.partial(back_second, 1),
        [shape(blocks), sums_shape, in_pack_shape],
        [pltpu.VMEM(blocks, F32), low, low],
        scal, got, mom0, table, back_ends1, ds1, drive1, states1, h1, norms1, dm1, cot, prm, input_map,
        scalars=1,
    )
    back1 = every(back_out)
    g0, ds0, dm0, pack0, ends_all, back_ends0 = call(
        functools.partial(back_first, 0, tokens),
        [shape(blocks), shape(blocks), shape(blocks), pack_shape, every_shape, ends_shape],
        [low] * 4,
        scal, back1, u1, h1, norms1, h0, norms0, sent0, states0, slope0, sig0, part0, prm, table, *maps[0],
        scalars=1,
    )
    got = every(ends_all)
    u0, back_out, in_pack0 = call(
        functools.partial(back_second, 0),
        [shape(blocks), sums_shape, in_pack_shape],
        [pltpu.VMEM(blocks, F32), low, low],
        scal, got, mom0, table, back_ends0, ds0, drive0, states0, h0, norms0, dm0, g0, prm, input_map,
        scalars=1,
    )
    u0 = across(u0).reshape(block, width)
    back0 = every(back_out)
    stream_grad, own_sums0 = call(
        functools.partial(last_kernel, tokens, parts),
        [shape((block, width)), shape((8, width))],
        [],
        scal, u0, stream, norms0, back0,
        scalars=1,
    )

    own_sums1 = lax.dynamic_slice_in_dim(
        jnp.sum(back1, axis=0).reshape(2, parts, width), mp, 1, axis=1
    ).reshape(2, width)
    gain_grad = jnp.stack([own_sums0[1], own_sums1[1]])
    shift_grad = jnp.stack([own_sums0[0], own_sums1[0]])

    vgo, inputs = [], []
    for pack, in_pack in ((pack0, in_pack0), (pack1, in_pack1)):
        full = reduced(jnp.concatenate([pack, in_pack], axis=1), count_dp)
        split = 3 * features + 16
        vgo.append(full[:split].astype(F32))
        inputs.append(full[split:])
    mats = jnp.stack([g[: 3 * features] for g in vgo]).reshape(layers, 3, features, width)
    vecs = jnp.stack([g[3 * features : 3 * features + 3] for g in vgo])
    in_own = jnp.stack([g[:features] for g in inputs])
    in_all = across(jnp.broadcast_to(in_own[None], (parts,) + in_own.shape))
    input_grad = in_all.transpose(1, 2, 0, 3).reshape(layers, features, features).astype(F32)
    state_vecs = jnp.stack([g[features : features + 6] for g in inputs]).astype(F32)
    state_vecs = state_vecs.reshape(layers, 2, 3, LANES).transpose(2, 0, 1, 3).reshape(3, layers, -1)
    decay_grad = -jnp.exp(decay_log) * state_vecs[0]
    phase_grad = jnp.exp(phase_log) * state_vecs[1]
    scale_grad = state_vecs[2]
    return (
        result,
        stream_grad,
        gain_grad,
        shift_grad,
        input_grad,
        decay_grad,
        phase_grad,
        scale_grad,
        mats[:, 2],
        vecs[:, 2],
        mats[:, 0],
        mats[:, 1],
        vecs[:, 0],
        vecs[:, 1],
    )


def solution(mesh):
    split = P("dp", "mp")
    cols = P(None, "mp")
    wide = P(None, None, "mp")
    placed = (
        split, split, P("dp"), cols, cols, P(), P(), P(), P(), wide, cols, wide, wide, cols, cols,
    )
    return jax.shard_map(
        on_device,
        mesh=mesh,
        in_specs=placed,
        out_specs=(
            split, split, cols, cols, P(), P(), P(), P(), wide, cols, wide, wide, cols, cols,
        ),
        check_vma=False,
    )
```

```python
import functools

import jax
import jax.numpy as jnp
from jax import lax
from jax.experimental import pallas as pl
from jax.experimental.pallas import tpu as pltpu
from jax.sharding import PartitionSpec as P

epsilon = 1e-05
LANES = 128
SUB = 8
ROOT = 0.7978845608028654
CUBE = 0.044715
AXES = ("dp", "mp")
F32 = jnp.float32
BF16 = jnp.bfloat16
NT = (((1,), (1,)), ((), ()))
TN = (((0,), (0,)), ((), ()))
GAIN, SHIFT, SKIP, VBIAS, GBIAS = range(5)
PARAMS = 5


class Copies:
    def __init__(self, sems):
        self.sems, self.used, self.open = sems, 0, []

    def start(self, src, dst):
        copy = pltpu.make_async_copy(src, dst, self.sems.at[self.used])
        self.used += 1
        copy.start()
        return copy

    def flush(self, src, dst):
        self.open.append(self.start(src, dst))

    def finish(self):
        for copy in self.open:
            copy.wait()
        self.open = []


def along(ref, part, parts):
    if parts == 1:
        return ref
    axis = len(ref.shape) - 2
    size = ref.shape[axis] // parts
    at = pl.ds(part * size, size)
    return ref.at[at] if axis == 0 else ref.at[:, at]


class Arrival:
    def __init__(self, copies, src, dst, parts):
        self.copies, self.src, self.dst, self.parts = copies, src, dst, parts
        self.waits = [None] * parts

    def begin(self, part):
        src, dst = (along(r, part, self.parts) for r in (self.src, self.dst))
        self.waits[part] = self.copies.start(src, dst)

    def part(self, part):
        if self.waits[part] is not None:
            self.waits[part].wait()
            self.waits[part] = None
        return self.dst

    def __call__(self):
        for part in range(self.parts):
            self.part(part)
        return self.dst


class Result:
    def __init__(self, copies, ref, dst):
        self.copies, self.ref, self.dst, self.sent = copies, ref, dst, False

    def flush(self, part=0, parts=1):
        self.sent = True
        self.copies.flush(along(self.ref, part, parts), along(self.dst, part, parts))


class Raw:
    def __init__(self, array):
        self.array = array


class Halves:
    def __init__(self, array):
        self.array = array


class Near:
    def __init__(self, array):
        self.array = array


class Here:
    def __init__(self, ref):
        self.ref = self.dst = ref

    def part(self, part):
        return self.ref

    def __call__(self):
        return self.ref

    def flush(self, part=0, parts=1):
        pass


def call(body, outs, scratch, *args, scalars=0):
    wraps = (Raw, Halves, Near)
    plain = [a.array if isinstance(a, wraps) else a for a in args]
    out_shapes = [o.array if isinstance(o, wraps) else o for o in outs]
    autos = [i for i, a in enumerate(args) if i >= scalars and not isinstance(a, (Raw, Near))]
    made = [i for i, o in enumerate(outs) if not isinstance(o, (Raw, Near))]
    rooms = [pltpu.VMEM(plain[i].shape, plain[i].dtype) for i in autos]
    rooms += [pltpu.VMEM(out_shapes[i].shape, out_shapes[i].dtype) for i in made]

    def kernel(*refs):
        ins, refs = refs[: len(args)], refs[len(args) :]
        dsts, refs = refs[: len(outs)], refs[len(outs) :]
        sems, refs = refs[0], refs[1:]
        vin, refs = refs[: len(autos)], refs[len(autos) :]
        vout, rest = refs[: len(made)], refs[len(made) :]
        copies = Copies(sems)
        operands = [Here(r) if isinstance(a, Near) else r for a, r in zip(args, ins, strict=True)]
        for i, room in zip(autos, vin, strict=True):
            parts = 2 if isinstance(args[i], Halves) else 1
            operands[i] = Arrival(copies, ins[i], room, parts)
        results = [Here(r) if isinstance(o, Near) else r for o, r in zip(outs, dsts, strict=True)]
        for i, room in zip(made, vout, strict=True):
            results[i] = Result(copies, room, dsts[i])

        def begin():
            for part in range(2):
                for i in autos:
                    if part < operands[i].parts:
                        operands[i].begin(part)

        body(copies, begin, *operands, *results, *rest)
        for r in results:
            if isinstance(r, Result) and not r.sent:
                r.flush()
        copies.finish()
        used.append(copies.used)

    near = pl.BlockSpec(memory_space=pltpu.VMEM)
    far = pl.BlockSpec(memory_space=pltpu.HBM)
    plain[scalars:] = [
        a if isinstance(w, Near) else pltpu.with_memory_space_constraint(a, pltpu.HBM)
        for w, a in zip(args[scalars:], plain[scalars:], strict=True)
    ]
    used = []

    def made_call(count):
        return pl.pallas_call(
            kernel,
            out_shape=[
                s if isinstance(o, Near) else pltpu.HBM(s.shape, s.dtype)
                for o, s in zip(outs, out_shapes, strict=True)
            ],
            in_specs=[pl.BlockSpec(memory_space=pltpu.SMEM)] * scalars
            + [near if isinstance(a, Near) else far for a in args[scalars:]],
            out_specs=[near if isinstance(o, Near) else far for o in outs],
            scratch_shapes=[pltpu.SemaphoreType.DMA((count,))] + rooms + list(scratch),
            compiler_params=pltpu.CompilerParams(vmem_limit_bytes=32 * 1024 * 1024),
        )

    jax.eval_shape(made_call(128), *plain)
    return made_call(max(used[0], 1))(*plain)


def cat(ref, rows):
    return jnp.concatenate([ref[j, rows, :] for j in range(ref.shape[0])], axis=1)


def put(ref, rows, val):
    for j in range(ref.shape[0]):
        ref[j, rows, :] = val[:, j * LANES : (j + 1) * LANES].astype(ref.dtype)


def rowcat(ref, r):
    return jnp.concatenate([ref[j, r : r + 1, :] for j in range(ref.shape[0])], axis=1)


def lanes(rows):
    return jnp.concatenate([rows[j : j + 1, :] for j in range(rows.shape[0])], axis=1)


def dot(a, b):
    return jnp.dot(a, b, preferred_element_type=F32)


def dot_nt(a, b):
    return lax.dot_general(a, b, NT, preferred_element_type=F32)


def dot_tn(a, b):
    return lax.dot_general(a, b, TN, preferred_element_type=F32)


def chunks(rows, count):
    size = rows // count
    return [slice(i * size, (i + 1) * size) for i in range(count)]


def sweep(src, dst, table, init, reset, reverse, conj, extra=None):
    halves = src.shape[0] // 2
    span = src.shape[1] // SUB
    rate_re = [jnp.broadcast_to(table[h : h + 1, :], (SUB, LANES)) for h in range(halves)]
    rate_im = [
        jnp.broadcast_to(table[halves + h : halves + h + 1, :], (SUB, LANES))
        for h in range(halves)
    ]
    if conj:
        rate_im = [-r for r in rate_im]
    base = lax.broadcasted_iota(jnp.int32, (SUB, LANES), 0) * span - reset

    def body(step, carry):
        j = span - 1 - step if reverse else step
        state, sums = carry
        drop = base == -j
        at = pl.ds(j, SUB, stride=span)
        new_re, new_im = [], []
        for h in range(halves):
            a = jnp.where(drop, 0.0, rate_re[h])
            b = jnp.where(drop, 0.0, rate_im[h])
            re, im = state[h], state[halves + h]
            new_re.append((src[h, at, :] + a * re) - b * im)
            new_im.append((src[halves + h, at, :] + a * im) + b * re)
        state = tuple(new_re + new_im)
        if dst is not None:
            for k in range(2 * halves):
                dst[k, at, :] = state[k]
        if extra is not None:
            sums = extra(at, state, sums)
        return state, sums

    sums = ()
    if extra is not None:
        sums = tuple(jnp.zeros((SUB, LANES), F32) for _ in range(2 * halves))
    return lax.fori_loop(0, span, body, (init, sums), unroll=8)


def zeros_state(halves):
    return tuple(jnp.zeros((SUB, LANES), F32) for _ in range(2 * halves))


def chain_segments(ends, first, table, reset, span, reverse, conj):
    halves = len(ends) // 2
    power_re = [table[4 + h : 5 + h, :] for h in range(halves)]
    power_im = [table[6 + h : 7 + h, :] for h in range(halves)]
    if conj:
        power_im = [-r for r in power_im]
    state = list(first)
    incoming = [[None] * SUB for _ in ends]
    order = range(SUB - 1, -1, -1) if reverse else range(SUB)
    for k in order:
        inside = (reset >= k * span) & (reset < (k + 1) * span)
        keep = jnp.where(inside, 0.0, 1.0)
        new = [None] * len(ends)
        for h in range(halves):
            re, im = state[h], state[halves + h]
            incoming[h][k], incoming[halves + h][k] = re, im
            new[h] = keep * (power_re[h] * re - power_im[h] * im) + ends[h][k : k + 1, :]
            new[halves + h] = (
                keep * (power_re[h] * im + power_im[h] * re) + ends[halves + h][k : k + 1, :]
            )
        state = new
    return [jnp.concatenate(rows, axis=0) for rows in incoming], state


def zero_rows(halves):
    return [jnp.zeros((1, LANES), F32) for _ in range(2 * halves)]


def emit_ends(out, ends_out, ends, table, reset, span, reverse, conj):
    halves = len(ends) // 2
    _, last = chain_segments(ends, zero_rows(halves), table, reset, span, reverse, conj)
    tile = jnp.concatenate(last, axis=0)
    out.ref[...] = jnp.broadcast_to(tile[None], out.ref.shape)
    out.flush()
    for k in range(2 * halves):
        ends_out.ref[k, :, :] = ends[k]
    ends_out.flush()


def carried_in(gathered, moments, table, me, reverse, conj):
    count = gathered.shape[0]
    power_re = table[8:10, :]
    power_im = table[10:12, :]
    if conj:
        power_im = -power_im
    flag = 3 if reverse else 2

    def body(i, state):
        d = count - 1 - i if reverse else i
        re, im = state
        keep = moments[d, flag : flag + 1, :]
        tile = gathered[d]
        return (
            keep * (power_re * re - power_im * im) + tile[0:2, :],
            keep * (power_re * im + power_im * re) + tile[2:4, :],
        )

    zero = jnp.zeros((2, LANES), F32)
    re, im = lax.fori_loop(0, count - 1 - me if reverse else me, body, (zero, zero))
    return [re[0:1, :], re[1:2, :], im[0:1, :], im[1:2, :]]


def place():
    mp = lax.axis_index("mp")
    return mp, lax.axis_index("dp") * lax.axis_size("mp") + mp


def local_resets(start, rows):
    offset = start[0]
    shift = jnp.where(offset > 0, offset - lax.axis_index("mp") * rows, -(1 << 20))
    return shift, shift - 1


def first_kernel(rows, copies, begin, start, stream, gain, shift, skip, vbias, gbias, decay, phase, scale,
                 moments, table_out, send1, send2, send3, held):
    mp, _ = place()
    total, width = held.shape
    parts = total // rows
    arrive = [copies.start(along(stream, i, parts), along(held, i, parts)) for i in range(parts)]
    begin()
    size = 128
    one = two = jnp.zeros((SUB, LANES), F32)

    def body(i, carry):
        one, two = carry
        x = held[pl.ds(i * size, size), :]
        for g in range(0, size, SUB):
            piece = x[g : g + SUB, :]
            one = one + piece
            two = two + piece * piece
        return one, two

    for i in range(parts):
        arrive[i].wait()
        one, two = lax.fori_loop(i * rows // size, (i + 1) * rows // size, body, (one, two))
    fwd, bwd = local_resets(start, rows)
    keep_f = jnp.where((fwd >= 0) & (fwd < rows), 0.0, 1.0)
    keep_b = jnp.where((bwd >= 0) & (bwd < rows), 0.0, 1.0)
    tile = jnp.concatenate(
        [
            jnp.sum(one, axis=0, keepdims=True),
            jnp.sum(two, axis=0, keepdims=True),
            jnp.full((1, LANES), keep_f, F32),
            jnp.full((1, LANES), keep_b, F32),
        ],
        axis=0,
    )
    moments.ref[...] = jnp.broadcast_to(tile[None], moments.ref.shape)
    moments.flush()
    gain, shift, skip, vbias, gbias = (a() for a in (gain, shift, skip, vbias, gbias))
    decay, phase, scale = decay(), phase(), scale()
    layers = decay.shape[0]
    plist = jnp.concatenate(
        [a[l : l + 1, :] for l in range(layers) for a in (gain, shift, skip, vbias, gbias)]
        + [jnp.zeros((16 - PARAMS * layers, width), F32)],
        axis=0,
    )
    high = plist.astype(BF16)
    rest = (plist - high.astype(F32)).astype(BF16)
    for k, send in ((1, send1), (2, send2), (3, send3)):
        base = (mp ^ k) * rows
        send.ref[0:rows, :] = held[pl.ds(pl.multiple_of(base, SUB), rows), :].astype(BF16)
        send.ref[rows : rows + 16, :] = high
        send.ref[rows + 16 : rows + 32, :] = rest
        send.flush()
    span = rows // SUB
    table = table_out.ref
    for layer in range(layers):
        for h in range(2):
            cols = slice(h * LANES, (h + 1) * LANES)
            radius = jnp.exp(-jnp.exp(decay[layer : layer + 1, cols]))
            angle = jnp.exp(phase[layer : layer + 1, cols])
            re, im = radius * jnp.cos(angle), radius * jnp.sin(angle)
            table[layer, h : h + 1, :] = re
            table[layer, 2 + h : 3 + h, :] = im
            length = 1
            while length < rows:
                re, im = re * re - im * im, 2.0 * re * im
                length *= 2
                if length == span:
                    table[layer, 4 + h : 5 + h, :] = re
                    table[layer, 6 + h : 7 + h, :] = im
            table[layer, 8 + h : 9 + h, :] = re
            table[layer, 10 + h : 11 + h, :] = im
            table[layer, 12 + h : 13 + h, :] = jnp.exp(scale[layer : layer + 1, cols])
            table[layer, 14 + h : 15 + h, :] = jnp.zeros((1, LANES), F32)


def pack_maps(layers, copies, begin, c_own, v_own, g_own, *packs):
    begin()
    for layer in range(layers):
        for i, own in enumerate((c_own, v_own, g_own)):
            deep = own().shape[1]
            packs[layer].ref[i * deep : (i + 1) * deep, :] = own()[layer]
        packs[layer].flush()


def pack_block(copies, begin, x, *sends):
    mp, _ = place()
    rows = sends[0].ref.shape[0]
    begin()
    whole = x()
    for k, send in enumerate(sends):
        base = pl.multiple_of((mp ^ (k + 1)) * rows, SUB)
        send.ref[...] = whole[pl.ds(base, rows), :].astype(BF16)
        send.flush()


def gather_block(copies, begin, got1, got2, got3, gain, shift, skip, vbias, gbias, stream, h, prm, held):
    mp, _ = place()
    rows = h.ref.shape[1]
    own = Later(copies, [(own_rows(stream, rows), held)], held)
    begin()
    plist = [a() for a in (gain, shift, skip, vbias, gbias)]
    layers = plist[0].shape[0]
    for k, got in ((1, got1), (2, got2), (3, got3)):
        got = got()
        h.ref[mp ^ k, :, :] = got[0:rows, :].astype(F32)
        pair = got[rows : rows + 16, :].astype(F32) + got[rows + 16 : rows + 32, :].astype(F32)
        prm.ref[mp ^ k, :, :] = pair
    mine = [a[l : l + 1, :] for l in range(layers) for a in plist]
    prm.ref[mp, 0 : PARAMS * layers, :] = jnp.concatenate(mine, axis=0)
    prm.ref[mp, PARAMS * layers :, :] = jnp.zeros((16 - PARAMS * layers, LANES), F32)
    h.ref[mp, :, :] = own()[...]


def norm_rows(mean, second, gain, shift):
    inverse = lax.rsqrt(second - mean * mean + epsilon)
    factor = inverse * gain
    return inverse, factor, shift - mean * factor


def drive_body(layer, mean, second, start, h, prm, table, weight, drive, norms, out, ends_out, slow):
    rows = drive.ref.shape[1]
    reverse = layer % 2 == 1
    base = layer * PARAMS
    inverse, factor, bias = norm_rows(
        mean, second, rowcat(prm, base + GAIN), rowcat(prm, base + SHIFT)
    )
    norms.ref[...] = jnp.concatenate(
        [factor, bias, inverse, mean] + [jnp.zeros_like(mean)] * 4, axis=0
    )
    norms.flush()
    gamma = lanes(table[layer, 12:14, :])
    gamma = jnp.concatenate([gamma, gamma], axis=1)
    for i, at in enumerate(chunks(rows, 2)):
        low = (cat(h, at) * factor + bias).astype(BF16)
        slow.ref[at, :] = low
        slow.flush(i, 2)
        put(drive.ref, at, dot(low, weight()[...]) * gamma)
        drive.flush(i, 2)
    fwd, bwd = local_resets(start, rows)
    reset = bwd if reverse else fwd
    ends, _ = sweep(drive.ref, None, table[layer], zeros_state(2), reset, reverse, False)
    emit_ends(out, ends_out, ends, table[layer], reset, rows // SUB, reverse, False)


class Later:
    def __init__(self, copies, pairs, dst):
        self.waits, self.dst = [copies.start(src, to) for src, to in pairs], dst

    def __call__(self):
        for copy in self.waits:
            copy.wait()
        self.waits = []
        return self.dst


def own_rows(ref, rows, k=0):
    mp, _ = place()
    return ref.at[pl.ds(pl.multiple_of((mp ^ k) * rows, SUB), rows)]


def total_of(gathered):
    tile = gathered[0]
    for d in range(1, gathered.shape[0]):
        tile = tile + gathered[d]
    return tile


def drive_first(total_tokens, copies, begin, start, mom, table, h, prm, weight, drive, norms, out, ends, slow, maps):
    weight = Later(copies, [(weight.at[0], maps)], maps)
    mom = mom()
    groups = h.ref.shape[0]
    sums = [mom[j, 0:2, :] for j in range(groups)]
    for d in range(groups, mom.shape[0]):
        sums[d % groups] = sums[d % groups] + mom[d, 0:2, :]
    both = jnp.concatenate(sums, axis=1) * (1.0 / total_tokens)
    drive_body(0, both[0:1, :], both[1:2, :], start, h(), prm(), table(), weight, drive, norms, out, ends, slow)


def drive_next(layer, total_tokens, copies, begin, start, mom, prm, table, h, weight, drive, norms, out, ends, slow, maps):
    weight = Later(copies, [(weight.at[layer], maps)], maps)
    tile = total_of(mom()) * (1.0 / total_tokens)
    half = tile.shape[0] // 2
    mean, second = lanes(tile[:half]), lanes(tile[half:])
    drive_body(layer, mean, second, start, h(), prm(), table(), weight, drive, norms, out, ends, slow)


def resume(start, rows, gathered, mom, tab, ends, reverse, conj):
    fwd, bwd = local_resets(start, rows)
    reset = bwd if reverse else fwd
    first = carried_in(gathered, mom, tab, place()[1], reverse, conj)
    incoming, _ = chain_segments(
        [ends[k] for k in range(4)], first, tab, reset, rows // SUB, reverse, conj
    )
    return tuple(incoming), reset


def assemble(copies, begin, p0, p1, p2, p3, maps):
    begin()
    mp, _ = place()
    count, deep = maps.ref.shape[0], maps.ref.shape[1]
    for k, piece in enumerate((p0, p1, p2, p3)):
        cols = pl.ds(pl.multiple_of((mp ^ k) * LANES, LANES), LANES)
        for i in range(count):
            maps.ref[i, :, cols] = piece()[i * deep : (i + 1) * deep, :]


def fetch_maps(copies, far, near, order=(0, 1, 2)):
    return {i: Later(copies, [(far.at[i], near.at[i])], near.at[i]) for i in order}


def mix_chunk(layer, at, h, norms, states, maps, prm):
    base = layer * PARAMS
    x = cat(h, at)
    scaled = x * norms[0:1, :] + norms[1:2, :]
    states_low = cat(states, at).astype(BF16)
    mixed = dot(states_low, maps[0]()[...]) + rowcat(prm, base + SKIP) * scaled
    square = mixed * mixed
    wave = jnp.tanh(ROOT * mixed * (1.0 + CUBE * square))
    half = 0.5 * (1.0 + wave)
    sent_low = (mixed * half).astype(BF16)
    slope = half + 0.5 * mixed * (1.0 - wave * wave) * (ROOT * (1.0 + 3.0 * CUBE * square))
    value = dot(sent_low, maps[1]()[...]) + rowcat(prm, base + VBIAS)
    gate = dot(sent_low, maps[2]()[...]) + rowcat(prm, base + GBIAS)
    sig = 0.5 + 0.5 * jnp.tanh(0.5 * gate)
    gated = value * sig
    return x, scaled, states_low, sent_low, slope, sig, gated


def back_chunk(i, at, g, sig, gain_part, scaled, slope, maps, outs, sums):
    dv, dg, dml, ds = outs
    dvalue = g * sig
    dgate = g * gain_part
    dv_low, dg_low = dvalue.astype(BF16), dgate.astype(BF16)
    dmixed = (dot_nt(dv_low, maps[1]()[...]) + dot_nt(dg_low, maps[2]()[...])) * slope()
    dm_low = dmixed.astype(BF16)
    put(ds.ref, at, dot_nt(dm_low, maps[0]()[...]))
    dv.ref[at, :] = dv_low
    dg.ref[at, :] = dg_low
    dml.ref[at, :] = dm_low
    for o in outs:
        o.flush(i, 2)
    add = lambda v: jnp.sum(v, axis=0, keepdims=True)
    return [
        s + n for s, n in zip(sums, [add(dvalue), add(dgate), add(dmixed * scaled())], strict=True)
    ]


def sums_rows(sums_out, sums):
    rows = sums + [jnp.zeros_like(sums[0])] * (8 - len(sums))
    sums_out.ref[...] = jnp.concatenate(rows, axis=0)
    sums_out.flush()


def share_out(keep, send, pack, copies):
    mp, _ = place()
    for ref, i, k in ((send, 0, 1), (send, 1, 3), (keep, 0, 0), (keep, 1, 2)):
        ref.ref[i, :, :] = pack[mp ^ k, :, :]


def weight_grads(copies, begin, sent, dv, dg, states, dml, sums, keep, send, pack):
    begin()
    width = sent.dst.shape[1]
    parts = pack.shape[0]
    both = jnp.concatenate([dv()[...], dg()[...]], axis=1)
    both = dot_tn(sent()[...], both)
    put(pack, slice(0, width), both[:, :width])
    put(pack, slice(width, 2 * width), both[:, width:])
    put(pack, slice(2 * width, 3 * width), dot_tn(states()[...], dml()[...]))
    sums = sums()
    for j in range(parts):
        cols = slice(j * LANES, (j + 1) * LANES)
        rows = jnp.concatenate([sums[:, cols], jnp.zeros((8, LANES), F32)], axis=0)
        pack[j, 3 * width : 3 * width + 16, :] = rows.astype(pack.dtype)
    share_out(keep, send, pack, copies)


def input_grads(layer, copies, begin, slow, dlow, prods, weight, keep, send, pack, held, maps):
    begin()
    weight = Later(copies, [(weight.at[layer], maps)], maps)
    width = slow.dst.shape[1]
    held[...] = dot_tn(slow()[...], dlow()[...])
    half = width // 2
    y_re = y_im = jnp.zeros((1, half), F32)
    size = 64
    for top in range(0, width, size):
        rows = slice(top, top + size)
        grad = held[rows, :]
        put(pack, rows, grad)
        grad_re, grad_im = grad[:, :half], grad[:, half:]
        w = weight()[rows, :].astype(F32)
        w_re, w_im = w[:, :half], w[:, half:]
        y_re = y_re + jnp.sum(grad_re * w_re + grad_im * w_im, axis=0, keepdims=True)
        y_im = y_im + jnp.sum(grad_im * w_re - grad_re * w_im, axis=0, keepdims=True)
    prods = prods()
    rows = []
    for h in range(2):
        cols = slice(h * LANES, (h + 1) * LANES)
        rows += [prods[2 * h : 2 * h + 1, :] - y_re[:, cols], prods[2 * h + 1 : 2 * h + 2, :] - y_im[:, cols]]
        rows += [y_re[:, cols]]
    tile = jnp.concatenate(rows + [jnp.zeros((10, LANES), F32)], axis=0).astype(pack.dtype)
    for j in range(pack.shape[0]):
        pack[j, width : width + 16, :] = tile
    share_out(keep, send, pack, copies)


def add_chunk(mom, one, two):
    tile = jnp.concatenate(
        [one[:, j * LANES : (j + 1) * LANES] for j in range(one.shape[1] // LANES)]
        + [two[:, j * LANES : (j + 1) * LANES] for j in range(two.shape[1] // LANES)],
        axis=0,
    )
    mom.ref[...] = jnp.broadcast_to(tile[None], mom.ref.shape)
    mom.flush()


def mix_first(layer, copies, begin, start, gathered, mom, table, ends, norms, prm, drive, h, far_maps,
              new_h, new_mom, h_far, states_low_out, sent, slope_out, sig_out, part_out, states, maps):
    rows = states.shape[1]
    ready = fetch_maps(copies, far_maps, maps)
    copies.flush(h.ref, h_far)
    reverse = layer % 2 == 1
    tab = table()[layer]
    init, reset = resume(start, rows, gathered(), mom(), tab, ends(), reverse, False)
    sweep(drive(), states, tab, init, reset, reverse, False)
    norms, prm = norms(), prm()
    one = two = 0.0
    for i, at in enumerate(chunks(rows, 2)):
        x, scaled, states_low, sent_low, slope, sig, gated = mix_chunk(
            layer, at, h(), norms, states, ready, prm
        )
        states_low_out.ref[at, :] = states_low
        sent.ref[at, :] = sent_low
        put(slope_out.ref, at, slope)
        put(sig_out.ref, at, sig)
        put(part_out.ref, at, gated * (1.0 - sig))
        new = x + gated
        put(new_h.ref, at, new)
        one = one + jnp.sum(new, axis=0, keepdims=True)
        two = two + jnp.sum(new * new, axis=0, keepdims=True)
        for o in (states_low_out, sent, slope_out, sig_out, part_out):
            o.flush(i, 2)
    add_chunk(new_mom, one, two)


def turn(layer, copies, begin, start, gathered, mom, table, ends, norms, prm, drive, h, far_maps,
         got1, got2, got3, cot,
         ds, out, ends_out, h_far, states_low_out, full_cot, sent, dv, dg, dml, sums_out, r0, r1, r2, r3,
         maps, states, new_h, cot_blocks):
    mp, _ = place()
    rows = states.shape[1]
    ready = fetch_maps(copies, far_maps, maps)
    own_cot = Later(copies, [(own_rows(cot, rows), cot_blocks.at[mp])], cot_blocks)
    copies.flush(h.ref, h_far)
    reverse = layer % 2 == 1
    tab = table()[layer]
    init, reset = resume(start, rows, gathered(), mom(), tab, ends(), reverse, False)
    sweep(drive(), states, tab, init, reset, reverse, False)
    for k, got in ((1, got1), (2, got2), (3, got3)):
        cot_blocks[mp ^ k, :, :] = got()[...].astype(F32)
    own_cot()
    norms, prm = norms(), prm()
    sums = [0.0, 0.0, 0.0]
    for i, at in enumerate(chunks(rows, 2)):
        x, scaled, states_low, sent_low, slope, sig, gated = mix_chunk(
            layer, at, h(), norms, states, ready, prm
        )
        states_low_out.ref[at, :] = states_low
        sent.ref[at, :] = sent_low
        put(new_h, at, x + gated)
        g = cat(cot_blocks, at)
        full_cot.ref[at, :] = g.astype(BF16)
        for o in (states_low_out, sent, full_cot):
            o.flush(i, 2)
        sums = back_chunk(i, at, g, sig, gated * (1.0 - sig), lambda: scaled, lambda: slope,
                          ready, (dv, dg, dml, ds), sums)
    sums_rows(sums_out, sums)
    for k, r in enumerate((r0, r1, r2, r3)):
        r.ref[...] = new_h[mp ^ k, :, :].astype(r.ref.dtype)
        r.flush()
    adjoint_start(layer, start, tab, ds.ref, out, ends_out)


def adjoint_start(layer, start, tab, ds, out, ends_out):
    rows = ds.shape[1]
    reverse = layer % 2 == 0
    fwd, bwd = local_resets(start, rows)
    reset = bwd if reverse else fwd
    ends, _ = sweep(ds, None, tab, zeros_state(2), reset, reverse, True)
    emit_ends(out, ends_out, ends, tab, reset, rows // SUB, reverse, True)


def back_first(layer, total_tokens, copies, begin, start, back, norms1, table, prm, u, norms,
               slow1, sig, part, slope, slow, far_maps, g_out, ds, out, ends_out, tile_out, dv, dg, dml, sums_out,
               maps):
    begin()
    maps = fetch_maps(copies, far_maps, maps, (1, 2, 0))
    rows = ds.ref.shape[1]
    tile = total_of(back())
    tile_out.ref[...] = tile
    norms1, norms, prm = norms1(), norms(), prm()
    half = tile.shape[0] // 2
    base = (layer + 1) * PARAMS
    over = 1.0 / rowcat(prm, base + GAIN)
    shift = rowcat(prm, base + SHIFT)
    factor = norms1[0:1, :] * (1.0 / total_tokens)
    m_one, m_two = factor * lanes(tile[:half]), factor * over * lanes(tile[half:])
    m_one = m_one - shift * m_two
    sums = [0.0, 0.0, 0.0]
    for i, at in enumerate(chunks(rows, 2)):
        g = cat(u(), at) - m_one - slow1.part(i)[at, :].astype(F32) * m_two
        put(g_out.ref, at, g)
        sums = back_chunk(i, at, g, cat(sig.part(i), at), cat(part.part(i), at),
                          lambda: slow.part(i)[at, :].astype(F32),
                          lambda: cat(slope.part(i), at), maps, (dv, dg, dml, ds), sums)
    sums_rows(sums_out, sums)
    adjoint_start(layer, start, table()[layer], ds.ref, out, ends_out)


def back_second(layer, copies, begin, start, gathered, mom, table, ends, norms, prm, ds, states_low, g, dml, h,
                weight, *refs):
    if layer == 0:
        back, prods, dlow, u0, u1, u2, u3, adj, states, maps, u_ref = refs
    else:
        back, u_out, prods, dlow, adj, states, maps = refs
        u_ref = u_out.ref
    begin()
    weight = Later(copies, [(weight.at[layer], maps)], maps)
    rows = adj.shape[1]
    reverse = layer % 2 == 0
    tab = table()[layer]
    init, reset = resume(start, rows, gathered(), mom(), tab, ends(), reverse, True)
    for at in chunks(rows, 8):
        put(states, at, states_low()[at, :].astype(F32))

    def extra(at, a, sums):
        new = []
        for h_ in range(2):
            re, im = a[h_], a[2 + h_]
            sre, sim = states[h_, at, :], states[2 + h_, at, :]
            new.append(re * sre + im * sim)
            new.append(im * sre - re * sim)
        return tuple(s + n for s, n in zip(sums, new, strict=True))

    _, sums = sweep(ds(), adj, tab, init, reset, reverse, True, extra)
    flat = [jnp.sum(s, axis=0, keepdims=True) for s in sums]
    prods.ref[...] = jnp.concatenate(flat + [jnp.zeros((8 - len(flat), LANES), F32)], axis=0)
    prods.flush()
    gamma = lanes(tab[12:14, :])
    gamma = jnp.concatenate([gamma, gamma], axis=1)
    base = layer * PARAMS
    prm, norms = prm(), norms()
    skip = rowcat(prm, base + SKIP)
    factor, bias, inverse, mean = (norms[i : i + 1, :] for i in range(4))
    one = two = 0.0
    for i, at in enumerate(chunks(rows, 2)):
        low = (cat(adj, at) * gamma).astype(BF16)
        dlow.ref[at, :] = low
        dlow.flush(i, 2)
        dscaled = dot_nt(low, weight()[...]) + dml.part(i)[at, :].astype(F32) * skip
        normed = (cat(h.part(i), at) - mean) * inverse
        own = g()[at, :].astype(F32) if layer == 1 else cat(g(), at)
        put(u_ref, at, own + factor * dscaled)
        one = one + jnp.sum(dscaled, axis=0, keepdims=True)
        two = two + jnp.sum(dscaled * normed, axis=0, keepdims=True)
    add_chunk(back, one, two)
    if layer == 0:
        mp, _ = place()
        for k, piece in enumerate((u0, u1, u2, u3)):
            piece.ref[...] = u_ref[mp ^ k, :, :].astype(piece.ref.dtype)
            piece.flush()


def result_kernel(copies, begin, r0, r1, r2, r3, result):
    begin()
    mp, _ = place()
    rows = r0.dst.shape[0]
    for k, r in ((1, r1), (2, r2), (3, r3), (0, r0)):
        at = pl.ds(pl.multiple_of((mp ^ k) * rows, SUB), rows)
        result.ref[at, :] = r()[...].astype(F32)
        copies.flush(result.ref.at[at], result.dst.at[at])
    result.sent = True


def last_kernel(total_tokens, copies, begin, norms, back, tile1, u0, u1, u2, u3, stream,
                out, gain_out, shift_out, held):
    begin()
    mp, _ = place()
    rows = u0.dst.shape[0]
    streams = [Later(copies, [(own_rows(stream, rows, k), held.at[k])], held.at[k]) for k in range(4)]
    tile, tile1, norms = total_of(back()), tile1(), norms()
    half = tile.shape[0] // 2
    zero = jnp.zeros((1, LANES), F32)
    one, two, factor, inverse, mean, later_one, later_two = [zero] * 7
    for j in range(half):
        mine = jnp.where(mp == j, 1.0, 0.0)
        cols = slice(j * LANES, (j + 1) * LANES)
        one = one + mine * tile[j : j + 1, :]
        two = two + mine * tile[half + j : half + j + 1, :]
        later_one = later_one + mine * tile1[j : j + 1, :]
        later_two = later_two + mine * tile1[half + j : half + j + 1, :]
        factor = factor + mine * norms[0:1, cols]
        inverse = inverse + mine * norms[2:3, cols]
        mean = mean + mine * norms[3:4, cols]
    scaled = factor * (1.0 / total_tokens)
    m_one, m_two = scaled * one, scaled * two
    for k, u in enumerate((u0, u1, u2, u3)):
        at = pl.ds(pl.multiple_of((mp ^ k) * rows, SUB), rows)
        normed = (streams[k]()[...] - mean) * inverse
        out.ref[at, :] = u()[...].astype(F32) - m_one - normed * m_two
        copies.flush(out.ref.at[at], out.dst.at[at])
    out.sent = True
    gain_out.ref[...] = jnp.concatenate([two, later_two], axis=0)
    shift_out.ref[...] = jnp.concatenate([one, later_one], axis=0)


def pair_sum(copies, begin, keep, got, mine, other):
    keep, got = keep(), got()
    size = keep.shape[1]
    for at in chunks(size, size // 16):
        other.ref[at, :] = (keep[1, at, :].astype(F32) + got[1, at, :].astype(F32)).astype(other.ref.dtype)
        mine.ref[at, :] = (keep[0, at, :].astype(F32) + got[0, at, :].astype(F32)).astype(mine.ref.dtype)


def four_sum(copies, begin, *refs):
    *ins, out = refs
    out = out.ref
    top = 0
    for mine, got in zip(ins[::2], ins[1::2], strict=True):
        mine, got = mine(), got()
        rows = mine.shape[0]
        for at in chunks(rows, rows // 16):
            total = mine[at, :].astype(F32) + got[at, :].astype(F32)
            out[top + at.start : top + at.stop, :] = total.astype(out.dtype)
        top += rows
    if top < out.shape[0]:
        out[top:, :] = jnp.zeros((out.shape[0] - top, out.shape[1]), out.dtype)


def piece_sum(copies, begin, pieces, out):
    pieces = pieces()
    count, rows = pieces.shape[0], pieces.shape[1]
    for at in chunks(rows, rows // 16):
        total = pieces[0, at, :].astype(F32)
        for d in range(1, count):
            total = total + pieces[d, at, :].astype(F32)
        low = total.astype(out.ref.dtype)
        for d in range(count):
            out.ref[d, at, :] = low


def hand_out(features, copies, begin, decay, phase, full0,
             in_own, o_grad, skip_grad, v_grad, g_grad, vb, gb, d_grad, p_grad, s_grad):
    begin()
    in_rows = features + 16
    full0 = full0()
    for layer in range(2):
        top = layer * in_rows
        in_own.ref[layer, :, :] = full0[top : top + features, :]
    decay, phase = decay(), phase()
    for layer, full, top in ((0, full0, 2 * in_rows), (1, full0, 2 * in_rows + 3 * features + 16)):
        for i, out in enumerate((v_grad, g_grad, o_grad)):
            out.ref[layer, :, :] = full[top + i * features : top + (i + 1) * features, :].astype(F32)
            copies.flush(out.ref.at[layer], out.dst.at[layer])
            out.sent = True
        top += 3 * features
        row = slice(layer, layer + 1)
        vecs = full[top : top + 16, :].astype(F32)
        vb.ref[row, :] = vecs[0:1, :]
        gb.ref[row, :] = vecs[1:2, :]
        skip_grad.ref[row, :] = vecs[2:3, :]
        top = layer * in_rows + features
        tile = full0[top : top + 16, :].astype(F32)
        for h in range(2):
            cols = slice(h * LANES, (h + 1) * LANES)
            d_grad.ref[row, cols] = -jnp.exp(decay[row, cols]) * tile[3 * h : 3 * h + 1, :]
            p_grad.ref[row, cols] = jnp.exp(phase[row, cols]) * tile[3 * h + 1 : 3 * h + 2, :]
            s_grad.ref[row, cols] = tile[3 * h + 2 : 3 * h + 3, :]


def input_kernel(copies, begin, p0, p1, p2, p3, out):
    begin()
    mp, _ = place()
    for k, piece in enumerate((p0, p1, p2, p3)):
        cols = pl.ds(pl.multiple_of((mp ^ k) * LANES, LANES), LANES)
        piece = piece()
        for layer in range(out.ref.shape[0]):
            out.ref[layer, :, cols] = piece[layer].astype(F32)


def shape(dims, dtype=F32):
    return jax.ShapeDtypeStruct(tuple(dims), dtype)


def every(x):
    return lax.all_to_all(x, AXES, 0, 0)


def hop(x, k):
    count = lax.axis_size("mp")
    return lax.ppermute(x, "mp", [(i, i ^ k) for i in range(count)])


def spread(x, then=None):
    far = hop(x, 2)
    held = far if then is None else after(far, then)
    return hop(x, 1), far, hop(held, 1)


def swap(sends):
    return [hop(x, k + 1) for k, x in enumerate(sends)]


def after(x, *ys):
    return lax.optimization_barrier((x, *ys))[0]


def on_device(
    stream,
    cotangent,
    start_offsets,
    norm_gain,
    norm_shift,
    input_map,
    decay_log,
    phase_log,
    scale_log,
    output_map,
    skip_gain,
    value_weight,
    gate_weight,
    value_bias,
    gate_bias,
):
    block, width = stream.shape
    layers = input_map.shape[0]
    count_dp, parts = lax.axis_size("dp"), lax.axis_size("mp")
    devices = count_dp * parts
    tokens = block * count_dp
    rows = block // parts
    features = width * parts
    assert width == LANES and features == 4 * LANES and layers == 2 and parts == 4

    plist = (norm_gain, norm_shift, skip_gain, value_bias, gate_bias)
    blocks = shape((parts, rows, width))
    v_blocks = pltpu.VMEM(blocks.shape, F32)
    one_block = (rows, width)
    low_block = shape(one_block, BF16)
    wide_low = shape((rows, features), BF16)
    near_blocks = Near(blocks)
    near_ends = Near(shape((4, SUB, LANES)))
    near_every = Near(shape((devices, 4, LANES)))
    near_sums = Near(shape((devices, 2 * parts, LANES)))
    near_norms = Near(shape((8, features)))
    near_low = Near(low_block)
    packed_w = shape((3 * features, width), BF16)
    one_map = pltpu.VMEM((features, features), BF16)
    maps = pltpu.VMEM((3, features, features), BF16)
    all_maps = shape((3, features, features), BF16)

    mom_out, table, *sends = call(
        functools.partial(first_kernel, rows),
        [near_every, Near(shape((layers, 16, LANES)))] + [Near(shape((rows + 32, width), BF16))] * 3,
        [pltpu.VMEM((block, width), F32)],
        start_offsets, Raw(stream), *plist, decay_log, phase_log, scale_log,
        scalars=1,
    )
    table = Near(table)
    got_h = [Near(x) for x in swap(sends)]
    mom0 = Near(every(after(mom_out, got_h[1].array)))
    h0, prm = call(
        gather_block,
        [near_blocks, Near(shape((parts, 16, width)))],
        [pltpu.VMEM(one_block, F32)],
        *got_h, *plist, Raw(stream),
    )
    h0, prm = Near(h0), Near(prm)
    packs = call(
        functools.partial(pack_maps, layers), [packed_w] * layers, [], output_map, value_weight, gate_weight
    )
    w0 = after(packs[0], got_h[1].array, got_h[2].array)
    (full0,) = call(assemble, [all_maps], [], w0, *[Near(w) for w in spread(w0, mom0.array)])

    drive0, norms0, ends_all, ends0, slow0 = call(
        functools.partial(drive_first, tokens),
        [near_blocks, near_norms, near_every, near_ends, wide_low],
        [one_map],
        start_offsets, mom0, table, h0, prm, Raw(input_map),
        scalars=1,
    )
    got = Near(after(every(ends_all), full0))
    norms0 = Near(norms0)
    h1, mom_out, h0, states0, sent0, slope0, sig0, part0 = call(
        functools.partial(mix_first, 0),
        [near_blocks, near_sums, Raw(blocks), wide_low, wide_low,
         blocks, blocks, blocks],
        [v_blocks, maps],
        start_offsets, got, mom0, table, Near(ends0), norms0, prm, Near(drive0), h0, Raw(full0),
        scalars=1,
    )
    h1 = Near(h1)
    sends = call(pack_block, [low_block] * 3, [], after(cotangent, got.array))
    mom1 = Near(after(every(mom_out), *sends))
    got_cot = [Near(x) for x in swap(sends)]
    w1 = after(packs[1], got.array)
    (full1,) = call(assemble, [all_maps], [], w1, *[Near(w) for w in spread(w1, mom1.array)])
    drive1, norms1, ends_all, ends1, slow1 = call(
        functools.partial(drive_next, 1, tokens),
        [near_blocks, near_norms, near_every, near_ends, wide_low],
        [one_map],
        start_offsets, mom1, prm, table, h1, Raw(input_map),
        scalars=1,
    )
    got = Near(after(every(ends_all), full1))
    norms1 = Near(norms1)
    vgo_rows, in_rows = 3 * features + 16, features + 16

    def pair_share(keep, send):
        size = Near(shape(keep.shape[1:], BF16))
        return call(pair_sum, [size, size], [], Near(keep), Near(hop(send, 1)))

    vgo_half = Near(shape((2, vgo_rows, width), BF16))
    in_half = Near(shape((2, in_rows, width), BF16))
    vgo_pack = pltpu.VMEM((parts, vgo_rows, width), BF16)
    in_pack = pltpu.VMEM((parts, in_rows, width), BF16)
    in_room = [in_pack, pltpu.VMEM((features, features), F32), one_map]
    ds1, ends_all, back_ends1, h1, states1, cot, sent1, dv, dg, dml1, sums, *res = call(
        functools.partial(turn, 1),
        [near_blocks, near_every, near_ends, Raw(blocks)] + [wide_low] * 6 + [near_norms.array, shape(one_block)]
        + [low_block] * 3,
        [maps, v_blocks, v_blocks, v_blocks],
        start_offsets, got, mom0, table, Near(ends1), norms1, prm, Near(drive1), h1, Raw(full1), *got_cot, Raw(cotangent),
        scalars=1,
    )
    got = Near(every(ends_all))
    keep1, send1 = call(
        weight_grads, [vgo_half, vgo_half], [vgo_pack], sent1, dv, dg, states1, dml1, sums
    )
    got = Near(after(got.array, keep1))
    send1 = after(send1, got.array)
    got = Near(after(got.array, keep1))
    back_out, u1, prods, dlow = call(
        functools.partial(back_second, 1),
        [near_sums, near_blocks, Near(shape((8, LANES))), Near(wide_low)],
        [v_blocks, v_blocks, one_map],
        start_offsets, got, mom0, table, Near(back_ends1), norms1, prm, Near(ds1), states1, cot, Halves(dml1),
        Halves(h1), Raw(input_map),
        scalars=1,
    )
    back1 = Near(every(back_out))
    in_keep1, in_send1 = call(
        functools.partial(input_grads, 1), [in_half, in_half], in_room, slow1, Near(dlow), Near(prods), Raw(input_map)
    )
    mine1, other1 = pair_share(keep1, send1)
    in_send1 = after(in_send1, back1.array)
    back1 = Near(after(back1.array, in_keep1, mine1))
    far1 = hop(other1, 2)
    g0, ds0, ends_all, back_ends0, tile1, dv, dg, dml0, sums = call(
        functools.partial(back_first, 0, tokens),
        [near_blocks, near_blocks, near_every, near_ends, Near(shape((2 * parts, LANES)))] + [wide_low] * 3
        + [near_norms.array],
        [maps],
        start_offsets, back1, norms1, table, prm, Near(u1), norms0,
        Halves(slow1), Halves(sig0), Halves(part0), Halves(slope0), Halves(slow0), Raw(full0),
        scalars=1,
    )
    got = Near(every(after(ends_all, far1)))
    keep0, send0 = call(
        weight_grads, [vgo_half, vgo_half], [vgo_pack], sent0, dv, dg, states0, dml0, sums
    )
    in_mine1, in_other1 = pair_share(in_keep1, in_send1)
    in_far1 = hop(in_other1, 2)
    send0 = after(send0, got.array)
    got = Near(after(got.array, keep0, in_mine1))
    back_out, prods, dlow, *us = call(
        functools.partial(back_second, 0),
        [near_sums, Near(shape((8, LANES))), Near(wide_low), Near(shape(one_block))] + [near_low] * 3,
        [v_blocks, v_blocks, one_map, v_blocks],
        start_offsets, got, mom0, table, Near(back_ends0), norms0, prm, Near(ds0), states0, Near(g0), Halves(dml0),
        Halves(h0), Raw(input_map),
        scalars=1,
    )
    in_keep0, in_send0 = call(
        functools.partial(input_grads, 0), [in_half, in_half], in_room, slow0, Near(dlow), Near(prods), Raw(input_map)
    )
    mine0, other0 = pair_share(keep0, send0)
    far0 = hop(other0, 2)
    us = (us[0], *swap([after(u, in_send0) for u in us[1:]]))
    back0 = Near(every(after(back_out, in_send0, mine0)))
    in_mine0, in_other0 = pair_share(in_keep0, in_send0)
    in_far0 = hop(in_other0, 2)
    back0 = Near(after(back0.array, in_mine0))
    stream_grad, gain_grad, shift_grad = call(
        functools.partial(last_kernel, tokens),
        [shape((block, width)), shape((layers, width)), shape((layers, width))],
        [pltpu.VMEM((4,) + one_block, F32)],
        norms0, back0, Near(tile1), *[Near(u) for u in us], Raw(stream),
    )

    full_rows = 2 * (vgo_rows + in_rows)
    unit = 16 * count_dp
    padded = -(-full_rows // unit) * unit
    (own0,) = call(
        four_sum, [Near(shape((padded, width), BF16))], [],
        Near(in_mine0), Near(in_far0), Near(in_mine1), Near(in_far1), Near(mine0), Near(far0), Near(mine1), Near(far1),
    )
    split = (count_dp, padded // count_dp, width)
    pieces = lax.all_to_all(after(own0, back0.array).reshape(split), "dp", 0, 0)
    (copied,) = call(piece_sum, [Near(shape(split, BF16))], [], Near(pieces))
    copied = after(copied, stream_grad)
    result = [res[0], *swap([after(r, copied) for r in res[1:]])]
    (result,) = call(result_kernel, [shape((block, width))], [], res[0], *[Near(r) for r in result[1:]])
    full0 = lax.all_to_all(copied, "dp", 0, 0).reshape(padded, width)
    full0 = after(full0, result)
    mat, vec, state = shape((layers, features, width)), shape((layers, width)), shape(decay_log.shape)
    in_own, o_grad, skip_grad, v_grad, g_grad, vb, gb, d_grad, p_grad, s_grad = call(
        functools.partial(hand_out, features),
        [Near(shape((layers, features, width), BF16)), mat, vec, mat, mat, vec, vec, state, state, state],
        [],
        decay_log, phase_log, Near(full0),
    )
    (input_grad,) = call(
        input_kernel, [shape((layers, features, features))], [], Near(in_own), *[Near(x) for x in spread(in_own)]
    )
    return (
        result, stream_grad, gain_grad, shift_grad, input_grad, d_grad, p_grad, s_grad,
        o_grad, skip_grad, v_grad, g_grad, vb, gb,
    )


def solution(mesh):
    split = P("dp", "mp")
    cols = P(None, "mp")
    wide = P(None, None, "mp")
    placed = (
        split, split, P("dp"), cols, cols, P(), P(), P(), P(), wide, cols, wide, wide, cols, cols,
    )
    return jax.shard_map(
        on_device,
        mesh=mesh,
        in_specs=placed,
        out_specs=(
            split, split, cols, cols, P(), P(), P(), P(), wide, cols, wide, wide, cols, cols,
        ),
        check_vma=False,
    )
```

```python
import functools

import jax
import jax.numpy as jnp
from jax import lax
from jax.experimental import pallas as pl
from jax.experimental.pallas import tpu as pltpu
from jax.sharding import PartitionSpec as P

epsilon = 1e-05
LANES = 128
SUB = 8
ROOT = 0.7978845608028654
CUBE = 0.044715
AXES = ("dp", "mp")
F32 = jnp.float32
BF16 = jnp.bfloat16
NT = (((1,), (1,)), ((), ()))
TN = (((0,), (0,)), ((), ()))
GAIN, SHIFT, SKIP, VBIAS, GBIAS = range(5)
PARAMS = 5


class Copies:
    def __init__(self, sems):
        self.sems, self.used, self.open = sems, 0, []

    def start(self, src, dst):
        copy = pltpu.make_async_copy(src, dst, self.sems.at[self.used])
        self.used += 1
        copy.start()
        return copy

    def flush(self, src, dst):
        self.open.append(self.start(src, dst))

    def finish(self):
        for copy in self.open:
            copy.wait()
        self.open = []


def along(ref, part, parts):
    if parts == 1:
        return ref
    axis = len(ref.shape) - 2
    size = ref.shape[axis] // parts
    at = pl.ds(part * size, size)
    return ref.at[at] if axis == 0 else ref.at[:, at]


class Arrival:
    def __init__(self, copies, src, dst, parts):
        self.copies, self.src, self.dst, self.parts = copies, src, dst, parts
        self.waits = [None] * parts

    def begin(self, part):
        src, dst = (along(r, part, self.parts) for r in (self.src, self.dst))
        self.waits[part] = self.copies.start(src, dst)

    def part(self, part):
        if self.waits[part] is not None:
            self.waits[part].wait()
            self.waits[part] = None
        return self.dst

    def __call__(self):
        for part in range(self.parts):
            self.part(part)
        return self.dst


class Result:
    def __init__(self, copies, ref, dst):
        self.copies, self.ref, self.dst, self.sent = copies, ref, dst, False

    def flush(self, part=0, parts=1):
        self.sent = True
        self.copies.flush(along(self.ref, part, parts), along(self.dst, part, parts))


class Raw:
    def __init__(self, array):
        self.array = array


class Halves:
    def __init__(self, array):
        self.array = array


class Near:
    def __init__(self, array):
        self.array = array


class Here:
    def __init__(self, ref):
        self.ref = self.dst = ref

    def part(self, part):
        return self.ref

    def __call__(self):
        return self.ref

    def flush(self, part=0, parts=1):
        pass


def call(body, outs, scratch, *args, scalars=0):
    wraps = (Raw, Halves, Near)
    plain = [a.array if isinstance(a, wraps) else a for a in args]
    out_shapes = [o.array if isinstance(o, wraps) else o for o in outs]
    autos = [i for i, a in enumerate(args) if i >= scalars and not isinstance(a, (Raw, Near))]
    made = [i for i, o in enumerate(outs) if not isinstance(o, (Raw, Near))]
    rooms = [pltpu.VMEM(plain[i].shape, plain[i].dtype) for i in autos]
    rooms += [pltpu.VMEM(out_shapes[i].shape, out_shapes[i].dtype) for i in made]

    def kernel(*refs):
        ins, refs = refs[: len(args)], refs[len(args) :]
        dsts, refs = refs[: len(outs)], refs[len(outs) :]
        sems, refs = refs[0], refs[1:]
        vin, refs = refs[: len(autos)], refs[len(autos) :]
        vout, rest = refs[: len(made)], refs[len(made) :]
        copies = Copies(sems)
        operands = [Here(r) if isinstance(a, Near) else r for a, r in zip(args, ins, strict=True)]
        for i, room in zip(autos, vin, strict=True):
            parts = 2 if isinstance(args[i], Halves) else 1
            operands[i] = Arrival(copies, ins[i], room, parts)
        results = [Here(r) if isinstance(o, Near) else r for o, r in zip(outs, dsts, strict=True)]
        for i, room in zip(made, vout, strict=True):
            results[i] = Result(copies, room, dsts[i])

        def begin(*some):
            for one in some or [operands[i] for i in autos]:
                operand, parts = one if isinstance(one, tuple) else (one, None)
                for part in range(operand.parts) if parts is None else (parts,):
                    operand.begin(part)

        body(copies, begin, *operands, *results, *rest)
        for r in results:
            if isinstance(r, Result) and not r.sent:
                r.flush()
        copies.finish()
        used.append(copies.used)

    near = pl.BlockSpec(memory_space=pltpu.VMEM)
    far = pl.BlockSpec(memory_space=pltpu.HBM)
    plain[scalars:] = [
        a if isinstance(w, Near) else pltpu.with_memory_space_constraint(a, pltpu.HBM)
        for w, a in zip(args[scalars:], plain[scalars:], strict=True)
    ]
    used = []

    def made_call(count):
        return pl.pallas_call(
            kernel,
            out_shape=[
                s if isinstance(o, Near) else pltpu.HBM(s.shape, s.dtype)
                for o, s in zip(outs, out_shapes, strict=True)
            ],
            in_specs=[pl.BlockSpec(memory_space=pltpu.SMEM)] * scalars
            + [near if isinstance(a, Near) else far for a in args[scalars:]],
            out_specs=[near if isinstance(o, Near) else far for o in outs],
            scratch_shapes=[pltpu.SemaphoreType.DMA((count,))] + rooms + list(scratch),
            compiler_params=pltpu.CompilerParams(vmem_limit_bytes=32 * 1024 * 1024),
        )

    jax.eval_shape(made_call(128), *plain)
    return made_call(max(used[0], 1))(*plain)


def cat(ref, rows):
    return jnp.concatenate([ref[j, rows, :] for j in range(ref.shape[0])], axis=1)


def put(ref, rows, val):
    for j in range(ref.shape[0]):
        ref[j, rows, :] = val[:, j * LANES : (j + 1) * LANES].astype(ref.dtype)


def rowcat(ref, r):
    return jnp.concatenate([ref[j, r : r + 1, :] for j in range(ref.shape[0])], axis=1)


def lanes(rows):
    return jnp.concatenate([rows[j : j + 1, :] for j in range(rows.shape[0])], axis=1)


def dot(a, b):
    return jnp.dot(a, b, preferred_element_type=F32)


def dot_nt(a, b):
    return lax.dot_general(a, b, NT, preferred_element_type=F32)


def dot_tn(a, b):
    return lax.dot_general(a, b, TN, preferred_element_type=F32)


def chunks(rows, count):
    size = rows // count
    return [slice(i * size, (i + 1) * size) for i in range(count)]


def sweep(src, dst, table, init, reset, reverse, conj):
    halves = src.shape[0] // 2
    span = src.shape[1] // SUB
    rate_re = [jnp.broadcast_to(table[h : h + 1, :], (SUB, LANES)) for h in range(halves)]
    rate_im = [
        jnp.broadcast_to(table[halves + h : halves + h + 1, :], (SUB, LANES))
        for h in range(halves)
    ]
    if conj:
        rate_im = [-r for r in rate_im]
    base = lax.broadcasted_iota(jnp.int32, (SUB, LANES), 0) * span - reset

    def body(step, state):
        j = span - 1 - step if reverse else step
        drop = base == -j
        at = pl.ds(j, SUB, stride=span)
        new_re, new_im = [], []
        for h in range(halves):
            a = jnp.where(drop, 0.0, rate_re[h])
            b = jnp.where(drop, 0.0, rate_im[h])
            re, im = state[h], state[halves + h]
            new_re.append((src[h, at, :] + a * re) - b * im)
            new_im.append((src[halves + h, at, :] + a * im) + b * re)
        state = tuple(new_re + new_im)
        if dst is not None:
            for k in range(2 * halves):
                dst[k, at, :] = state[k]
        return state

    return lax.fori_loop(0, span, body, init, unroll=8)


def zeros_state(halves):
    return tuple(jnp.zeros((SUB, LANES), F32) for _ in range(2 * halves))


def chain_segments(ends, first, table, reset, span, reverse, conj):
    halves = len(ends) // 2
    power_re = [table[4 + h : 5 + h, :] for h in range(halves)]
    power_im = [table[6 + h : 7 + h, :] for h in range(halves)]
    if conj:
        power_im = [-r for r in power_im]
    state = list(first)
    incoming = [[None] * SUB for _ in ends]
    order = range(SUB - 1, -1, -1) if reverse else range(SUB)
    for k in order:
        inside = (reset >= k * span) & (reset < (k + 1) * span)
        keep = jnp.where(inside, 0.0, 1.0)
        new = [None] * len(ends)
        for h in range(halves):
            re, im = state[h], state[halves + h]
            incoming[h][k], incoming[halves + h][k] = re, im
            new[h] = keep * (power_re[h] * re - power_im[h] * im) + ends[h][k : k + 1, :]
            new[halves + h] = (
                keep * (power_re[h] * im + power_im[h] * re) + ends[halves + h][k : k + 1, :]
            )
        state = new
    return [jnp.concatenate(rows, axis=0) for rows in incoming], state


def zero_rows(halves):
    return [jnp.zeros((1, LANES), F32) for _ in range(2 * halves)]


def emit_ends(out, ends_out, ends, table, reset, span, reverse, conj):
    halves = len(ends) // 2
    _, last = chain_segments(ends, zero_rows(halves), table, reset, span, reverse, conj)
    tile = jnp.concatenate(last, axis=0)
    out.ref[...] = jnp.broadcast_to(tile[None], out.ref.shape)
    out.flush()
    for k in range(2 * halves):
        ends_out.ref[k, :, :] = ends[k]
    ends_out.flush()


def carried_in(gathered, moments, table, me, reverse, conj):
    count = gathered.shape[0]
    power_re = table[8:10, :]
    power_im = table[10:12, :]
    if conj:
        power_im = -power_im
    flag = 3 if reverse else 2

    def body(i, state):
        d = count - 1 - i if reverse else i
        re, im = state
        keep = moments[d, flag : flag + 1, :]
        tile = gathered[d]
        return (
            keep * (power_re * re - power_im * im) + tile[0:2, :],
            keep * (power_re * im + power_im * re) + tile[2:4, :],
        )

    zero = jnp.zeros((2, LANES), F32)
    re, im = lax.fori_loop(0, count - 1 - me if reverse else me, body, (zero, zero))
    return [re[0:1, :], re[1:2, :], im[0:1, :], im[1:2, :]]


def place():
    mp = lax.axis_index("mp")
    return mp, lax.axis_index("dp") * lax.axis_size("mp") + mp


def local_resets(start, rows):
    offset = start[0]
    shift = jnp.where(offset > 0, offset - lax.axis_index("mp") * rows, -(1 << 20))
    return shift, shift - 1


def first_kernel(rows, copies, begin, start, stream, gain, shift, skip, vbias, gbias, decay, phase, scale,
                 moments, table_out, send1, send2, send3, held):
    mp, _ = place()
    total, width = held.shape
    parts = total // rows
    arrive = [copies.start(along(stream, i, parts), along(held, i, parts)) for i in range(parts)]
    begin()
    size = 128
    one = two = jnp.zeros((SUB, LANES), F32)

    def body(i, carry):
        one, two = carry
        x = held[pl.ds(i * size, size), :]
        for g in range(0, size, SUB):
            piece = x[g : g + SUB, :]
            one = one + piece
            two = two + piece * piece
        return one, two

    for i in range(parts):
        arrive[i].wait()
        one, two = lax.fori_loop(i * rows // size, (i + 1) * rows // size, body, (one, two))
    fwd, bwd = local_resets(start, rows)
    keep_f = jnp.where((fwd >= 0) & (fwd < rows), 0.0, 1.0)
    keep_b = jnp.where((bwd >= 0) & (bwd < rows), 0.0, 1.0)
    tile = jnp.concatenate(
        [
            jnp.sum(one, axis=0, keepdims=True),
            jnp.sum(two, axis=0, keepdims=True),
            jnp.full((1, LANES), keep_f, F32),
            jnp.full((1, LANES), keep_b, F32),
        ],
        axis=0,
    )
    moments.ref[...] = jnp.broadcast_to(tile[None], moments.ref.shape)
    moments.flush()
    gain, shift, skip, vbias, gbias = (a() for a in (gain, shift, skip, vbias, gbias))
    decay, phase, scale = decay(), phase(), scale()
    layers = decay.shape[0]
    plist = jnp.concatenate(
        [a[l : l + 1, :] for l in range(layers) for a in (gain, shift, skip, vbias, gbias)]
        + [jnp.zeros((16 - PARAMS * layers, width), F32)],
        axis=0,
    )
    high = plist.astype(BF16)
    rest = (plist - high.astype(F32)).astype(BF16)
    for k, send in ((1, send1), (2, send2), (3, send3)):
        base = (mp ^ k) * rows
        send.ref[0:rows, :] = held[pl.ds(pl.multiple_of(base, SUB), rows), :].astype(BF16)
        send.ref[rows : rows + 16, :] = high
        send.ref[rows + 16 : rows + 32, :] = rest
        send.flush()
    span = rows // SUB
    table = table_out.ref
    for layer in range(layers):
        for h in range(2):
            cols = slice(h * LANES, (h + 1) * LANES)
            radius = jnp.exp(-jnp.exp(decay[layer : layer + 1, cols]))
            angle = jnp.exp(phase[layer : layer + 1, cols])
            re, im = radius * jnp.cos(angle), radius * jnp.sin(angle)
            table[layer, h : h + 1, :] = re
            table[layer, 2 + h : 3 + h, :] = im
            length = 1
            while length < rows:
                re, im = re * re - im * im, 2.0 * re * im
                length *= 2
                if length == span:
                    table[layer, 4 + h : 5 + h, :] = re
                    table[layer, 6 + h : 7 + h, :] = im
            table[layer, 8 + h : 9 + h, :] = re
            table[layer, 10 + h : 11 + h, :] = im
            table[layer, 12 + h : 13 + h, :] = jnp.exp(scale[layer : layer + 1, cols])
            table[layer, 14 + h : 15 + h, :] = jnp.zeros((1, LANES), F32)


def pack_maps(layers, copies, begin, c_own, v_own, g_own, *packs):
    begin()
    for layer in range(layers):
        for i, own in enumerate((c_own, v_own, g_own)):
            deep = own().shape[1]
            packs[layer].ref[i * deep : (i + 1) * deep, :] = own()[layer]
        packs[layer].flush()


def pack_block(copies, begin, x, *sends):
    mp, _ = place()
    rows = sends[0].ref.shape[0]
    begin()
    whole = x()
    for k, send in enumerate(sends):
        base = pl.multiple_of((mp ^ (k + 1)) * rows, SUB)
        send.ref[...] = whole[pl.ds(base, rows), :].astype(BF16)
        send.flush()


def gather_block(copies, begin, got1, got2, got3, gain, shift, skip, vbias, gbias, stream, h, prm, held):
    mp, _ = place()
    rows = h.ref.shape[1]
    own = Later(copies, [(own_rows(stream, rows), held)], held)
    begin()
    plist = [a() for a in (gain, shift, skip, vbias, gbias)]
    layers = plist[0].shape[0]
    for k, got in ((1, got1), (2, got2), (3, got3)):
        got = got()
        h.ref[mp ^ k, :, :] = got[0:rows, :].astype(F32)
        pair = got[rows : rows + 16, :].astype(F32) + got[rows + 16 : rows + 32, :].astype(F32)
        prm.ref[mp ^ k, :, :] = pair
    mine = [a[l : l + 1, :] for l in range(layers) for a in plist]
    prm.ref[mp, 0 : PARAMS * layers, :] = jnp.concatenate(mine, axis=0)
    prm.ref[mp, PARAMS * layers :, :] = jnp.zeros((16 - PARAMS * layers, LANES), F32)
    h.ref[mp, :, :] = own()[...]


def norm_rows(mean, second, gain, shift):
    inverse = lax.rsqrt(second - mean * mean + epsilon)
    factor = inverse * gain
    return inverse, factor, shift - mean * factor


def drive_body(layer, mean, second, start, h, prm, table, weight, drive, norms, out, ends_out, slow):
    rows = drive.ref.shape[1]
    reverse = layer % 2 == 1
    base = layer * PARAMS
    inverse, factor, bias = norm_rows(
        mean, second, rowcat(prm, base + GAIN), rowcat(prm, base + SHIFT)
    )
    norms.ref[...] = jnp.concatenate(
        [factor, bias, inverse, mean] + [jnp.zeros_like(mean)] * 4, axis=0
    )
    norms.flush()
    gamma = lanes(table[layer, 12:14, :])
    gamma = jnp.concatenate([gamma, gamma], axis=1)
    for i, at in enumerate(chunks(rows, 2)):
        low = (cat(h, at) * factor + bias).astype(BF16)
        slow.ref[at, :] = low
        slow.flush(i, 2)
        put(drive.ref, at, dot(low, weight()[...]) * gamma)
        drive.flush(i, 2)
    fwd, bwd = local_resets(start, rows)
    reset = bwd if reverse else fwd
    ends = sweep(drive.ref, None, table[layer], zeros_state(2), reset, reverse, False)
    emit_ends(out, ends_out, ends, table[layer], reset, rows // SUB, reverse, False)


class Later:
    def __init__(self, copies, pairs, dst):
        self.waits, self.dst = [copies.start(src, to) for src, to in pairs], dst

    def __call__(self):
        for copy in self.waits:
            copy.wait()
        self.waits = []
        return self.dst


def own_rows(ref, rows, k=0):
    mp, _ = place()
    return ref.at[pl.ds(pl.multiple_of((mp ^ k) * rows, SUB), rows)]


def total_of(gathered):
    tile = gathered[0]
    for d in range(1, gathered.shape[0]):
        tile = tile + gathered[d]
    return tile


def drive_first(total_tokens, copies, begin, start, mom, table, h, prm, weight, drive, norms, out, ends, slow, maps):
    weight = Later(copies, [(weight.at[0], maps)], maps)
    mom = mom()
    groups = h.ref.shape[0]
    sums = [mom[j, 0:2, :] for j in range(groups)]
    for d in range(groups, mom.shape[0]):
        sums[d % groups] = sums[d % groups] + mom[d, 0:2, :]
    both = jnp.concatenate(sums, axis=1) * (1.0 / total_tokens)
    drive_body(0, both[0:1, :], both[1:2, :], start, h(), prm(), table(), weight, drive, norms, out, ends, slow)


def drive_next(layer, total_tokens, copies, begin, start, mom, prm, table, h, weight, drive, norms, out, ends, slow, maps):
    weight = Later(copies, [(weight.at[layer], maps)], maps)
    tile = total_of(mom()) * (1.0 / total_tokens)
    half = tile.shape[0] // 2
    mean, second = lanes(tile[:half]), lanes(tile[half:])
    drive_body(layer, mean, second, start, h(), prm(), table(), weight, drive, norms, out, ends, slow)


def resume(start, rows, gathered, mom, tab, ends, reverse, conj):
    fwd, bwd = local_resets(start, rows)
    reset = bwd if reverse else fwd
    first = carried_in(gathered, mom, tab, place()[1], reverse, conj)
    incoming, _ = chain_segments(
        [ends[k] for k in range(4)], first, tab, reset, rows // SUB, reverse, conj
    )
    return tuple(incoming), reset


def assemble(copies, begin, p0, p1, p2, p3, maps):
    begin()
    mp, _ = place()
    count, deep = maps.ref.shape[0], maps.ref.shape[1]
    for k, piece in enumerate((p0, p1, p2, p3)):
        cols = pl.ds(pl.multiple_of((mp ^ k) * LANES, LANES), LANES)
        for i in range(count):
            maps.ref[i, :, cols] = piece()[i * deep : (i + 1) * deep, :]


def gather_cotangent(copies, begin, got1, got2, got3, cot, full):
    begin()
    mp, _ = place()
    rows = full.ref.shape[0]
    own = cot()[pl.ds(pl.multiple_of(mp * rows, SUB), rows), :].astype(BF16)
    for k, block in enumerate((own, got1()[...], got2()[...], got3()[...])):
        full.ref[:, pl.ds(pl.multiple_of((mp ^ k) * LANES, LANES), LANES)] = block


def fetch_maps(copies, far, near, order=(0, 1, 2)):
    return {i: Later(copies, [(far.at[i], near.at[i])], near.at[i]) for i in order}


def mix_chunk(layer, at, h, norms, states, maps, prm):
    base = layer * PARAMS
    x = cat(h, at)
    scaled = x * norms[0:1, :] + norms[1:2, :]
    states_low = cat(states, at).astype(BF16)
    mixed = dot(states_low, maps[0]()[...]) + rowcat(prm, base + SKIP) * scaled
    square = mixed * mixed
    wave = jnp.tanh(ROOT * mixed * (1.0 + CUBE * square))
    half = 0.5 * (1.0 + wave)
    sent_low = (mixed * half).astype(BF16)
    slope = half + 0.5 * mixed * (1.0 - wave * wave) * (ROOT * (1.0 + 3.0 * CUBE * square))
    value = dot(sent_low, maps[1]()[...]) + rowcat(prm, base + VBIAS)
    gate = dot(sent_low, maps[2]()[...]) + rowcat(prm, base + GBIAS)
    sig = 0.5 + 0.5 * jnp.tanh(0.5 * gate)
    gated = value * sig
    return x, scaled, states_low, sent_low, slope, sig, gated


def back_chunk(i, at, g, sig, gain_part, scaled, slope, maps, outs, sums):
    dv, dg, dml, ds = outs
    dvalue = g * sig
    dgate = g * gain_part
    dv_low, dg_low = dvalue.astype(BF16), dgate.astype(BF16)
    dmixed = (dot_nt(dv_low, maps[1]()[...]) + dot_nt(dg_low, maps[2]()[...])) * slope()
    dm_low = dmixed.astype(BF16)
    put(ds.ref, at, dot_nt(dm_low, maps[0]()[...]))
    dv.ref[at, :] = dv_low
    dg.ref[at, :] = dg_low
    dml.ref[at, :] = dm_low
    for o in outs:
        o.flush(i, 2)
    add = lambda v: jnp.sum(v, axis=0, keepdims=True)
    return [
        s + n for s, n in zip(sums, [add(dvalue), add(dgate), add(dmixed * scaled())], strict=True)
    ]


def sums_rows(sums_out, sums):
    rows = sums + [jnp.zeros_like(sums[0])] * (8 - len(sums))
    sums_out.ref[...] = jnp.concatenate(rows, axis=0)
    sums_out.flush()


def share_out(keep, send, pack, copies):
    mp, _ = place()
    for ref, i, k in ((send, 0, 1), (send, 1, 3), (keep, 0, 0), (keep, 1, 2)):
        ref.ref[i, :, :] = pack[mp ^ k, :, :]


def weight_share(sent, dv, dg, states, dml, sums, pack):
    width = sent.dst.shape[1]
    parts = pack.shape[0]
    both = jnp.concatenate([dv()[...], dg()[...]], axis=1)
    both = dot_tn(sent()[...], both)
    put(pack, slice(0, width), both[:, :width])
    put(pack, slice(width, 2 * width), both[:, width:])
    put(pack, slice(2 * width, 3 * width), dot_tn(states()[...], dml()[...]))
    sums = sums()
    for j in range(parts):
        cols = slice(j * LANES, (j + 1) * LANES)
        rows = jnp.concatenate([sums[:, cols], jnp.zeros((8, LANES), F32)], axis=0)
        pack[j, 3 * width : 3 * width + 16, :] = rows.astype(pack.dtype)


def weight_grads(copies, begin, sent, dv, dg, states, dml, sums, keep, send, pack):
    begin()
    weight_share(sent, dv, dg, states, dml, sums, pack)
    share_out(keep, send, pack, copies)


def input_share(base, copies, slow, dlow, prods, weight, pack, held):
    width = slow.dst.shape[1]
    held[...] = dot_tn(slow()[...], dlow()[...])
    half = width // 2
    y_re = y_im = jnp.zeros((1, half), F32)
    size = 64
    for top in range(0, width, size):
        rows = slice(top, top + size)
        grad = held[rows, :]
        put(pack, slice(base + top, base + top + size), grad)
        grad_re, grad_im = grad[:, :half], grad[:, half:]
        w = weight()[rows, :].astype(F32)
        w_re, w_im = w[:, :half], w[:, half:]
        y_re = y_re + jnp.sum(grad_re * w_re + grad_im * w_im, axis=0, keepdims=True)
        y_im = y_im + jnp.sum(grad_im * w_re - grad_re * w_im, axis=0, keepdims=True)
    prods = prods()
    rows = []
    for h in range(2):
        cols = slice(h * LANES, (h + 1) * LANES)
        rows += [prods[2 * h : 2 * h + 1, :] - y_re[:, cols], prods[2 * h + 1 : 2 * h + 2, :] - y_im[:, cols]]
        rows += [y_re[:, cols]]
    tile = jnp.concatenate(rows + [jnp.zeros((10, LANES), F32)], axis=0).astype(pack.dtype)
    for j in range(pack.shape[0]):
        pack[j, base + width : base + width + 16, :] = tile


def input_grads(layer, copies, begin, slow, dlow, prods, weight, keep, send, pack, held, maps):
    begin()
    weight = Later(copies, [(weight.at[layer], maps)], maps)
    input_share(0, copies, slow, dlow, prods, weight, pack, held)
    share_out(keep, send, pack, copies)


def both_grads(layer, copies, begin, sent, dv, dg, states, dml, sums, slow, dlow, prods, weight, keep, send,
               pack, held, maps):
    begin()
    weight = Later(copies, [(weight.at[layer + 1], maps)], maps)
    weight_share(sent, dv, dg, states, dml, sums, pack)
    input_share(3 * sent.dst.shape[1] + 16, copies, slow, dlow, prods, weight, pack, held)
    share_out(keep, send, pack, copies)


def add_chunk(mom, one, two):
    tile = jnp.concatenate(
        [one[:, j * LANES : (j + 1) * LANES] for j in range(one.shape[1] // LANES)]
        + [two[:, j * LANES : (j + 1) * LANES] for j in range(two.shape[1] // LANES)],
        axis=0,
    )
    mom.ref[...] = jnp.broadcast_to(tile[None], mom.ref.shape)
    mom.flush()


def mix_first(layer, copies, begin, start, gathered, mom, table, ends, norms, prm, drive, h, far_maps,
              new_h, new_mom, h_far, states_low_out, sent, slope_out, sig_out, part_out, states, maps):
    rows = states.shape[1]
    ready = fetch_maps(copies, far_maps, maps)
    copies.flush(h.ref, h_far)
    reverse = layer % 2 == 1
    tab = table()[layer]
    init, reset = resume(start, rows, gathered(), mom(), tab, ends(), reverse, False)
    sweep(drive(), states, tab, init, reset, reverse, False)
    norms, prm = norms(), prm()
    one = two = 0.0
    for i, at in enumerate(chunks(rows, 2)):
        x, scaled, states_low, sent_low, slope, sig, gated = mix_chunk(
            layer, at, h(), norms, states, ready, prm
        )
        states_low_out.ref[at, :] = states_low
        sent.ref[at, :] = sent_low
        slope_out.ref[at, :] = slope.astype(BF16)
        sig_out.ref[at, :] = sig.astype(BF16)
        part_out.ref[at, :] = (gated * (1.0 - sig)).astype(BF16)
        new = x + gated
        put(new_h.ref, at, new)
        one = one + jnp.sum(new, axis=0, keepdims=True)
        two = two + jnp.sum(new * new, axis=0, keepdims=True)
        for o in (states_low_out, sent, slope_out, sig_out, part_out):
            o.flush(i, 2)
    add_chunk(new_mom, one, two)


def turn(layer, copies, begin, start, gathered, mom, table, ends, norms, prm, drive, h, far_maps, cot,
         ds, out, ends_out, h_far, states_low_out, sent, dv, dg, dml, sums_out, r0, r1, r2, r3,
         maps, states, new_h):
    mp, _ = place()
    rows = states.shape[1]
    ready = fetch_maps(copies, far_maps, maps)
    begin()
    copies.flush(h.ref, h_far)
    reverse = layer % 2 == 1
    tab = table()[layer]
    init, reset = resume(start, rows, gathered(), mom(), tab, ends(), reverse, False)
    sweep(drive(), states, tab, init, reset, reverse, False)
    norms, prm = norms(), prm()
    sums = [0.0, 0.0, 0.0]
    for i, at in enumerate(chunks(rows, 2)):
        x, scaled, states_low, sent_low, slope, sig, gated = mix_chunk(
            layer, at, h(), norms, states, ready, prm
        )
        states_low_out.ref[at, :] = states_low
        sent.ref[at, :] = sent_low
        put(new_h, at, x + gated)
        g = cot.part(i)[at, :].astype(F32)
        for o in (states_low_out, sent):
            o.flush(i, 2)
        sums = back_chunk(i, at, g, sig, gated * (1.0 - sig), lambda: scaled, lambda: slope,
                          ready, (dv, dg, dml, ds), sums)
    sums_rows(sums_out, sums)
    for k, r in enumerate((r0, r1, r2, r3)):
        r.ref[...] = new_h[mp ^ k, :, :].astype(r.ref.dtype)
        r.flush()
    adjoint_start(layer, start, tab, ds.ref, out, ends_out)


def adjoint_start(layer, start, tab, ds, out, ends_out):
    rows = ds.shape[1]
    reverse = layer % 2 == 0
    fwd, bwd = local_resets(start, rows)
    reset = bwd if reverse else fwd
    ends = sweep(ds, None, tab, zeros_state(2), reset, reverse, True)
    emit_ends(out, ends_out, ends, tab, reset, rows // SUB, reverse, True)


def back_first(layer, total_tokens, copies, begin, start, back, norms1, table, prm, u, norms,
               slow1, sig, part, slope, slow, far_maps, g_out, ds, out, ends_out, tile_out, dv, dg, dml, sums_out,
               maps):
    begin((slow1, 0), (sig, 0), (part, 0))
    ready = fetch_maps(copies, far_maps, maps, (1, 2))
    rows = ds.ref.shape[1]
    tile = total_of(back())
    tile_out.ref[...] = tile
    norms1, norms, prm = norms1(), norms(), prm()
    half = tile.shape[0] // 2
    base = (layer + 1) * PARAMS
    over = 1.0 / rowcat(prm, base + GAIN)
    shift = rowcat(prm, base + SHIFT)
    factor = norms1[0:1, :] * (1.0 / total_tokens)
    m_one, m_two = factor * lanes(tile[:half]), factor * over * lanes(tile[half:])
    m_one = m_one - shift * m_two
    sums = [0.0, 0.0, 0.0]
    for i, at in enumerate(chunks(rows, 2)):
        g = cat(u(), at) - m_one - slow1.part(i)[at, :].astype(F32) * m_two
        if i == 0:
            begin((slope, 0))
            ready.update(fetch_maps(copies, far_maps, maps, (0,)))
            begin((slow, 0), (slow1, 1), (sig, 1), (part, 1), (slope, 1), (slow, 1))
        put(g_out.ref, at, g)
        g_out.flush(i, 2)
        low = lambda x: x.part(i)[at, :].astype(F32)
        sums = back_chunk(i, at, g, low(sig), low(part), lambda: low(slow), lambda: low(slope),
                          ready, (dv, dg, dml, ds), sums)
    sums_rows(sums_out, sums)
    adjoint_start(layer, start, table()[layer], ds.ref, out, ends_out)


def back_second(layer, copies, begin, start, gathered, mom, table, ends, norms, prm, ds, states_low, g, dml, h,
                weight, *refs):
    if layer == 0:
        back, prods, dlow, u0, u1, u2, u3, adj, maps, u_ref = refs
    else:
        back, u_out, prods, dlow, adj, maps = refs
        u_ref = u_out.ref
        begin(g)
    begin(states_low)
    weight = Later(copies, [(weight.at[layer], maps)], maps)
    begin((dml, 0), (h, 0))
    if layer == 0:
        begin((g, 0), (g, 1))
    begin((dml, 1), (h, 1))
    rows = adj.shape[1]
    reverse = layer % 2 == 0
    tab = table()[layer]
    init, reset = resume(start, rows, gathered(), mom(), tab, ends(), reverse, True)
    sweep(ds(), adj, tab, init, reset, reverse, True)
    half = adj.shape[0] // 2 * LANES
    prod_re = prod_im = jnp.zeros((SUB, half), F32)
    for at in chunks(rows, 16):
        a, s = cat(adj, at), states_low()[at, :].astype(F32)
        a_re, a_im, s_re, s_im = a[:, :half], a[:, half:], s[:, :half], s[:, half:]
        re, im = a_re * s_re + a_im * s_im, a_im * s_re - a_re * s_im
        for top in range(0, re.shape[0], SUB):
            prod_re = prod_re + re[top : top + SUB, :]
            prod_im = prod_im + im[top : top + SUB, :]
    flat = [jnp.sum(x, axis=0, keepdims=True) for x in (prod_re, prod_im)]
    flat = [x[:, h_ * LANES : (h_ + 1) * LANES] for h_ in range(2) for x in flat]
    prods.ref[...] = jnp.concatenate(flat + [jnp.zeros((8 - len(flat), LANES), F32)], axis=0)
    prods.flush()
    gamma = lanes(tab[12:14, :])
    gamma = jnp.concatenate([gamma, gamma], axis=1)
    base = layer * PARAMS
    prm, norms = prm(), norms()
    skip = rowcat(prm, base + SKIP)
    factor, bias, inverse, mean = (norms[i : i + 1, :] for i in range(4))
    one = two = 0.0
    for i, at in enumerate(chunks(rows, 2)):
        low = (cat(adj, at) * gamma).astype(BF16)
        dlow.ref[at, :] = low
        dlow.flush(i, 2)
        dscaled = dot_nt(low, weight()[...]) + dml.part(i)[at, :].astype(F32) * skip
        normed = (cat(h.part(i), at) - mean) * inverse
        own = g()[at, :].astype(F32) if layer == 1 else cat(g.part(i), at)
        put(u_ref, at, own + factor * dscaled)
        one = one + jnp.sum(dscaled, axis=0, keepdims=True)
        two = two + jnp.sum(dscaled * normed, axis=0, keepdims=True)
    add_chunk(back, one, two)
    if layer == 0:
        mp, _ = place()
        for k, piece in enumerate((u0, u1, u2, u3)):
            piece.ref[...] = u_ref[mp ^ k, :, :].astype(piece.ref.dtype)
            piece.flush()


def result_kernel(copies, begin, r0, r1, r2, r3, result):
    begin()
    mp, _ = place()
    rows = r0.dst.shape[0]
    for k, r in ((1, r1), (2, r2), (3, r3), (0, r0)):
        at = pl.ds(pl.multiple_of((mp ^ k) * rows, SUB), rows)
        result.ref[at, :] = r()[...].astype(F32)
        copies.flush(result.ref.at[at], result.dst.at[at])
    result.sent = True


def last_kernel(total_tokens, copies, begin, norms, back, tile1, u0, u1, u2, u3, stream,
                out, gain_out, shift_out, held):
    begin()
    mp, _ = place()
    rows = u0.dst.shape[0]
    streams = [Later(copies, [(own_rows(stream, rows, k), held.at[k])], held.at[k]) for k in range(4)]
    tile, tile1, norms = total_of(back()), tile1(), norms()
    half = tile.shape[0] // 2
    zero = jnp.zeros((1, LANES), F32)
    one, two, factor, inverse, mean, later_one, later_two = [zero] * 7
    for j in range(half):
        mine = jnp.where(mp == j, 1.0, 0.0)
        cols = slice(j * LANES, (j + 1) * LANES)
        one = one + mine * tile[j : j + 1, :]
        two = two + mine * tile[half + j : half + j + 1, :]
        later_one = later_one + mine * tile1[j : j + 1, :]
        later_two = later_two + mine * tile1[half + j : half + j + 1, :]
        factor = factor + mine * norms[0:1, cols]
        inverse = inverse + mine * norms[2:3, cols]
        mean = mean + mine * norms[3:4, cols]
    scaled = factor * (1.0 / total_tokens)
    m_one, m_two = scaled * one, scaled * two
    for k, u in enumerate((u0, u1, u2, u3)):
        at = pl.ds(pl.multiple_of((mp ^ k) * rows, SUB), rows)
        normed = (streams[k]()[...] - mean) * inverse
        out.ref[at, :] = u()[...].astype(F32) - m_one - normed * m_two
        copies.flush(out.ref.at[at], out.dst.at[at])
    out.sent = True
    gain_out.ref[...] = jnp.concatenate([two, later_two], axis=0)
    shift_out.ref[...] = jnp.concatenate([one, later_one], axis=0)


def pair_sum(copies, begin, keep, got, mine, other):
    keep, got = keep(), got()
    size = keep.shape[1]
    for at in chunks(size, size // 16):
        other.ref[at, :] = (keep[1, at, :].astype(F32) + got[1, at, :].astype(F32)).astype(other.ref.dtype)
        mine.ref[at, :] = (keep[0, at, :].astype(F32) + got[0, at, :].astype(F32)).astype(mine.ref.dtype)


def four_sum(first, order, copies, begin, *refs):
    *ins, out = refs
    out = out.ref
    count, piece = out.shape[0], out.shape[1]
    tops = {True: 0, False: 0}

    def place_of(top, is_input):
        size = first if is_input else piece - first
        base = 0 if is_input else first
        return top // size, base + top % size

    for mine, got, spans in zip(ins[::2], ins[1::2], order, strict=True):
        mine, got = mine(), got()
        row = 0
        for rows, is_input in spans:
            for _ in range(rows // 16):
                d, top = place_of(tops[is_input], is_input)
                at = slice(row, row + 16)
                total = mine[at, :].astype(F32) + got[at, :].astype(F32)
                out[d, top : top + 16, :] = total.astype(out.dtype)
                tops[is_input] += 16
                row += 16
    for is_input in (True, False):
        size = first if is_input else piece - first
        while tops[is_input] < count * size:
            d, top = place_of(tops[is_input], is_input)
            out[d, top : top + 16, :] = jnp.zeros((16, out.shape[2]), out.dtype)
            tops[is_input] += 16


def piece_sum(copies, begin, pieces, first, rest):
    pieces = pieces()
    count, rows = pieces.shape[0], pieces.shape[1]
    split = first.ref.shape[1]
    for at in chunks(rows, rows // 16):
        total = pieces[0, at, :].astype(F32)
        for d in range(1, count):
            total = total + pieces[d, at, :].astype(F32)
        low = total.astype(first.ref.dtype)
        out, top = (first.ref, 0) if at.start < split else (rest.ref, split)
        for d in range(count):
            out[d, at.start - top : at.stop - top, :] = low


def hand_out(features, copies, begin, decay, phase, full_in, full,
             o_grad, skip_grad, v_grad, g_grad, vb, gb, d_grad, p_grad, s_grad):
    begin()
    in_rows, vgo_rows = features + 16, 3 * features + 16
    full, full_in = full(), full_in()
    decay, phase = decay(), phase()
    for layer in range(2):
        top = layer * vgo_rows
        for i, out in enumerate((v_grad, g_grad, o_grad)):
            out.ref[layer, :, :] = full[top + i * features : top + (i + 1) * features, :].astype(F32)
            copies.flush(out.ref.at[layer], out.dst.at[layer])
            out.sent = True
        top += 3 * features
        row = slice(layer, layer + 1)
        vecs = full[top : top + 16, :].astype(F32)
        vb.ref[row, :] = vecs[0:1, :]
        gb.ref[row, :] = vecs[1:2, :]
        skip_grad.ref[row, :] = vecs[2:3, :]
        top = layer * in_rows + features
        tile = full_in[top : top + 16, :].astype(F32)
        for h in range(2):
            cols = slice(h * LANES, (h + 1) * LANES)
            d_grad.ref[row, cols] = -jnp.exp(decay[row, cols]) * tile[3 * h : 3 * h + 1, :]
            p_grad.ref[row, cols] = jnp.exp(phase[row, cols]) * tile[3 * h + 1 : 3 * h + 2, :]
            s_grad.ref[row, cols] = tile[3 * h + 2 : 3 * h + 3, :]


def input_kernel(features, copies, begin, p0, p1, p2, p3, out):
    begin()
    mp, _ = place()
    for k, piece in enumerate((p0, p1, p2, p3)):
        cols = pl.ds(pl.multiple_of((mp ^ k) * LANES, LANES), LANES)
        piece = piece()
        for layer in range(out.ref.shape[0]):
            top = layer * (features + 16)
            out.ref[layer, :, cols] = piece[top : top + features, :].astype(F32)


def shape(dims, dtype=F32):
    return jax.ShapeDtypeStruct(tuple(dims), dtype)


def every(x):
    return lax.all_to_all(x, AXES, 0, 0)


def hop(x, k):
    count = lax.axis_size("mp")
    return lax.ppermute(x, "mp", [(i, i ^ k) for i in range(count)])


def spread(x, then=None):
    far = hop(x, 2)
    held = far if then is None else after(far, then)
    return hop(x, 1), far, hop(held, 1)


def swap(sends):
    return [hop(x, k + 1) for k, x in enumerate(sends)]


def after(x, *ys):
    return lax.optimization_barrier((x, *ys))[0]


def on_device(
    stream,
    cotangent,
    start_offsets,
    norm_gain,
    norm_shift,
    input_map,
    decay_log,
    phase_log,
    scale_log,
    output_map,
    skip_gain,
    value_weight,
    gate_weight,
    value_bias,
    gate_bias,
):
    block, width = stream.shape
    layers = input_map.shape[0]
    count_dp, parts = lax.axis_size("dp"), lax.axis_size("mp")
    devices = count_dp * parts
    tokens = block * count_dp
    rows = block // parts
    features = width * parts
    assert width == LANES and features == 4 * LANES and layers == 2 and parts == 4

    plist = (norm_gain, norm_shift, skip_gain, value_bias, gate_bias)
    blocks = shape((parts, rows, width))
    v_blocks = pltpu.VMEM(blocks.shape, F32)
    one_block = (rows, width)
    low_block = shape(one_block, BF16)
    wide_low = shape((rows, features), BF16)
    near_blocks = Near(blocks)
    near_ends = Near(shape((4, SUB, LANES)))
    near_every = Near(shape((devices, 4, LANES)))
    near_sums = Near(shape((devices, 2 * parts, LANES)))
    near_norms = Near(shape((8, features)))
    near_low = Near(low_block)
    packed_w = shape((3 * features, width), BF16)
    one_map = pltpu.VMEM((features, features), BF16)
    maps = pltpu.VMEM((3, features, features), BF16)
    all_maps = shape((3, features, features), BF16)

    mom_out, table, *sends = call(
        functools.partial(first_kernel, rows),
        [near_every, Near(shape((layers, 16, LANES)))] + [Near(shape((rows + 32, width), BF16))] * 3,
        [pltpu.VMEM((block, width), F32)],
        start_offsets, Raw(stream), *plist, decay_log, phase_log, scale_log,
        scalars=1,
    )
    table = Near(table)
    got_h = [Near(x) for x in swap(sends)]
    mom0 = Near(every(after(mom_out, *[g.array for g in got_h])))
    h0, prm = call(
        gather_block,
        [near_blocks, Near(shape((parts, 16, width)))],
        [pltpu.VMEM(one_block, F32)],
        *got_h, *plist, Raw(stream),
    )
    h0, prm = Near(h0), Near(prm)
    packs = call(
        functools.partial(pack_maps, layers), [packed_w] * layers, [], output_map, value_weight, gate_weight
    )
    w0 = after(packs[0], got_h[1].array, got_h[2].array)
    (full0,) = call(assemble, [all_maps], [], w0, *[Near(w) for w in spread(w0, mom0.array)])

    drive0, norms0, ends_all, ends0, slow0 = call(
        functools.partial(drive_first, tokens),
        [near_blocks, near_norms, near_every, near_ends, wide_low],
        [one_map],
        start_offsets, mom0, table, h0, prm, Raw(input_map),
        scalars=1,
    )
    got = Near(after(every(ends_all), full0))
    norms0 = Near(norms0)
    h1, mom_out, h0, states0, sent0, slope0, sig0, part0 = call(
        functools.partial(mix_first, 0),
        [near_blocks, near_sums, Raw(blocks)] + [wide_low] * 5,
        [v_blocks, maps],
        start_offsets, got, mom0, table, Near(ends0), norms0, prm, Near(drive0), h0, Raw(full0),
        scalars=1,
    )
    h1 = Near(h1)
    sends = call(pack_block, [low_block] * 3, [], after(cotangent, got.array))
    mom1 = Near(after(every(mom_out), *sends))
    w1 = after(packs[1], got.array)
    (full1,) = call(assemble, [all_maps], [], w1, *[Near(w) for w in spread(w1, mom1.array)])
    drive1, norms1, ends_all, ends1, slow1 = call(
        functools.partial(drive_next, 1, tokens),
        [near_blocks, near_norms, near_every, near_ends, wide_low],
        [one_map],
        start_offsets, mom1, prm, table, h1, Raw(input_map),
        scalars=1,
    )
    got_cot = [Near(x) for x in swap([after(s, norms1) for s in sends])]
    (cot,) = call(gather_cotangent, [wide_low], [], *got_cot, after(cotangent, full1))
    got = Near(after(every(ends_all), full1, cot))
    norms1 = Near(norms1)
    vgo_rows, in_rows = 3 * features + 16, features + 16

    def pair_share(keep, send):
        size = Near(shape(keep.shape[1:], BF16))
        return call(pair_sum, [size, size], [], Near(keep), Near(hop(send, 1)))

    vgo_half = Near(shape((2, vgo_rows, width), BF16))
    in_half = Near(shape((2, in_rows, width), BF16))
    vgo_pack = pltpu.VMEM((parts, vgo_rows, width), BF16)
    both_half = Near(shape((2, vgo_rows + in_rows, width), BF16))
    both_pack = pltpu.VMEM((parts, vgo_rows + in_rows, width), BF16)
    in_pack = pltpu.VMEM((parts, in_rows, width), BF16)
    in_room = [in_pack, pltpu.VMEM((features, features), F32), one_map]
    ds1, ends_all, back_ends1, h1, states1, sent1, dv, dg, dml1, sums, *res = call(
        functools.partial(turn, 1),
        [near_blocks, near_every, near_ends, Raw(blocks)] + [wide_low] * 5 + [near_norms.array, shape(one_block)]
        + [low_block] * 3,
        [maps, v_blocks, v_blocks],
        start_offsets, got, mom0, table, Near(ends1), norms1, prm, Near(drive1), h1, Raw(full1), Halves(cot),
        scalars=1,
    )
    got = Near(every(ends_all))
    keep1, send1 = call(
        weight_grads, [vgo_half, vgo_half], [vgo_pack], sent1, dv, dg, states1, dml1, sums
    )
    got = Near(after(got.array, keep1))
    send1 = after(send1, got.array)
    got = Near(after(got.array, keep1))
    back_out, u1, prods, dlow = call(
        functools.partial(back_second, 1),
        [near_sums, near_blocks, shape((8, LANES)), wide_low],
        [v_blocks, one_map],
        start_offsets, got, mom0, table, Near(back_ends1), norms1, prm, Near(ds1), states1, cot, Halves(dml1),
        Halves(h1), Raw(input_map),
        scalars=1,
    )
    back1 = Near(every(back_out))
    late1 = (slow1, dlow, prods)
    mine1, other1 = pair_share(after(keep1, back_out), send1)
    back1 = Near(after(back1.array, mine1))
    far1 = hop(other1, 2)
    g0, ds0, ends_all, back_ends0, tile1, dv, dg, dml0, sums = call(
        functools.partial(back_first, 0, tokens),
        [blocks, near_blocks, near_every, near_ends, Near(shape((2 * parts, LANES)))] + [wide_low] * 3
        + [near_norms.array],
        [maps],
        start_offsets, back1, norms1, table, prm, Near(u1), norms0,
        Halves(slow1), Halves(sig0), Halves(part0), Halves(slope0), Halves(slow0), Raw(full0),
        scalars=1,
    )
    got = Near(every(after(ends_all, far1)))
    keep0, send0 = call(
        functools.partial(both_grads, 0), [both_half, both_half], [both_pack] + in_room[1:],
        sent0, dv, dg, states0, dml0, sums, *late1, Raw(input_map),
    )
    send0 = after(send0, got.array)
    got = Near(after(got.array, keep0))
    back_out, prods, dlow, *us = call(
        functools.partial(back_second, 0),
        [near_sums, Near(shape((8, LANES))), Near(wide_low), Near(shape(one_block))] + [near_low] * 3,
        [v_blocks, one_map, v_blocks],
        start_offsets, got, mom0, table, Near(back_ends0), norms0, prm, Near(ds0), states0, Halves(g0), Halves(dml0),
        Halves(h0), Raw(input_map),
        scalars=1,
    )
    mine0, other0 = pair_share(keep0, send0)
    far0 = hop(other0, 2)
    prods = after(prods, mine0)
    in_keep0, in_send0 = call(
        functools.partial(input_grads, 0), [in_half, in_half], in_room, slow0, Near(dlow), Near(prods), Raw(input_map)
    )
    us = (us[0], *swap([after(u, in_send0) for u in us[1:]]))
    back0 = Near(every(after(back_out, in_send0, mine0)))
    in_mine0, in_other0 = pair_share(in_keep0, in_send0)
    in_far0 = hop(in_other0, 2)
    back0 = Near(after(back0.array, in_mine0))
    stream_grad, gain_grad, shift_grad = call(
        functools.partial(last_kernel, tokens),
        [shape((block, width)), shape((layers, width)), shape((layers, width))],
        [pltpu.VMEM((4,) + one_block, F32)],
        norms0, back0, Near(tile1), *[Near(u) for u in us], Raw(stream),
    )

    unit = 16 * count_dp
    in_piece = -(-2 * in_rows // unit) * 16
    piece = in_piece + -(-2 * vgo_rows // unit) * 16
    order = (((in_rows, True),), ((vgo_rows, False), (in_rows, True)), ((vgo_rows, False),))
    (own,) = call(
        functools.partial(four_sum, in_piece, order), [Near(shape((count_dp, piece, width), BF16))], [],
        Near(in_mine0), Near(in_far0), Near(mine0), Near(far0), Near(mine1), Near(far1),
    )
    pieces = lax.all_to_all(after(own, back0.array), "dp", 0, 0)
    first, rest = call(
        piece_sum,
        [Near(shape((count_dp, n, width), BF16)) for n in (in_piece, piece - in_piece)],
        [],
        Near(pieces),
    )
    result = [res[0], *swap([after(r, own) for r in res[1:]])]
    (result,) = call(result_kernel, [shape((block, width))], [], res[0], *[Near(r) for r in result[1:]])
    full_in = lax.all_to_all(after(first, stream_grad, result), "dp", 0, 0).reshape(-1, width)
    rest = after(rest, full_in)
    (input_grad,) = call(
        functools.partial(input_kernel, features), [shape((layers, features, features))], [],
        Near(full_in), *[Near(x) for x in spread(full_in)],
    )
    full = lax.all_to_all(rest, "dp", 0, 0).reshape(-1, width)
    full = after(full, input_grad)
    mat, vec, state = shape((layers, features, width)), shape((layers, width)), shape(decay_log.shape)
    o_grad, skip_grad, v_grad, g_grad, vb, gb, d_grad, p_grad, s_grad = call(
        functools.partial(hand_out, features),
        [mat, vec, mat, mat, vec, vec, state, state, state],
        [],
        decay_log, phase_log, Near(full_in), Near(full),
    )
    return (
        result, stream_grad, gain_grad, shift_grad, input_grad, d_grad, p_grad, s_grad,
        o_grad, skip_grad, v_grad, g_grad, vb, gb,
    )


def solution(mesh):
    split = P("dp", "mp")
    cols = P(None, "mp")
    wide = P(None, None, "mp")
    placed = (
        split, split, P("dp"), cols, cols, P(), P(), P(), P(), wide, cols, wide, wide, cols, cols,
    )
    return jax.shard_map(
        on_device,
        mesh=mesh,
        in_specs=placed,
        out_specs=(
            split, split, cols, cols, P(), P(), P(), P(), wide, cols, wide, wide, cols, cols,
        ),
        check_vma=False,
    )
```

```python
import functools

import jax
import jax.numpy as jnp
from jax import lax
from jax.experimental import pallas as pl
from jax.experimental.pallas import tpu as pltpu
from jax.sharding import PartitionSpec as P

epsilon = 1e-05
LANES = 128
SUB = 8
ROOT = 0.7978845608028654
CUBE = 0.044715
AXES = ("dp", "mp")
F32 = jnp.float32
BF16 = jnp.bfloat16
NT = (((1,), (1,)), ((), ()))
TN = (((0,), (0,)), ((), ()))
GAIN, SHIFT, SKIP, VBIAS, GBIAS = range(5)
PARAMS = 5


class Copies:
    def __init__(self, sems):
        self.sems, self.used, self.open = sems, 0, []

    def start(self, src, dst):
        copy = pltpu.make_async_copy(src, dst, self.sems.at[self.used])
        self.used += 1
        copy.start()
        return copy

    def flush(self, src, dst):
        self.open.append(self.start(src, dst))

    def finish(self):
        for copy in self.open:
            copy.wait()
        self.open = []


def along(ref, part, parts):
    if parts == 1:
        return ref
    axis = len(ref.shape) - 2
    size = ref.shape[axis] // parts
    at = pl.ds(part * size, size)
    return ref.at[at] if axis == 0 else ref.at[:, at]


class Arrival:
    def __init__(self, copies, src, dst, parts):
        self.copies, self.src, self.dst, self.parts = copies, src, dst, parts
        self.waits = [None] * parts

    def begin(self, part):
        src, dst = (along(r, part, self.parts) for r in (self.src, self.dst))
        self.waits[part] = self.copies.start(src, dst)

    def part(self, part):
        if self.waits[part] is not None:
            self.waits[part].wait()
            self.waits[part] = None
        return self.dst

    def __call__(self):
        for part in range(self.parts):
            self.part(part)
        return self.dst


class Result:
    def __init__(self, copies, ref, dst):
        self.copies, self.ref, self.dst, self.sent = copies, ref, dst, False

    def flush(self, part=0, parts=1):
        self.sent = True
        self.copies.flush(along(self.ref, part, parts), along(self.dst, part, parts))


class Raw:
    def __init__(self, array):
        self.array = array


class Halves:
    def __init__(self, array):
        self.array = array


class Near:
    def __init__(self, array):
        self.array = array


class Here:
    def __init__(self, ref):
        self.ref = self.dst = ref

    def part(self, part):
        return self.ref

    def __call__(self):
        return self.ref

    def flush(self, part=0, parts=1):
        pass


def call(body, outs, scratch, *args, scalars=0):
    wraps = (Raw, Halves, Near)
    plain = [a.array if isinstance(a, wraps) else a for a in args]
    out_shapes = [o.array if isinstance(o, wraps) else o for o in outs]
    autos = [i for i, a in enumerate(args) if i >= scalars and not isinstance(a, (Raw, Near))]
    made = [i for i, o in enumerate(outs) if not isinstance(o, (Raw, Near))]
    rooms = [pltpu.VMEM(plain[i].shape, plain[i].dtype) for i in autos]
    rooms += [pltpu.VMEM(out_shapes[i].shape, out_shapes[i].dtype) for i in made]

    def kernel(*refs):
        ins, refs = refs[: len(args)], refs[len(args) :]
        dsts, refs = refs[: len(outs)], refs[len(outs) :]
        sems, refs = refs[0], refs[1:]
        vin, refs = refs[: len(autos)], refs[len(autos) :]
        vout, rest = refs[: len(made)], refs[len(made) :]
        copies = Copies(sems)
        operands = [Here(r) if isinstance(a, Near) else r for a, r in zip(args, ins, strict=True)]
        for i, room in zip(autos, vin, strict=True):
            parts = 2 if isinstance(args[i], Halves) else 1
            operands[i] = Arrival(copies, ins[i], room, parts)
        results = [Here(r) if isinstance(o, Near) else r for o, r in zip(outs, dsts, strict=True)]
        for i, room in zip(made, vout, strict=True):
            results[i] = Result(copies, room, dsts[i])

        def begin(*some):
            for one in some or [operands[i] for i in autos]:
                operand, parts = one if isinstance(one, tuple) else (one, None)
                for part in range(operand.parts) if parts is None else (parts,):
                    operand.begin(part)

        body(copies, begin, *operands, *results, *rest)
        for r in results:
            if isinstance(r, Result) and not r.sent:
                r.flush()
        copies.finish()
        used.append(copies.used)

    near = pl.BlockSpec(memory_space=pltpu.VMEM)
    far = pl.BlockSpec(memory_space=pltpu.HBM)
    plain[scalars:] = [
        a if isinstance(w, Near) else pltpu.with_memory_space_constraint(a, pltpu.HBM)
        for w, a in zip(args[scalars:], plain[scalars:], strict=True)
    ]
    used = []

    def made_call(count):
        return pl.pallas_call(
            kernel,
            out_shape=[
                s if isinstance(o, Near) else pltpu.HBM(s.shape, s.dtype)
                for o, s in zip(outs, out_shapes, strict=True)
            ],
            in_specs=[pl.BlockSpec(memory_space=pltpu.SMEM)] * scalars
            + [near if isinstance(a, Near) else far for a in args[scalars:]],
            out_specs=[near if isinstance(o, Near) else far for o in outs],
            scratch_shapes=[pltpu.SemaphoreType.DMA((count,))] + rooms + list(scratch),
            compiler_params=pltpu.CompilerParams(vmem_limit_bytes=32 * 1024 * 1024),
        )

    jax.eval_shape(made_call(128), *plain)
    return made_call(max(used[0], 1))(*plain)


def cat(ref, rows):
    return jnp.concatenate([ref[j, rows, :] for j in range(ref.shape[0])], axis=1)


def put(ref, rows, val):
    for j in range(ref.shape[0]):
        ref[j, rows, :] = val[:, j * LANES : (j + 1) * LANES].astype(ref.dtype)


def rowcat(ref, r):
    return jnp.concatenate([ref[j, r : r + 1, :] for j in range(ref.shape[0])], axis=1)


def lanes(rows):
    return jnp.concatenate([rows[j : j + 1, :] for j in range(rows.shape[0])], axis=1)


def dot(a, b):
    return jnp.dot(a, b, preferred_element_type=F32)


def dot_nt(a, b):
    return lax.dot_general(a, b, NT, preferred_element_type=F32)


def dot_tn(a, b):
    return lax.dot_general(a, b, TN, preferred_element_type=F32)


def chunks(rows, count):
    size = rows // count
    return [slice(i * size, (i + 1) * size) for i in range(count)]


def sweep(src, dst, table, init, reset, reverse, conj):
    halves = src.shape[0] // 2
    span = src.shape[1] // SUB
    rate_re = [jnp.broadcast_to(table[h : h + 1, :], (SUB, LANES)) for h in range(halves)]
    rate_im = [
        jnp.broadcast_to(table[halves + h : halves + h + 1, :], (SUB, LANES))
        for h in range(halves)
    ]
    if conj:
        rate_im = [-r for r in rate_im]
    base = lax.broadcasted_iota(jnp.int32, (SUB, LANES), 0) * span - reset

    def body(step, state):
        j = span - 1 - step if reverse else step
        drop = base == -j
        at = pl.ds(j, SUB, stride=span)
        new_re, new_im = [], []
        for h in range(halves):
            a = jnp.where(drop, 0.0, rate_re[h])
            b = jnp.where(drop, 0.0, rate_im[h])
            re, im = state[h], state[halves + h]
            new_re.append((src[h, at, :] + a * re) - b * im)
            new_im.append((src[halves + h, at, :] + a * im) + b * re)
        state = tuple(new_re + new_im)
        if dst is not None:
            for k in range(2 * halves):
                dst[k, at, :] = state[k]
        return state

    return lax.fori_loop(0, span, body, init, unroll=8)


def zeros_state(halves):
    return tuple(jnp.zeros((SUB, LANES), F32) for _ in range(2 * halves))


def chain_segments(ends, first, table, reset, span, reverse, conj):
    halves = len(ends) // 2
    power_re = [table[4 + h : 5 + h, :] for h in range(halves)]
    power_im = [table[6 + h : 7 + h, :] for h in range(halves)]
    if conj:
        power_im = [-r for r in power_im]
    state = list(first)
    incoming = [[None] * SUB for _ in ends]
    order = range(SUB - 1, -1, -1) if reverse else range(SUB)
    for k in order:
        inside = (reset >= k * span) & (reset < (k + 1) * span)
        keep = jnp.where(inside, 0.0, 1.0)
        new = [None] * len(ends)
        for h in range(halves):
            re, im = state[h], state[halves + h]
            incoming[h][k], incoming[halves + h][k] = re, im
            new[h] = keep * (power_re[h] * re - power_im[h] * im) + ends[h][k : k + 1, :]
            new[halves + h] = (
                keep * (power_re[h] * im + power_im[h] * re) + ends[halves + h][k : k + 1, :]
            )
        state = new
    return [jnp.concatenate(rows, axis=0) for rows in incoming], state


def zero_rows(halves):
    return [jnp.zeros((1, LANES), F32) for _ in range(2 * halves)]


def emit_ends(out, ends_out, ends, table, reset, span, reverse, conj):
    halves = len(ends) // 2
    _, last = chain_segments(ends, zero_rows(halves), table, reset, span, reverse, conj)
    tile = jnp.concatenate(last, axis=0)
    out.ref[...] = jnp.broadcast_to(tile[None], out.ref.shape)
    out.flush()
    for k in range(2 * halves):
        ends_out.ref[k, :, :] = ends[k]
    ends_out.flush()


def carried_in(gathered, moments, table, me, reverse, conj):
    count = gathered.shape[0]
    power_re = table[8:10, :]
    power_im = table[10:12, :]
    if conj:
        power_im = -power_im
    flag = 3 if reverse else 2

    def body(i, state):
        d = count - 1 - i if reverse else i
        re, im = state
        keep = moments[d, flag : flag + 1, :]
        tile = gathered[d]
        return (
            keep * (power_re * re - power_im * im) + tile[0:2, :],
            keep * (power_re * im + power_im * re) + tile[2:4, :],
        )

    zero = jnp.zeros((2, LANES), F32)
    re, im = lax.fori_loop(0, count - 1 - me if reverse else me, body, (zero, zero))
    return [re[0:1, :], re[1:2, :], im[0:1, :], im[1:2, :]]


def place():
    mp = lax.axis_index("mp")
    return mp, lax.axis_index("dp") * lax.axis_size("mp") + mp


def local_resets(start, rows):
    offset = start[0]
    shift = jnp.where(offset > 0, offset - lax.axis_index("mp") * rows, -(1 << 20))
    return shift, shift - 1


def first_kernel(rows, copies, begin, start, stream, gain, shift, skip, vbias, gbias, decay, phase, scale,
                 moments, table_out, send1, send2, send3, held):
    mp, _ = place()
    total, width = held.shape
    parts = total // rows
    arrive = [copies.start(along(stream, i, parts), along(held, i, parts)) for i in range(parts)]
    begin()
    size = 128
    one = two = jnp.zeros((SUB, LANES), F32)

    def body(i, carry):
        one, two = carry
        x = held[pl.ds(i * size, size), :]
        for g in range(0, size, SUB):
            piece = x[g : g + SUB, :]
            one = one + piece
            two = two + piece * piece
        return one, two

    for i in range(parts):
        arrive[i].wait()
        one, two = lax.fori_loop(i * rows // size, (i + 1) * rows // size, body, (one, two))
    fwd, bwd = local_resets(start, rows)
    keep_f = jnp.where((fwd >= 0) & (fwd < rows), 0.0, 1.0)
    keep_b = jnp.where((bwd >= 0) & (bwd < rows), 0.0, 1.0)
    tile = jnp.concatenate(
        [
            jnp.sum(one, axis=0, keepdims=True),
            jnp.sum(two, axis=0, keepdims=True),
            jnp.full((1, LANES), keep_f, F32),
            jnp.full((1, LANES), keep_b, F32),
        ],
        axis=0,
    )
    moments.ref[...] = jnp.broadcast_to(tile[None], moments.ref.shape)
    moments.flush()
    gain, shift, skip, vbias, gbias = (a() for a in (gain, shift, skip, vbias, gbias))
    decay, phase, scale = decay(), phase(), scale()
    layers = decay.shape[0]
    plist = jnp.concatenate(
        [a[l : l + 1, :] for l in range(layers) for a in (gain, shift, skip, vbias, gbias)]
        + [jnp.zeros((16 - PARAMS * layers, width), F32)],
        axis=0,
    )
    high = plist.astype(BF16)
    rest = (plist - high.astype(F32)).astype(BF16)
    for k, send in ((1, send1), (2, send2), (3, send3)):
        base = (mp ^ k) * rows
        send.ref[0:rows, :] = held[pl.ds(pl.multiple_of(base, SUB), rows), :].astype(BF16)
        send.ref[rows : rows + 16, :] = high
        send.ref[rows + 16 : rows + 32, :] = rest
        send.flush()
    span = rows // SUB
    table = table_out.ref
    for layer in range(layers):
        for h in range(2):
            cols = slice(h * LANES, (h + 1) * LANES)
            radius = jnp.exp(-jnp.exp(decay[layer : layer + 1, cols]))
            angle = jnp.exp(phase[layer : layer + 1, cols])
            re, im = radius * jnp.cos(angle), radius * jnp.sin(angle)
            table[layer, h : h + 1, :] = re
            table[layer, 2 + h : 3 + h, :] = im
            length = 1
            while length < rows:
                re, im = re * re - im * im, 2.0 * re * im
                length *= 2
                if length == span:
                    table[layer, 4 + h : 5 + h, :] = re
                    table[layer, 6 + h : 7 + h, :] = im
            table[layer, 8 + h : 9 + h, :] = re
            table[layer, 10 + h : 11 + h, :] = im
            table[layer, 12 + h : 13 + h, :] = jnp.exp(scale[layer : layer + 1, cols])
            table[layer, 14 + h : 15 + h, :] = jnp.zeros((1, LANES), F32)


def pack_maps(layers, copies, begin, c_own, v_own, g_own, weight, *packs):
    begin()
    *packs, near = packs
    copies.flush(weight.at[0], near.ref)
    for layer in range(layers):
        for i, own in enumerate((c_own, v_own, g_own)):
            deep = own().shape[1]
            packs[layer].ref[i * deep : (i + 1) * deep, :] = own()[layer]
        packs[layer].flush()


def pack_block(copies, begin, x, weight, near, *sends):
    mp, _ = place()
    rows = sends[0].ref.shape[0]
    begin()
    copies.flush(weight.at[1], near.ref)
    whole = x()
    for k, send in enumerate(sends):
        base = pl.multiple_of((mp ^ (k + 1)) * rows, SUB)
        send.ref[...] = whole[pl.ds(base, rows), :].astype(BF16)
        send.flush()


def gather_block(copies, begin, got1, got2, got3, gain, shift, skip, vbias, gbias, stream, h, prm, held):
    mp, _ = place()
    rows = h.ref.shape[1]
    own = Later(copies, [(own_rows(stream, rows), held)], held)
    begin()
    plist = [a() for a in (gain, shift, skip, vbias, gbias)]
    layers = plist[0].shape[0]
    for k, got in ((1, got1), (2, got2), (3, got3)):
        got = got()
        h.ref[mp ^ k, :, :] = got[0:rows, :].astype(F32)
        pair = got[rows : rows + 16, :].astype(F32) + got[rows + 16 : rows + 32, :].astype(F32)
        prm.ref[mp ^ k, :, :] = pair
    mine = [a[l : l + 1, :] for l in range(layers) for a in plist]
    prm.ref[mp, 0 : PARAMS * layers, :] = jnp.concatenate(mine, axis=0)
    prm.ref[mp, PARAMS * layers :, :] = jnp.zeros((16 - PARAMS * layers, LANES), F32)
    h.ref[mp, :, :] = own()[...]


def norm_rows(mean, second, gain, shift):
    inverse = lax.rsqrt(second - mean * mean + epsilon)
    factor = inverse * gain
    return inverse, factor, shift - mean * factor


def drive_body(layer, mean, second, start, h, prm, table, weight, drive, norms, out, ends_out, slow):
    rows = drive.ref.shape[1]
    reverse = layer % 2 == 1
    base = layer * PARAMS
    inverse, factor, bias = norm_rows(
        mean, second, rowcat(prm, base + GAIN), rowcat(prm, base + SHIFT)
    )
    norms.ref[...] = jnp.concatenate(
        [factor, bias, inverse, mean] + [jnp.zeros_like(mean)] * 4, axis=0
    )
    norms.flush()
    gamma = lanes(table[layer, 12:14, :])
    gamma = jnp.concatenate([gamma, gamma], axis=1)
    for i, at in enumerate(chunks(rows, 2)):
        low = (cat(h, at) * factor + bias).astype(BF16)
        slow.ref[at, :] = low
        slow.flush(i, 2)
        put(drive.ref, at, dot(low, weight()[...]) * gamma)
        drive.flush(i, 2)
    fwd, bwd = local_resets(start, rows)
    reset = bwd if reverse else fwd
    ends = sweep(drive.ref, None, table[layer], zeros_state(2), reset, reverse, False)
    emit_ends(out, ends_out, ends, table[layer], reset, rows // SUB, reverse, False)


class Later:
    def __init__(self, copies, pairs, dst):
        self.waits, self.dst = [copies.start(src, to) for src, to in pairs], dst

    def __call__(self):
        for copy in self.waits:
            copy.wait()
        self.waits = []
        return self.dst


def own_rows(ref, rows, k=0):
    mp, _ = place()
    return ref.at[pl.ds(pl.multiple_of((mp ^ k) * rows, SUB), rows)]


def total_of(gathered):
    tile = gathered[0]
    for d in range(1, gathered.shape[0]):
        tile = tile + gathered[d]
    return tile


def drive_first(total_tokens, copies, begin, start, mom, table, h, prm, weight, drive, norms, out, ends, slow):
    mom = mom()
    groups = h.ref.shape[0]
    sums = [mom[j, 0:2, :] for j in range(groups)]
    for d in range(groups, mom.shape[0]):
        sums[d % groups] = sums[d % groups] + mom[d, 0:2, :]
    both = jnp.concatenate(sums, axis=1) * (1.0 / total_tokens)
    drive_body(0, both[0:1, :], both[1:2, :], start, h(), prm(), table(), weight, drive, norms, out, ends, slow)


def drive_next(layer, total_tokens, copies, begin, start, mom, prm, table, h, weight, drive, norms, out, ends, slow):
    tile = total_of(mom()) * (1.0 / total_tokens)
    half = tile.shape[0] // 2
    mean, second = lanes(tile[:half]), lanes(tile[half:])
    drive_body(layer, mean, second, start, h(), prm(), table(), weight, drive, norms, out, ends, slow)


def resume(start, rows, gathered, mom, tab, ends, reverse, conj):
    fwd, bwd = local_resets(start, rows)
    reset = bwd if reverse else fwd
    first = carried_in(gathered, mom, tab, place()[1], reverse, conj)
    incoming, _ = chain_segments(
        [ends[k] for k in range(4)], first, tab, reset, rows // SUB, reverse, conj
    )
    return tuple(incoming), reset


def assemble(copies, begin, p0, p1, p2, p3, maps):
    begin()
    mp, _ = place()
    count, deep = maps.ref.shape[0], maps.ref.shape[1]
    for k, piece in enumerate((p0, p1, p2, p3)):
        cols = pl.ds(pl.multiple_of((mp ^ k) * LANES, LANES), LANES)
        for i in range(count):
            maps.ref[i, :, cols] = piece()[i * deep : (i + 1) * deep, :]


def gather_cotangent(copies, begin, got1, got2, got3, cot, full):
    begin()
    mp, _ = place()
    rows = full.ref.shape[0]
    own = cot()[pl.ds(pl.multiple_of(mp * rows, SUB), rows), :].astype(BF16)
    for k, block in enumerate((own, got1()[...], got2()[...], got3()[...])):
        full.ref[:, pl.ds(pl.multiple_of((mp ^ k) * LANES, LANES), LANES)] = block


def fetch_maps(copies, far, near, order=(0, 1, 2)):
    return {i: Later(copies, [(far.at[i], near.at[i])], near.at[i]) for i in order}


def mix_chunk(layer, at, h, norms, states, maps, prm):
    base = layer * PARAMS
    x = cat(h, at)
    scaled = x * norms[0:1, :] + norms[1:2, :]
    states_low = cat(states, at).astype(BF16)
    mixed = dot(states_low, maps[0]()[...]) + rowcat(prm, base + SKIP) * scaled
    square = mixed * mixed
    wave = jnp.tanh(ROOT * mixed * (1.0 + CUBE * square))
    half = 0.5 * (1.0 + wave)
    sent_low = (mixed * half).astype(BF16)
    slope = half + 0.5 * mixed * (1.0 - wave * wave) * (ROOT * (1.0 + 3.0 * CUBE * square))
    value = dot(sent_low, maps[1]()[...]) + rowcat(prm, base + VBIAS)
    gate = dot(sent_low, maps[2]()[...]) + rowcat(prm, base + GBIAS)
    sig = 0.5 + 0.5 * jnp.tanh(0.5 * gate)
    gated = value * sig
    return x, scaled, states_low, sent_low, slope, sig, gated


def back_chunk(i, at, g, sig, gain_part, scaled, slope, maps, outs, sums):
    dv, dg, dml, ds = outs
    dvalue = g * sig
    dgate = g * gain_part
    dv_low, dg_low = dvalue.astype(BF16), dgate.astype(BF16)
    dmixed = (dot_nt(dv_low, maps[1]()[...]) + dot_nt(dg_low, maps[2]()[...])) * slope()
    dm_low = dmixed.astype(BF16)
    put(ds.ref, at, dot_nt(dm_low, maps[0]()[...]))
    dv.ref[at, :] = dv_low
    dg.ref[at, :] = dg_low
    dml.ref[at, :] = dm_low
    for o in outs:
        o.flush(i, 2)
    add = lambda v: jnp.sum(v, axis=0, keepdims=True)
    return [
        s + n for s, n in zip(sums, [add(dvalue), add(dgate), add(dmixed * scaled())], strict=True)
    ]


def sums_rows(sums_out, sums):
    rows = sums + [jnp.zeros_like(sums[0])] * (8 - len(sums))
    sums_out.ref[...] = jnp.concatenate(rows, axis=0)
    sums_out.flush()


def share_out(keep, send, pack, copies):
    mp, _ = place()
    for ref, i, k in ((send, 0, 1), (send, 1, 3), (keep, 0, 0), (keep, 1, 2)):
        ref.ref[i, :, :] = pack[mp ^ k, :, :]


def weight_share(sent, dv, dg, states, dml, sums, pack):
    width = sent.dst.shape[1]
    parts = pack.shape[0]
    both = jnp.concatenate([dv()[...], dg()[...]], axis=1)
    both = dot_tn(sent()[...], both)
    put(pack, slice(0, width), both[:, :width])
    put(pack, slice(width, 2 * width), both[:, width:])
    put(pack, slice(2 * width, 3 * width), dot_tn(states()[...], dml()[...]))
    sums = sums()
    for j in range(parts):
        cols = slice(j * LANES, (j + 1) * LANES)
        rows = jnp.concatenate([sums[:, cols], jnp.zeros((8, LANES), F32)], axis=0)
        pack[j, 3 * width : 3 * width + 16, :] = rows.astype(pack.dtype)


def weight_grads(copies, begin, sent, dv, dg, states, dml, sums, keep, send, pack):
    begin()
    weight_share(sent, dv, dg, states, dml, sums, pack)
    share_out(keep, send, pack, copies)


def input_share(base, copies, slow, dlow, prods, weight, pack, held, sums=None):
    width = slow.dst.shape[1]
    held[...] = dot_tn(slow()[...], dlow()[...])
    half = width // 2
    y_re = y_im = jnp.zeros((1, half), F32)
    size = 64
    for top in range(0, width, size):
        rows = slice(top, top + size)
        grad = held[rows, :]
        put(pack, slice(base + top, base + top + size), grad)
        grad_re, grad_im = grad[:, :half], grad[:, half:]
        w = weight()[rows, :].astype(F32)
        w_re, w_im = w[:, :half], w[:, half:]
        y_re = y_re + jnp.sum(grad_re * w_re + grad_im * w_im, axis=0, keepdims=True)
        y_im = y_im + jnp.sum(grad_im * w_re - grad_re * w_im, axis=0, keepdims=True)
    prods = prods()
    rows = []
    for h in range(2):
        cols = slice(h * LANES, (h + 1) * LANES)
        rows += [prods[2 * h : 2 * h + 1, :] - y_re[:, cols], prods[2 * h + 1 : 2 * h + 2, :] - y_im[:, cols]]
        rows += [y_re[:, cols]]
    for j in range(pack.shape[0]):
        cols = slice(j * LANES, (j + 1) * LANES)
        more = [] if sums is None else [sums()[0:2, cols]]
        tile = rows + more + [jnp.zeros((10 - 2 * len(more), LANES), F32)]
        pack[j, base + width : base + width + 16, :] = jnp.concatenate(tile, axis=0).astype(pack.dtype)


def input_grads(layer, copies, begin, slow, dlow, prods, sums, weight, keep, send, pack, held, maps):
    begin()
    weight = Later(copies, [(weight.at[layer], maps)], maps)
    input_share(0, copies, slow, dlow, prods, weight, pack, held, sums)
    share_out(keep, send, pack, copies)


def both_grads(layer, copies, begin, sent, dv, dg, states, dml, sums, slow, dlow, prods, weight, keep, send,
               pack, held, maps):
    begin()
    weight = Later(copies, [(weight.at[layer + 1], maps)], maps)
    weight_share(sent, dv, dg, states, dml, sums, pack)
    input_share(3 * sent.dst.shape[1] + 16, copies, slow, dlow, prods, weight, pack, held)
    share_out(keep, send, pack, copies)


def add_chunk(mom, one, two):
    tile = jnp.concatenate(
        [one[:, j * LANES : (j + 1) * LANES] for j in range(one.shape[1] // LANES)]
        + [two[:, j * LANES : (j + 1) * LANES] for j in range(two.shape[1] // LANES)],
        axis=0,
    )
    mom.ref[...] = jnp.broadcast_to(tile[None], mom.ref.shape)
    mom.flush()


def mix_first(layer, copies, begin, start, gathered, mom, table, ends, norms, prm, drive, h, far_maps,
              new_h, new_mom, h_far, states_low_out, sent, slope_out, sig_out, part_out, states, maps):
    rows = states.shape[1]
    ready = fetch_maps(copies, far_maps, maps)
    copies.flush(h.ref, h_far)
    reverse = layer % 2 == 1
    tab = table()[layer]
    init, reset = resume(start, rows, gathered(), mom(), tab, ends(), reverse, False)
    sweep(drive(), states, tab, init, reset, reverse, False)
    norms, prm = norms(), prm()
    one = two = 0.0
    for i, at in enumerate(chunks(rows, 2)):
        x, scaled, states_low, sent_low, slope, sig, gated = mix_chunk(
            layer, at, h(), norms, states, ready, prm
        )
        states_low_out.ref[at, :] = states_low
        sent.ref[at, :] = sent_low
        slope_out.ref[at, :] = slope.astype(BF16)
        sig_out.ref[at, :] = sig.astype(BF16)
        part_out.ref[at, :] = (gated * (1.0 - sig)).astype(BF16)
        new = x + gated
        put(new_h.ref, at, new)
        one = one + jnp.sum(new, axis=0, keepdims=True)
        two = two + jnp.sum(new * new, axis=0, keepdims=True)
        for o in (states_low_out, sent, slope_out, sig_out, part_out):
            o.flush(i, 2)
    add_chunk(new_mom, one, two)


def turn(layer, copies, begin, start, gathered, mom, table, ends, norms, prm, drive, h, far_maps, cot,
         ds, out, ends_out, h_far, states_low_out, sent, dv, dg, dml, sums_out, r0, r1, r2, r3,
         maps, states, new_h):
    mp, _ = place()
    rows = states.shape[1]
    ready = fetch_maps(copies, far_maps, maps)
    begin()
    copies.flush(h.ref, h_far)
    reverse = layer % 2 == 1
    tab = table()[layer]
    init, reset = resume(start, rows, gathered(), mom(), tab, ends(), reverse, False)
    sweep(drive(), states, tab, init, reset, reverse, False)
    norms, prm = norms(), prm()
    sums = [0.0, 0.0, 0.0]
    for i, at in enumerate(chunks(rows, 2)):
        x, scaled, states_low, sent_low, slope, sig, gated = mix_chunk(
            layer, at, h(), norms, states, ready, prm
        )
        states_low_out.ref[at, :] = states_low
        sent.ref[at, :] = sent_low
        put(new_h, at, x + gated)
        g = cot.part(i)[at, :].astype(F32)
        for o in (states_low_out, sent):
            o.flush(i, 2)
        sums = back_chunk(i, at, g, sig, gated * (1.0 - sig), lambda: scaled, lambda: slope,
                          ready, (dv, dg, dml, ds), sums)
    sums_rows(sums_out, sums)
    for k, r in enumerate((r0, r1, r2, r3)):
        r.ref[...] = new_h[mp ^ k, :, :].astype(r.ref.dtype)
        r.flush()
    adjoint_start(layer, start, tab, ds.ref, out, ends_out)


def adjoint_start(layer, start, tab, ds, out, ends_out):
    rows = ds.shape[1]
    reverse = layer % 2 == 0
    fwd, bwd = local_resets(start, rows)
    reset = bwd if reverse else fwd
    ends = sweep(ds, None, tab, zeros_state(2), reset, reverse, True)
    emit_ends(out, ends_out, ends, tab, reset, rows // SUB, reverse, True)


def back_first(layer, total_tokens, copies, begin, start, back, norms1, table, prm, u, norms,
               slow1, sig, part, slope, slow, far_maps, g_out, ds, out, ends_out, tile_out, dv, dg, dml, sums_out,
               maps):
    begin((slow1, 0), (sig, 0), (part, 0))
    ready = fetch_maps(copies, far_maps, maps, (1, 2))
    rows = ds.ref.shape[1]
    tile = total_of(back())
    tile_out.ref[...] = tile
    norms1, norms, prm = norms1(), norms(), prm()
    half = tile.shape[0] // 2
    base = (layer + 1) * PARAMS
    over = 1.0 / rowcat(prm, base + GAIN)
    shift = rowcat(prm, base + SHIFT)
    factor = norms1[0:1, :] * (1.0 / total_tokens)
    m_one, m_two = factor * lanes(tile[:half]), factor * over * lanes(tile[half:])
    m_one = m_one - shift * m_two
    sums = [0.0, 0.0, 0.0]
    for i, at in enumerate(chunks(rows, 2)):
        g = cat(u(), at) - m_one - slow1.part(i)[at, :].astype(F32) * m_two
        if i == 0:
            begin((slope, 0))
            ready.update(fetch_maps(copies, far_maps, maps, (0,)))
            begin((slow, 0), (slow1, 1), (sig, 1), (part, 1), (slope, 1), (slow, 1))
        put(g_out.ref, at, g)
        g_out.flush(i, 2)
        low = lambda x: x.part(i)[at, :].astype(F32)
        sums = back_chunk(i, at, g, low(sig), low(part), lambda: low(slow), lambda: low(slope),
                          ready, (dv, dg, dml, ds), sums)
    sums_rows(sums_out, sums)
    adjoint_start(layer, start, table()[layer], ds.ref, out, ends_out)


def back_second(layer, copies, begin, start, gathered, mom, table, ends, norms, prm, ds, states_low, g, dml, h,
                weight, *refs):
    if layer == 0:
        back, prods, dlow, u0, u1, u2, u3, adj, maps, u_ref = refs
    else:
        back, u_out, prods, dlow, adj, maps = refs
        u_ref = u_out.ref
        begin(g)
    begin(states_low)
    weight = Later(copies, [(weight.at[layer], maps)], maps)
    begin((dml, 0), (h, 0))
    if layer == 0:
        begin((g, 0), (g, 1))
    begin((dml, 1), (h, 1))
    rows = adj.shape[1]
    reverse = layer % 2 == 0
    tab = table()[layer]
    init, reset = resume(start, rows, gathered(), mom(), tab, ends(), reverse, True)
    sweep(ds(), adj, tab, init, reset, reverse, True)
    half = adj.shape[0] // 2 * LANES
    prod_re = prod_im = jnp.zeros((SUB, half), F32)
    for at in chunks(rows, 16):
        a, s = cat(adj, at), states_low()[at, :].astype(F32)
        a_re, a_im, s_re, s_im = a[:, :half], a[:, half:], s[:, :half], s[:, half:]
        re, im = a_re * s_re + a_im * s_im, a_im * s_re - a_re * s_im
        for top in range(0, re.shape[0], SUB):
            prod_re = prod_re + re[top : top + SUB, :]
            prod_im = prod_im + im[top : top + SUB, :]
    flat = [jnp.sum(x, axis=0, keepdims=True) for x in (prod_re, prod_im)]
    flat = [x[:, h_ * LANES : (h_ + 1) * LANES] for h_ in range(2) for x in flat]
    prods.ref[...] = jnp.concatenate(flat + [jnp.zeros((8 - len(flat), LANES), F32)], axis=0)
    prods.flush()
    gamma = lanes(tab[12:14, :])
    gamma = jnp.concatenate([gamma, gamma], axis=1)
    base = layer * PARAMS
    prm, norms = prm(), norms()
    skip = rowcat(prm, base + SKIP)
    factor, bias, inverse, mean = (norms[i : i + 1, :] for i in range(4))
    one = two = 0.0
    for i, at in enumerate(chunks(rows, 2)):
        low = (cat(adj, at) * gamma).astype(BF16)
        dlow.ref[at, :] = low
        dlow.flush(i, 2)
        dscaled = dot_nt(low, weight()[...]) + dml.part(i)[at, :].astype(F32) * skip
        normed = (cat(h.part(i), at) - mean) * inverse
        own = g()[at, :].astype(F32) if layer == 1 else cat(g.part(i), at)
        put(u_ref, at, own + factor * dscaled)
        one = one + jnp.sum(dscaled, axis=0, keepdims=True)
        two = two + jnp.sum(dscaled * normed, axis=0, keepdims=True)
    if layer == 0:
        back.ref[...] = jnp.concatenate([one, two] + [jnp.zeros_like(one)] * 6, axis=0)
        mp, _ = place()
        for k, piece in enumerate((u0, u1, u2, u3)):
            piece.ref[...] = u_ref[mp ^ k, :, :].astype(piece.ref.dtype)
            piece.flush()
    else:
        add_chunk(back, one, two)


def result_kernel(copies, begin, r0, r1, r2, r3, result):
    begin()
    mp, _ = place()
    rows = r0.dst.shape[0]
    for k, r in ((1, r1), (2, r2), (3, r3), (0, r0)):
        at = pl.ds(pl.multiple_of((mp ^ k) * rows, SUB), rows)
        result.ref[at, :] = r()[...].astype(F32)
        copies.flush(result.ref.at[at], result.dst.at[at])
    result.sent = True


def last_kernel(total_tokens, in_piece, copies, begin, norms, back, tile1, u0, u1, u2, u3, stream,
                out, gain_out, shift_out, held):
    begin()
    mp, _ = place()
    rows = u0.dst.shape[0]
    streams = [Later(copies, [(own_rows(stream, rows, k), held.at[k])], held.at[k]) for k in range(4)]
    tile1, norms = tile1(), norms()
    width = norms.shape[1]
    ((_, _, sums),) = unpieced(back(), 0, in_piece, width, 16)
    sums = sums.astype(F32)
    one, two = sums[6:7, :], sums[7:8, :]
    half = tile1.shape[0] // 2
    zero = jnp.zeros((1, LANES), F32)
    factor, inverse, mean, later_one, later_two = [zero] * 5
    for j in range(half):
        mine = jnp.where(mp == j, 1.0, 0.0)
        cols = slice(j * LANES, (j + 1) * LANES)
        later_one = later_one + mine * tile1[j : j + 1, :]
        later_two = later_two + mine * tile1[half + j : half + j + 1, :]
        factor = factor + mine * norms[0:1, cols]
        inverse = inverse + mine * norms[2:3, cols]
        mean = mean + mine * norms[3:4, cols]
    scaled = factor * (1.0 / total_tokens)
    m_one, m_two = scaled * one, scaled * two
    for k, u in enumerate((u0, u1, u2, u3)):
        at = pl.ds(pl.multiple_of((mp ^ k) * rows, SUB), rows)
        normed = (streams[k]()[...] - mean) * inverse
        out.ref[at, :] = u()[...].astype(F32) - m_one - normed * m_two
        copies.flush(out.ref.at[at], out.dst.at[at])
    out.sent = True
    gain_out.ref[...] = jnp.concatenate([two, later_two], axis=0)
    shift_out.ref[...] = jnp.concatenate([one, later_one], axis=0)


def pair_sum(copies, begin, keep, got, mine, other):
    keep, got = keep(), got()
    size = keep.shape[1]
    for at in chunks(size, size // 16):
        other.ref[at, :] = (keep[1, at, :].astype(F32) + got[1, at, :].astype(F32)).astype(other.ref.dtype)
        mine.ref[at, :] = (keep[0, at, :].astype(F32) + got[0, at, :].astype(F32)).astype(mine.ref.dtype)


def four_sum(order, copies, begin, *refs):
    *ins, out = refs
    out = out.ref
    for mine, got, spans in zip(ins[::2], ins[1::2], order, strict=True):
        mine, got = mine(), got()
        row = 0
        for rows, size, base in spans:
            for i in range(0, out.shape[0] * size, 16):
                d, top = i // size, base + i % size
                if i < rows:
                    at = slice(row + i, row + i + 16)
                    total = (mine[at, :].astype(F32) + got[at, :].astype(F32)).astype(out.dtype)
                else:
                    total = jnp.zeros((16, out.shape[2]), out.dtype)
                out[d, top : top + 16, :] = total
            row += rows


def piece_total(pieces, at):
    total = pieces[0, at, :].astype(F32)
    for d in range(1, pieces.shape[0]):
        total = total + pieces[d, at, :].astype(F32)
    return total.astype(BF16)


def piece_sum(copies, begin, pieces, out):
    for at in chunks(out.ref.shape[0], out.ref.shape[0] // 16):
        out.ref[at, :] = piece_total(pieces(), at)


def piece_sums(sizes, copies, begin, pieces, other, first, rest):
    in_piece, vgo_piece = sizes
    rows = pieces().shape[1]
    for at in chunks(rows, rows // 16):
        low = piece_total(pieces(), at)
        inputs = at.start < 2 * in_piece
        out, top = (first.ref, at.start) if inputs else (rest.ref, at.start - 2 * in_piece)
        for d in range(out.shape[0]):
            out[d, top : top + 16, :] = low
    for at in chunks(vgo_piece, vgo_piece // 16):
        low = other()[at, :]
        for d in range(rest.ref.shape[0]):
            rest.ref[d, vgo_piece + at.start : vgo_piece + at.stop, :] = low


def unpieced(pieces, offset, size, first, rows):
    at = first
    while at < first + rows:
        piece, inside = at // size, at % size
        count = min(size - inside, first + rows - at)
        yield at - first, count, pieces[piece, offset + inside : offset + inside + count, :]
        at += count


def hand_out(features, sizes, copies, begin, decay, phase, full_in, full,
             o_grad, skip_grad, v_grad, g_grad, vb, gb, d_grad, p_grad, s_grad):
    begin()
    full, full_in = full(), full_in()
    decay, phase = decay(), phase()
    in_piece, vgo_piece = sizes
    for layer in range(2):
        base = layer * vgo_piece
        for i, out in enumerate((v_grad, g_grad, o_grad)):
            for at, count, rows in unpieced(full, base, vgo_piece, i * features, features):
                out.ref[layer, at : at + count, :] = rows.astype(F32)
            copies.flush(out.ref.at[layer], out.dst.at[layer])
            out.sent = True
        row = slice(layer, layer + 1)
        ((_, _, vecs),) = unpieced(full, base, vgo_piece, 3 * features, 16)
        vecs = vecs.astype(F32)
        vb.ref[row, :] = vecs[0:1, :]
        gb.ref[row, :] = vecs[1:2, :]
        skip_grad.ref[row, :] = vecs[2:3, :]
        ((_, _, tile),) = unpieced(full_in, layer * in_piece, in_piece, features, 16)
        tile = tile.astype(F32)
        for h in range(2):
            cols = slice(h * LANES, (h + 1) * LANES)
            d_grad.ref[row, cols] = -jnp.exp(decay[row, cols]) * tile[3 * h : 3 * h + 1, :]
            p_grad.ref[row, cols] = jnp.exp(phase[row, cols]) * tile[3 * h + 1 : 3 * h + 2, :]
            s_grad.ref[row, cols] = tile[3 * h + 2 : 3 * h + 3, :]


def input_kernel(features, size, copies, begin, p0, p1, p2, p3, out):
    begin()
    mp, _ = place()
    for k, pieces in enumerate((p0, p1, p2, p3)):
        cols = pl.ds(pl.multiple_of((mp ^ k) * LANES, LANES), LANES)
        for layer in range(out.ref.shape[0]):
            for at, count, rows in unpieced(pieces(), layer * size, size, 0, features):
                out.ref[layer, at : at + count, cols] = rows.astype(F32)


def shape(dims, dtype=F32):
    return jax.ShapeDtypeStruct(tuple(dims), dtype)


def every(x):
    return lax.all_to_all(x, AXES, 0, 0)


def hop(x, k):
    count = lax.axis_size("mp")
    return lax.ppermute(x, "mp", [(i, i ^ k) for i in range(count)])


def spread(x, then=None):
    far = hop(x, 2)
    held = far if then is None else after(far, then)
    return hop(x, 1), far, hop(held, 1)


def swap(sends):
    return [hop(x, k + 1) for k, x in enumerate(sends)]


def after(x, *ys):
    return lax.optimization_barrier((x, *ys))[0]


def on_device(
    stream,
    cotangent,
    start_offsets,
    norm_gain,
    norm_shift,
    input_map,
    decay_log,
    phase_log,
    scale_log,
    output_map,
    skip_gain,
    value_weight,
    gate_weight,
    value_bias,
    gate_bias,
):
    block, width = stream.shape
    layers = input_map.shape[0]
    count_dp, parts = lax.axis_size("dp"), lax.axis_size("mp")
    devices = count_dp * parts
    tokens = block * count_dp
    rows = block // parts
    features = width * parts
    assert width == LANES and features == 4 * LANES and layers == 2 and parts == 4

    plist = (norm_gain, norm_shift, skip_gain, value_bias, gate_bias)
    blocks = shape((parts, rows, width))
    v_blocks = pltpu.VMEM(blocks.shape, F32)
    one_block = (rows, width)
    low_block = shape(one_block, BF16)
    wide_low = shape((rows, features), BF16)
    near_blocks = Near(blocks)
    near_ends = Near(shape((4, SUB, LANES)))
    near_every = Near(shape((devices, 4, LANES)))
    near_sums = Near(shape((devices, 2 * parts, LANES)))
    near_norms = Near(shape((8, features)))
    near_low = Near(low_block)
    packed_w = shape((3 * features, width), BF16)
    one_map = pltpu.VMEM((features, features), BF16)
    maps = pltpu.VMEM((3, features, features), BF16)
    all_maps = shape((3, features, features), BF16)
    near_map = Near(shape((features, features), BF16))

    mom_out, table, *sends = call(
        functools.partial(first_kernel, rows),
        [near_every, Near(shape((layers, 16, LANES)))] + [Near(shape((rows + 32, width), BF16))] * 3,
        [pltpu.VMEM((block, width), F32)],
        start_offsets, Raw(stream), *plist, decay_log, phase_log, scale_log,
        scalars=1,
    )
    table = Near(table)
    got_h = [Near(x) for x in swap(sends)]
    mom0 = every(after(mom_out, *[g.array for g in got_h]))
    h0, prm = call(
        gather_block,
        [near_blocks, Near(shape((parts, 16, width)))],
        [pltpu.VMEM(one_block, F32)],
        *got_h, *plist, Raw(stream),
    )
    h0, prm, mom0 = Near(h0), Near(prm), Near(after(mom0, h0))
    *packs, near_in = call(
        functools.partial(pack_maps, layers), [packed_w] * layers + [near_map], [],
        output_map, value_weight, gate_weight, Raw(input_map),
    )
    w0 = after(packs[0], got_h[1].array, got_h[2].array)
    (full0,) = call(assemble, [all_maps], [], w0, *[Near(w) for w in spread(w0, mom0.array)])

    drive0, norms0, ends_all, ends0, slow0 = call(
        functools.partial(drive_first, tokens),
        [near_blocks, near_norms, near_every, near_ends, wide_low],
        [],
        start_offsets, mom0, table, h0, prm, Near(near_in),
        scalars=1,
    )
    got = Near(after(every(ends_all), full0))
    norms0 = Near(norms0)
    h1, mom_out, h0, states0, sent0, slope0, sig0, part0 = call(
        functools.partial(mix_first, 0),
        [near_blocks, near_sums, Raw(blocks)] + [wide_low] * 5,
        [v_blocks, maps],
        start_offsets, got, mom0, table, Near(ends0), norms0, prm, Near(drive0), h0, Raw(full0),
        scalars=1,
    )
    h1 = Near(h1)
    near_in, *sends = call(
        pack_block, [near_map] + [low_block] * 3, [], after(cotangent, got.array), Raw(input_map)
    )
    mom1 = Near(after(every(mom_out), *sends))
    w1 = after(packs[1], got.array)
    (full1,) = call(assemble, [all_maps], [], w1, *[Near(w) for w in spread(w1, mom1.array)])
    drive1, norms1, ends_all, ends1, slow1 = call(
        functools.partial(drive_next, 1, tokens),
        [near_blocks, near_norms, near_every, near_ends, wide_low],
        [],
        start_offsets, mom1, prm, table, h1, Near(near_in),
        scalars=1,
    )
    got_cot = [Near(x) for x in swap([after(s, norms1) for s in sends])]
    (cot,) = call(gather_cotangent, [wide_low], [], *got_cot, after(cotangent, full1))
    got = Near(after(every(ends_all), full1, cot))
    norms1 = Near(norms1)
    vgo_rows, in_rows = 3 * features + 16, features + 16

    def pair_share(keep, send):
        size = Near(shape(keep.shape[1:], BF16))
        return call(pair_sum, [size, size], [], Near(keep), Near(hop(send, 1)))

    vgo_half = Near(shape((2, vgo_rows, width), BF16))
    in_half = Near(shape((2, in_rows, width), BF16))
    vgo_pack = pltpu.VMEM((parts, vgo_rows, width), BF16)
    both_half = Near(shape((2, vgo_rows + in_rows, width), BF16))
    both_pack = pltpu.VMEM((parts, vgo_rows + in_rows, width), BF16)
    in_pack = pltpu.VMEM((parts, in_rows, width), BF16)
    in_room = [in_pack, pltpu.VMEM((features, features), F32), one_map]
    ds1, ends_all, back_ends1, h1, states1, sent1, dv, dg, dml1, sums, *res = call(
        functools.partial(turn, 1),
        [near_blocks, near_every, near_ends, Raw(blocks)] + [wide_low] * 5 + [near_norms.array, shape(one_block)]
        + [low_block] * 3,
        [maps, v_blocks, v_blocks],
        start_offsets, got, mom0, table, Near(ends1), norms1, prm, Near(drive1), h1, Raw(full1), Halves(cot),
        scalars=1,
    )
    got = Near(every(ends_all))
    keep1, send1 = call(
        weight_grads, [vgo_half, vgo_half], [vgo_pack], sent1, dv, dg, states1, dml1, sums
    )
    got = Near(after(got.array, keep1))
    send1 = after(send1, got.array)
    got = Near(after(got.array, keep1))
    back_out, u1, prods, dlow = call(
        functools.partial(back_second, 1),
        [near_sums, near_blocks, shape((8, LANES)), wide_low],
        [v_blocks, one_map],
        start_offsets, got, mom0, table, Near(back_ends1), norms1, prm, Near(ds1), states1, cot, Halves(dml1),
        Halves(h1), Raw(input_map),
        scalars=1,
    )
    back1 = Near(every(back_out))
    late1 = (slow1, dlow, prods)
    mine1, other1 = pair_share(after(keep1, back_out), send1)
    back1 = Near(after(back1.array, mine1))
    far1 = hop(other1, 2)
    g0, ds0, ends_all, back_ends0, tile1, dv, dg, dml0, sums = call(
        functools.partial(back_first, 0, tokens),
        [blocks, near_blocks, near_every, near_ends, Near(shape((2 * parts, LANES)))] + [wide_low] * 3
        + [near_norms.array],
        [maps],
        start_offsets, back1, norms1, table, prm, Near(u1), norms0,
        Halves(slow1), Halves(sig0), Halves(part0), Halves(slope0), Halves(slow0), Raw(full0),
        scalars=1,
    )
    unit = 16 * count_dp
    in_piece, vgo_piece = (-(-n // unit) * 16 for n in (in_rows, vgo_rows))

    def joined(order, *operands):
        piece = max(base + size for spans in order for _, size, base in spans)
        out = Near(shape((count_dp, piece, width), BF16))
        return call(functools.partial(four_sum, order), [out], [], *map(Near, operands))[0]

    own1 = joined((((vgo_rows, vgo_piece, 0),),), mine1, far1)
    got = Near(every(after(ends_all, far1)))
    keep0, send0 = call(
        functools.partial(both_grads, 0), [both_half, both_half], [both_pack] + in_room[1:],
        sent0, dv, dg, states0, dml0, sums, *late1, Raw(input_map),
    )
    pieces = lax.all_to_all(after(own1, got.array), "dp", 0, 0)
    (summed1,) = call(piece_sum, [Near(shape((vgo_piece, width), BF16))], [], Near(pieces))
    send0 = after(send0, got.array)
    got = Near(after(got.array, keep0))
    back_out, prods, dlow, *us = call(
        functools.partial(back_second, 0),
        [near_norms, Near(shape((8, LANES))), Near(wide_low), Near(shape(one_block))] + [near_low] * 3,
        [v_blocks, one_map, v_blocks],
        start_offsets, got, mom0, table, Near(back_ends0), norms0, prm, Near(ds0), states0, Halves(g0), Halves(dml0),
        Halves(h0), Raw(input_map),
        scalars=1,
    )
    mine0, other0 = pair_share(keep0, send0)
    far0 = hop(other0, 2)
    prods = after(prods, mine0)
    in_keep0, in_send0 = call(
        functools.partial(input_grads, 0), [in_half, in_half], in_room, slow0, Near(dlow), Near(prods), Near(back_out), Raw(input_map)
    )
    us = (us[0], *swap([after(u, in_send0) for u in us[1:]]))
    in_mine0, in_other0 = pair_share(in_keep0, in_send0)
    in_far0 = hop(in_other0, 2)

    order = (
        ((in_rows, in_piece, 0),),
        ((vgo_rows, vgo_piece, 2 * in_piece), (in_rows, in_piece, in_piece)),
    )
    own0 = joined(order, in_mine0, in_far0, mine0, far0)
    pieces = lax.all_to_all(after(own0, summed1), "dp", 0, 0)
    first, rest = call(
        functools.partial(piece_sums, (in_piece, vgo_piece)),
        [Near(shape((count_dp, 2 * n, width), BF16)) for n in (in_piece, vgo_piece)],
        [],
        Near(pieces), Near(summed1),
    )
    result = [res[0], *swap([after(r, own0) for r in res[1:]])]
    (result,) = call(result_kernel, [shape((block, width))], [], res[0], *[Near(r) for r in result[1:]])
    full_in = lax.all_to_all(after(first, result, *us[1:]), "dp", 0, 0)
    stream_grad, gain_grad, shift_grad = call(
        functools.partial(last_kernel, tokens, in_piece),
        [shape((block, width)), shape((layers, width)), shape((layers, width))],
        [pltpu.VMEM((4,) + one_block, F32)],
        norms0, Near(full_in), Near(tile1), *[Near(u) for u in us], Raw(stream),
    )
    rest = after(rest, full_in)
    (input_grad,) = call(
        functools.partial(input_kernel, features, in_piece), [shape((layers, features, features))], [],
        Near(full_in), *[Near(x) for x in spread(full_in)],
    )
    full = lax.all_to_all(rest, "dp", 0, 0)
    full = after(full, input_grad, stream_grad)
    mat, vec, state = shape((layers, features, width)), shape((layers, width)), shape(decay_log.shape)
    o_grad, skip_grad, v_grad, g_grad, vb, gb, d_grad, p_grad, s_grad = call(
        functools.partial(hand_out, features, (in_piece, vgo_piece)),
        [mat, vec, mat, mat, vec, vec, state, state, state],
        [],
        decay_log, phase_log, Near(full_in), Near(full),
    )
    return (
        result, stream_grad, gain_grad, shift_grad, input_grad, d_grad, p_grad, s_grad,
        o_grad, skip_grad, v_grad, g_grad, vb, gb,
    )


def solution(mesh):
    split = P("dp", "mp")
    cols = P(None, "mp")
    wide = P(None, None, "mp")
    placed = (
        split, split, P("dp"), cols, cols, P(), P(), P(), P(), wide, cols, wide, wide, cols, cols,
    )
    return jax.shard_map(
        on_device,
        mesh=mesh,
        in_specs=placed,
        out_specs=(
            split, split, cols, cols, P(), P(), P(), P(), wide, cols, wide, wide, cols, cols,
        ),
        check_vma=False,
    )
```

```python
import functools

import jax
import jax.numpy as jnp
from jax import lax
from jax.experimental import pallas as pl
from jax.experimental.pallas import tpu as pltpu
from jax.sharding import PartitionSpec as P

epsilon = 1e-05
LANES = 128
SUB = 8
ROOT = 0.7978845608028654
CUBE = 0.044715
AXES = ("dp", "mp")
F32 = jnp.float32
BF16 = jnp.bfloat16
NT = (((1,), (1,)), ((), ()))
TN = (((0,), (0,)), ((), ()))
GAIN, SHIFT, SKIP, VBIAS, GBIAS = range(5)
PARAMS = 5


class Copies:
    def __init__(self, sems):
        self.sems, self.used, self.open = sems, 0, []

    def start(self, src, dst):
        copy = pltpu.make_async_copy(src, dst, self.sems.at[self.used])
        self.used += 1
        copy.start()
        return copy

    def flush(self, src, dst):
        self.open.append(self.start(src, dst))

    def finish(self):
        for copy in self.open:
            copy.wait()
        self.open = []


def along(ref, part, parts):
    if parts == 1:
        return ref
    axis = len(ref.shape) - 2
    size = ref.shape[axis] // parts
    at = pl.ds(part * size, size)
    return ref.at[at] if axis == 0 else ref.at[:, at]


class Arrival:
    def __init__(self, copies, src, dst, parts):
        self.copies, self.src, self.dst, self.parts = copies, src, dst, parts
        self.waits = [None] * parts

    def begin(self, part):
        src, dst = (along(r, part, self.parts) for r in (self.src, self.dst))
        self.waits[part] = self.copies.start(src, dst)

    def part(self, part):
        if self.waits[part] is not None:
            self.waits[part].wait()
            self.waits[part] = None
        return self.dst

    def __call__(self):
        for part in range(self.parts):
            self.part(part)
        return self.dst


class Result:
    def __init__(self, copies, ref, dst):
        self.copies, self.ref, self.dst, self.sent = copies, ref, dst, False

    def flush(self, part=0, parts=1):
        self.sent = True
        self.copies.flush(along(self.ref, part, parts), along(self.dst, part, parts))


class Raw:
    def __init__(self, array):
        self.array = array


class Halves:
    def __init__(self, array):
        self.array = array


class Near:
    def __init__(self, array):
        self.array = array


class Here:
    def __init__(self, ref):
        self.ref = self.dst = ref

    def part(self, part):
        return self.ref

    def __call__(self):
        return self.ref

    def flush(self, part=0, parts=1):
        pass


def call(body, outs, scratch, *args, scalars=0):
    wraps = (Raw, Halves, Near)
    plain = [a.array if isinstance(a, wraps) else a for a in args]
    out_shapes = [o.array if isinstance(o, wraps) else o for o in outs]
    autos = [i for i, a in enumerate(args) if i >= scalars and not isinstance(a, (Raw, Near))]
    made = [i for i, o in enumerate(outs) if not isinstance(o, (Raw, Near))]
    rooms = [pltpu.VMEM(plain[i].shape, plain[i].dtype) for i in autos]
    rooms += [pltpu.VMEM(out_shapes[i].shape, out_shapes[i].dtype) for i in made]

    def kernel(*refs):
        ins, refs = refs[: len(args)], refs[len(args) :]
        dsts, refs = refs[: len(outs)], refs[len(outs) :]
        sems, refs = refs[0], refs[1:]
        vin, refs = refs[: len(autos)], refs[len(autos) :]
        vout, rest = refs[: len(made)], refs[len(made) :]
        copies = Copies(sems)
        operands = [Here(r) if isinstance(a, Near) else r for a, r in zip(args, ins, strict=True)]
        for i, room in zip(autos, vin, strict=True):
            parts = 2 if isinstance(args[i], Halves) else 1
            operands[i] = Arrival(copies, ins[i], room, parts)
        results = [Here(r) if isinstance(o, Near) else r for o, r in zip(outs, dsts, strict=True)]
        for i, room in zip(made, vout, strict=True):
            results[i] = Result(copies, room, dsts[i])

        def begin(*some):
            for one in some or [operands[i] for i in autos]:
                operand, parts = one if isinstance(one, tuple) else (one, None)
                for part in range(operand.parts) if parts is None else (parts,):
                    operand.begin(part)

        body(copies, begin, *operands, *results, *rest)
        for r in results:
            if isinstance(r, Result) and not r.sent:
                r.flush()
        copies.finish()
        used.append(copies.used)

    near = pl.BlockSpec(memory_space=pltpu.VMEM)
    far = pl.BlockSpec(memory_space=pltpu.HBM)
    plain[scalars:] = [
        a if isinstance(w, Near) else pltpu.with_memory_space_constraint(a, pltpu.HBM)
        for w, a in zip(args[scalars:], plain[scalars:], strict=True)
    ]
    used = []

    def made_call(count):
        return pl.pallas_call(
            kernel,
            out_shape=[
                s if isinstance(o, Near) else pltpu.HBM(s.shape, s.dtype)
                for o, s in zip(outs, out_shapes, strict=True)
            ],
            in_specs=[pl.BlockSpec(memory_space=pltpu.SMEM)] * scalars
            + [near if isinstance(a, Near) else far for a in args[scalars:]],
            out_specs=[near if isinstance(o, Near) else far for o in outs],
            scratch_shapes=[pltpu.SemaphoreType.DMA((count,))] + rooms + list(scratch),
            compiler_params=pltpu.CompilerParams(vmem_limit_bytes=32 * 1024 * 1024),
        )

    jax.eval_shape(made_call(128), *plain)
    return made_call(max(used[0], 1))(*plain)


def cat(ref, rows):
    return jnp.concatenate([ref[j, rows, :] for j in range(ref.shape[0])], axis=1)


def put(ref, rows, val):
    for j in range(ref.shape[0]):
        ref[j, rows, :] = val[:, j * LANES : (j + 1) * LANES].astype(ref.dtype)


def rowcat(ref, r):
    return jnp.concatenate([ref[j, r : r + 1, :] for j in range(ref.shape[0])], axis=1)


def lanes(rows):
    return jnp.concatenate([rows[j : j + 1, :] for j in range(rows.shape[0])], axis=1)


def dot(a, b):
    return jnp.dot(a, b, preferred_element_type=F32)


def dot_nt(a, b):
    return lax.dot_general(a, b, NT, preferred_element_type=F32)


def dot_tn(a, b):
    return lax.dot_general(a, b, TN, preferred_element_type=F32)


def chunks(rows, count):
    size = rows // count
    return [slice(i * size, (i + 1) * size) for i in range(count)]


def sweep(src, dst, table, init, reset, reverse, conj):
    halves = src.shape[0] // 2
    span = src.shape[1] // SUB
    rate_re = [jnp.broadcast_to(table[h : h + 1, :], (SUB, LANES)) for h in range(halves)]
    rate_im = [
        jnp.broadcast_to(table[halves + h : halves + h + 1, :], (SUB, LANES))
        for h in range(halves)
    ]
    if conj:
        rate_im = [-r for r in rate_im]
    base = lax.broadcasted_iota(jnp.int32, (SUB, LANES), 0) * span - reset

    def body(step, state):
        j = span - 1 - step if reverse else step
        drop = base == -j
        at = pl.ds(j, SUB, stride=span)
        new_re, new_im = [], []
        for h in range(halves):
            a = jnp.where(drop, 0.0, rate_re[h])
            b = jnp.where(drop, 0.0, rate_im[h])
            re, im = state[h], state[halves + h]
            new_re.append((src[h, at, :] + a * re) - b * im)
            new_im.append((src[halves + h, at, :] + a * im) + b * re)
        state = tuple(new_re + new_im)
        if dst is not None:
            for k in range(2 * halves):
                dst[k, at, :] = state[k]
        return state

    return lax.fori_loop(0, span, body, init, unroll=8)


def zeros_state(halves):
    return tuple(jnp.zeros((SUB, LANES), F32) for _ in range(2 * halves))


def chain_segments(ends, first, table, reset, span, reverse, conj):
    halves = len(ends) // 2
    power_re = [table[4 + h : 5 + h, :] for h in range(halves)]
    power_im = [table[6 + h : 7 + h, :] for h in range(halves)]
    if conj:
        power_im = [-r for r in power_im]
    state = list(first)
    incoming = [[None] * SUB for _ in ends]
    order = range(SUB - 1, -1, -1) if reverse else range(SUB)
    for k in order:
        inside = (reset >= k * span) & (reset < (k + 1) * span)
        keep = jnp.where(inside, 0.0, 1.0)
        new = [None] * len(ends)
        for h in range(halves):
            re, im = state[h], state[halves + h]
            incoming[h][k], incoming[halves + h][k] = re, im
            new[h] = keep * (power_re[h] * re - power_im[h] * im) + ends[h][k : k + 1, :]
            new[halves + h] = (
                keep * (power_re[h] * im + power_im[h] * re) + ends[halves + h][k : k + 1, :]
            )
        state = new
    return [jnp.concatenate(rows, axis=0) for rows in incoming], state


def zero_rows(halves):
    return [jnp.zeros((1, LANES), F32) for _ in range(2 * halves)]


def emit_ends(out, ends_out, ends, table, reset, span, reverse, conj):
    halves = len(ends) // 2
    _, last = chain_segments(ends, zero_rows(halves), table, reset, span, reverse, conj)
    tile = jnp.concatenate(last, axis=0)
    out.ref[...] = jnp.broadcast_to(tile[None], out.ref.shape)
    out.flush()
    for k in range(2 * halves):
        ends_out.ref[k, :, :] = ends[k]
    ends_out.flush()


def carried_in(gathered, moments, table, me, reverse, conj):
    count = gathered.shape[0]
    power_re = table[8:10, :]
    power_im = table[10:12, :]
    if conj:
        power_im = -power_im
    flag = 3 if reverse else 2

    def body(i, state):
        d = count - 1 - i if reverse else i
        re, im = state
        keep = moments[d, flag : flag + 1, :]
        tile = gathered[d]
        return (
            keep * (power_re * re - power_im * im) + tile[0:2, :],
            keep * (power_re * im + power_im * re) + tile[2:4, :],
        )

    zero = jnp.zeros((2, LANES), F32)
    re, im = lax.fori_loop(0, count - 1 - me if reverse else me, body, (zero, zero))
    return [re[0:1, :], re[1:2, :], im[0:1, :], im[1:2, :]]


def place():
    mp = lax.axis_index("mp")
    return mp, lax.axis_index("dp") * lax.axis_size("mp") + mp


def local_resets(start, rows):
    offset = start[0]
    shift = jnp.where(offset > 0, offset - lax.axis_index("mp") * rows, -(1 << 20))
    return shift, shift - 1


def first_kernel(rows, copies, begin, start, stream, gain, shift, skip, vbias, gbias, decay, phase, scale,
                 moments, table_out, send1, send2, send3, held):
    mp, _ = place()
    total, width = held.shape
    parts = total // rows
    arrive = [copies.start(along(stream, i, parts), along(held, i, parts)) for i in range(parts)]
    begin()
    size = 128
    one = two = jnp.zeros((SUB, LANES), F32)

    def body(i, carry):
        one, two = carry
        x = held[pl.ds(i * size, size), :]
        for g in range(0, size, SUB):
            piece = x[g : g + SUB, :]
            one = one + piece
            two = two + piece * piece
        return one, two

    for i in range(parts):
        arrive[i].wait()
        one, two = lax.fori_loop(i * rows // size, (i + 1) * rows // size, body, (one, two))
    fwd, bwd = local_resets(start, rows)
    keep_f = jnp.where((fwd >= 0) & (fwd < rows), 0.0, 1.0)
    keep_b = jnp.where((bwd >= 0) & (bwd < rows), 0.0, 1.0)
    tile = jnp.concatenate(
        [
            jnp.sum(one, axis=0, keepdims=True),
            jnp.sum(two, axis=0, keepdims=True),
            jnp.full((1, LANES), keep_f, F32),
            jnp.full((1, LANES), keep_b, F32),
        ],
        axis=0,
    )
    moments.ref[...] = jnp.broadcast_to(tile[None], moments.ref.shape)
    moments.flush()
    gain, shift, skip, vbias, gbias = (a() for a in (gain, shift, skip, vbias, gbias))
    decay, phase, scale = decay(), phase(), scale()
    layers = decay.shape[0]
    plist = jnp.concatenate(
        [a[l : l + 1, :] for l in range(layers) for a in (gain, shift, skip, vbias, gbias)]
        + [jnp.zeros((16 - PARAMS * layers, width), F32)],
        axis=0,
    )
    high = plist.astype(BF16)
    rest = (plist - high.astype(F32)).astype(BF16)
    for k, send in ((1, send1), (2, send2), (3, send3)):
        base = (mp ^ k) * rows
        send.ref[0:rows, :] = held[pl.ds(pl.multiple_of(base, SUB), rows), :].astype(BF16)
        send.ref[rows : rows + 16, :] = high
        send.ref[rows + 16 : rows + 32, :] = rest
        send.flush()
    span = rows // SUB
    table = table_out.ref
    for layer in range(layers):
        for h in range(2):
            cols = slice(h * LANES, (h + 1) * LANES)
            radius = jnp.exp(-jnp.exp(decay[layer : layer + 1, cols]))
            angle = jnp.exp(phase[layer : layer + 1, cols])
            re, im = radius * jnp.cos(angle), radius * jnp.sin(angle)
            table[layer, h : h + 1, :] = re
            table[layer, 2 + h : 3 + h, :] = im
            length = 1
            while length < rows:
                re, im = re * re - im * im, 2.0 * re * im
                length *= 2
                if length == span:
                    table[layer, 4 + h : 5 + h, :] = re
                    table[layer, 6 + h : 7 + h, :] = im
            table[layer, 8 + h : 9 + h, :] = re
            table[layer, 10 + h : 11 + h, :] = im
            table[layer, 12 + h : 13 + h, :] = jnp.exp(scale[layer : layer + 1, cols])
            table[layer, 14 + h : 15 + h, :] = jnp.zeros((1, LANES), F32)


def pack_maps(layers, copies, begin, c_own, v_own, g_own, weight, *packs):
    begin()
    *packs, near = packs
    copies.flush(weight.at[0], near.ref)
    for layer in range(layers):
        for i, own in enumerate((c_own, v_own, g_own)):
            deep = own().shape[1]
            packs[layer].ref[i * deep : (i + 1) * deep, :] = own()[layer]
        packs[layer].flush()


def pack_block(copies, begin, x, weight, near, *sends):
    mp, _ = place()
    rows = sends[0].ref.shape[0]
    begin()
    copies.flush(weight.at[1], near.ref)
    whole = x()
    for k, send in enumerate(sends):
        base = pl.multiple_of((mp ^ (k + 1)) * rows, SUB)
        send.ref[...] = whole[pl.ds(base, rows), :].astype(BF16)
        send.flush()


def gather_block(copies, begin, got1, got2, got3, gain, shift, skip, vbias, gbias, stream, h, prm, held):
    mp, _ = place()
    rows = h.ref.shape[1]
    own = Later(copies, [(own_rows(stream, rows), held)], held)
    begin()
    plist = [a() for a in (gain, shift, skip, vbias, gbias)]
    layers = plist[0].shape[0]
    for k, got in ((1, got1), (2, got2), (3, got3)):
        got = got()
        h.ref[mp ^ k, :, :] = got[0:rows, :].astype(F32)
        pair = got[rows : rows + 16, :].astype(F32) + got[rows + 16 : rows + 32, :].astype(F32)
        prm.ref[mp ^ k, :, :] = pair
    mine = [a[l : l + 1, :] for l in range(layers) for a in plist]
    prm.ref[mp, 0 : PARAMS * layers, :] = jnp.concatenate(mine, axis=0)
    prm.ref[mp, PARAMS * layers :, :] = jnp.zeros((16 - PARAMS * layers, LANES), F32)
    h.ref[mp, :, :] = own()[...]


def norm_rows(mean, second, gain, shift):
    inverse = lax.rsqrt(second - mean * mean + epsilon)
    factor = inverse * gain
    return inverse, factor, shift - mean * factor


def drive_body(layer, mean, second, start, h, prm, table, weight, drive, norms, out, ends_out, slow):
    rows = drive.ref.shape[1]
    reverse = layer % 2 == 1
    base = layer * PARAMS
    inverse, factor, bias = norm_rows(
        mean, second, rowcat(prm, base + GAIN), rowcat(prm, base + SHIFT)
    )
    norms.ref[...] = jnp.concatenate(
        [factor, bias, inverse, mean] + [jnp.zeros_like(mean)] * 4, axis=0
    )
    norms.flush()
    gamma = lanes(table[layer, 12:14, :])
    gamma = jnp.concatenate([gamma, gamma], axis=1)
    for i, at in enumerate(chunks(rows, 2)):
        low = (cat(h, at) * factor + bias).astype(BF16)
        slow.ref[at, :] = low
        slow.flush(i, 2)
        put(drive.ref, at, dot(low, weight()[...]) * gamma)
        drive.flush(i, 2)
    fwd, bwd = local_resets(start, rows)
    reset = bwd if reverse else fwd
    ends = sweep(drive.ref, None, table[layer], zeros_state(2), reset, reverse, False)
    emit_ends(out, ends_out, ends, table[layer], reset, rows // SUB, reverse, False)


class Later:
    def __init__(self, copies, pairs, dst):
        self.waits, self.dst = [copies.start(src, to) for src, to in pairs], dst

    def __call__(self):
        for copy in self.waits:
            copy.wait()
        self.waits = []
        return self.dst


def own_rows(ref, rows, k=0):
    mp, _ = place()
    return ref.at[pl.ds(pl.multiple_of((mp ^ k) * rows, SUB), rows)]


def total_of(gathered):
    tile = gathered[0]
    for d in range(1, gathered.shape[0]):
        tile = tile + gathered[d]
    return tile


def drive_first(total_tokens, copies, begin, start, mom, table, h, prm, weight, drive, norms, out, ends, slow):
    mom = mom()
    groups = h.ref.shape[0]
    sums = [mom[j, 0:2, :] for j in range(groups)]
    for d in range(groups, mom.shape[0]):
        sums[d % groups] = sums[d % groups] + mom[d, 0:2, :]
    both = jnp.concatenate(sums, axis=1) * (1.0 / total_tokens)
    drive_body(0, both[0:1, :], both[1:2, :], start, h(), prm(), table(), weight, drive, norms, out, ends, slow)


def drive_next(layer, total_tokens, copies, begin, start, mom, prm, table, h, weight, drive, norms, out, ends, slow):
    tile = total_of(mom()) * (1.0 / total_tokens)
    half = tile.shape[0] // 2
    mean, second = lanes(tile[:half]), lanes(tile[half:])
    drive_body(layer, mean, second, start, h(), prm(), table(), weight, drive, norms, out, ends, slow)


def resume(start, rows, gathered, mom, tab, ends, reverse, conj):
    fwd, bwd = local_resets(start, rows)
    reset = bwd if reverse else fwd
    first = carried_in(gathered, mom, tab, place()[1], reverse, conj)
    incoming, _ = chain_segments(
        [ends[k] for k in range(4)], first, tab, reset, rows // SUB, reverse, conj
    )
    return tuple(incoming), reset


def assemble(copies, begin, p0, p1, p2, p3, maps):
    begin()
    mp, _ = place()
    count, deep = maps.ref.shape[0], maps.ref.shape[1]
    for k, piece in enumerate((p0, p1, p2, p3)):
        cols = pl.ds(pl.multiple_of((mp ^ k) * LANES, LANES), LANES)
        for i in range(count):
            maps.ref[i, :, cols] = piece()[i * deep : (i + 1) * deep, :]


def gather_cotangent(copies, begin, got1, got2, got3, cot, full):
    begin()
    mp, _ = place()
    rows = full.ref.shape[0]
    own = cot()[pl.ds(pl.multiple_of(mp * rows, SUB), rows), :].astype(BF16)
    for k, block in enumerate((own, got1()[...], got2()[...], got3()[...])):
        full.ref[:, pl.ds(pl.multiple_of((mp ^ k) * LANES, LANES), LANES)] = block


def fetch_maps(copies, far, near, order=(0, 1, 2)):
    return {i: Later(copies, [(far.at[i], near.at[i])], near.at[i]) for i in order}


def mix_chunk(layer, at, h, norms, states, maps, prm):
    base = layer * PARAMS
    x = cat(h, at)
    scaled = x * norms[0:1, :] + norms[1:2, :]
    states_low = cat(states, at).astype(BF16)
    mixed = dot(states_low, maps[0]()[...]) + rowcat(prm, base + SKIP) * scaled
    square = mixed * mixed
    wave = jnp.tanh(ROOT * mixed * (1.0 + CUBE * square))
    half = 0.5 * (1.0 + wave)
    sent_low = (mixed * half).astype(BF16)
    slope = half + 0.5 * mixed * (1.0 - wave * wave) * (ROOT * (1.0 + 3.0 * CUBE * square))
    value = dot(sent_low, maps[1]()[...]) + rowcat(prm, base + VBIAS)
    gate = dot(sent_low, maps[2]()[...]) + rowcat(prm, base + GBIAS)
    sig = 0.5 + 0.5 * jnp.tanh(0.5 * gate)
    gated = value * sig
    return x, scaled, states_low, sent_low, slope, sig, gated


def back_chunk(i, at, g, sig, gain_part, scaled, slope, maps, outs, sums):
    dv, dg, dml, ds = outs
    dvalue = g * sig
    dgate = g * gain_part
    dv_low, dg_low = dvalue.astype(BF16), dgate.astype(BF16)
    dmixed = (dot_nt(dv_low, maps[1]()[...]) + dot_nt(dg_low, maps[2]()[...])) * slope()
    dm_low = dmixed.astype(BF16)
    put(ds.ref, at, dot_nt(dm_low, maps[0]()[...]))
    dv.ref[at, :] = dv_low
    dg.ref[at, :] = dg_low
    dml.ref[at, :] = dm_low
    for o in outs:
        o.flush(i, 2)
    add = lambda v: jnp.sum(v, axis=0, keepdims=True)
    return [
        s + n for s, n in zip(sums, [add(dvalue), add(dgate), add(dmixed * scaled())], strict=True)
    ]


def sums_rows(sums_out, sums):
    rows = sums + [jnp.zeros_like(sums[0])] * (8 - len(sums))
    sums_out.ref[...] = jnp.concatenate(rows, axis=0)
    sums_out.flush()


def share_out(keep, send, pack, copies):
    mp, _ = place()
    for ref, i, k in ((send, 0, 1), (send, 1, 3), (keep, 0, 0), (keep, 1, 2)):
        ref.ref[i, :, :] = pack[mp ^ k, :, :]


def weight_share(sent, dv, dg, states, dml, sums, pack):
    width = sent.dst.shape[1]
    parts = pack.shape[0]
    both = jnp.concatenate([dv()[...], dg()[...]], axis=1)
    both = dot_tn(sent()[...], both)
    put(pack, slice(0, width), both[:, :width])
    put(pack, slice(width, 2 * width), both[:, width:])
    put(pack, slice(2 * width, 3 * width), dot_tn(states()[...], dml()[...]))
    sums = sums()
    for j in range(parts):
        cols = slice(j * LANES, (j + 1) * LANES)
        rows = jnp.concatenate([sums[:, cols], jnp.zeros((8, LANES), F32)], axis=0)
        pack[j, 3 * width : 3 * width + 16, :] = rows.astype(pack.dtype)


def weight_grads(copies, begin, sent, dv, dg, states, dml, sums, keep, send, pack):
    begin()
    weight_share(sent, dv, dg, states, dml, sums, pack)
    share_out(keep, send, pack, copies)


def input_share(base, copies, slow, dlow, prods, weight, pack, held, sums=None):
    width = slow.dst.shape[1]
    held[...] = dot_tn(slow()[...], dlow()[...])
    half = width // 2
    y_re = y_im = jnp.zeros((1, half), F32)
    size = 64
    for top in range(0, width, size):
        rows = slice(top, top + size)
        grad = held[rows, :]
        put(pack, slice(base + top, base + top + size), grad)
        grad_re, grad_im = grad[:, :half], grad[:, half:]
        w = weight()[rows, :].astype(F32)
        w_re, w_im = w[:, :half], w[:, half:]
        y_re = y_re + jnp.sum(grad_re * w_re + grad_im * w_im, axis=0, keepdims=True)
        y_im = y_im + jnp.sum(grad_im * w_re - grad_re * w_im, axis=0, keepdims=True)
    prods = prods()
    rows = []
    for h in range(2):
        cols = slice(h * LANES, (h + 1) * LANES)
        rows += [prods[2 * h : 2 * h + 1, :] - y_re[:, cols], prods[2 * h + 1 : 2 * h + 2, :] - y_im[:, cols]]
        rows += [y_re[:, cols]]
    for j in range(pack.shape[0]):
        cols = slice(j * LANES, (j + 1) * LANES)
        more = [] if sums is None else [sums()[0:2, cols]]
        tile = rows + more + [jnp.zeros((10 - 2 * len(more), LANES), F32)]
        pack[j, base + width : base + width + 16, :] = jnp.concatenate(tile, axis=0).astype(pack.dtype)


def input_grads(layer, copies, begin, slow, dlow, prods, sums, weight, keep, send, pack, held, maps):
    begin()
    weight = Later(copies, [(weight.at[layer], maps)], maps)
    input_share(0, copies, slow, dlow, prods, weight, pack, held, sums)
    share_out(keep, send, pack, copies)


def both_grads(layer, copies, begin, sent, dv, dg, states, dml, sums, slow, dlow, prods, weight, keep, send,
               pack, held, maps):
    begin()
    weight = Later(copies, [(weight.at[layer + 1], maps)], maps)
    weight_share(sent, dv, dg, states, dml, sums, pack)
    input_share(3 * sent.dst.shape[1] + 16, copies, slow, dlow, prods, weight, pack, held)
    share_out(keep, send, pack, copies)


def add_chunk(mom, one, two):
    tile = jnp.concatenate(
        [one[:, j * LANES : (j + 1) * LANES] for j in range(one.shape[1] // LANES)]
        + [two[:, j * LANES : (j + 1) * LANES] for j in range(two.shape[1] // LANES)],
        axis=0,
    )
    mom.ref[...] = jnp.broadcast_to(tile[None], mom.ref.shape)
    mom.flush()


def mix_first(layer, copies, begin, start, gathered, mom, table, ends, norms, prm, drive, h, far_maps,
              new_h, new_mom, h_far, states_low_out, sent, slope_out, sig_out, part_out, states, maps):
    rows = states.shape[1]
    ready = fetch_maps(copies, far_maps, maps)
    copies.flush(h.ref, h_far)
    reverse = layer % 2 == 1
    tab = table()[layer]
    init, reset = resume(start, rows, gathered(), mom(), tab, ends(), reverse, False)
    sweep(drive(), states, tab, init, reset, reverse, False)
    norms, prm = norms(), prm()
    one = two = 0.0
    for i, at in enumerate(chunks(rows, 2)):
        x, scaled, states_low, sent_low, slope, sig, gated = mix_chunk(
            layer, at, h(), norms, states, ready, prm
        )
        states_low_out.ref[at, :] = states_low
        sent.ref[at, :] = sent_low
        slope_out.ref[at, :] = slope.astype(BF16)
        sig_out.ref[at, :] = sig.astype(BF16)
        part_out.ref[at, :] = (gated * (1.0 - sig)).astype(BF16)
        new = x + gated
        put(new_h.ref, at, new)
        one = one + jnp.sum(new, axis=0, keepdims=True)
        two = two + jnp.sum(new * new, axis=0, keepdims=True)
        for o in (states_low_out, sent, slope_out, sig_out, part_out):
            o.flush(i, 2)
    add_chunk(new_mom, one, two)


def turn(layer, copies, begin, start, gathered, mom, table, ends, norms, prm, drive, h, far_maps, cot,
         ds, out, ends_out, h_far, states_low_out, sent, dv, dg, dml, sums_out, r0, r1, r2, r3,
         maps, states, new_h):
    mp, _ = place()
    rows = states.shape[1]
    ready = fetch_maps(copies, far_maps, maps)
    begin()
    copies.flush(h.ref, h_far)
    reverse = layer % 2 == 1
    tab = table()[layer]
    init, reset = resume(start, rows, gathered(), mom(), tab, ends(), reverse, False)
    sweep(drive(), states, tab, init, reset, reverse, False)
    norms, prm = norms(), prm()
    sums = [0.0, 0.0, 0.0]
    for i, at in enumerate(chunks(rows, 2)):
        x, scaled, states_low, sent_low, slope, sig, gated = mix_chunk(
            layer, at, h(), norms, states, ready, prm
        )
        states_low_out.ref[at, :] = states_low
        sent.ref[at, :] = sent_low
        put(new_h, at, x + gated)
        g = cot.part(i)[at, :].astype(F32)
        for o in (states_low_out, sent):
            o.flush(i, 2)
        sums = back_chunk(i, at, g, sig, gated * (1.0 - sig), lambda: scaled, lambda: slope,
                          ready, (dv, dg, dml, ds), sums)
    sums_rows(sums_out, sums)
    for k, r in enumerate((r0, r1, r2, r3)):
        r.ref[...] = new_h[mp ^ k, :, :].astype(r.ref.dtype)
        r.flush()
    adjoint_start(layer, start, tab, ds.ref, out, ends_out)


def adjoint_start(layer, start, tab, ds, out, ends_out):
    rows = ds.shape[1]
    reverse = layer % 2 == 0
    fwd, bwd = local_resets(start, rows)
    reset = bwd if reverse else fwd
    ends = sweep(ds, None, tab, zeros_state(2), reset, reverse, True)
    emit_ends(out, ends_out, ends, tab, reset, rows // SUB, reverse, True)


def back_first(layer, total_tokens, copies, begin, start, back, norms1, table, prm, u, norms,
               slow1, sig, part, slope, slow, far_maps, g_out, ds, out, ends_out, tile_out, dv, dg, dml, sums_out,
               maps):
    begin((slow1, 0), (sig, 0), (part, 0))
    ready = fetch_maps(copies, far_maps, maps, (1, 2))
    rows = ds.ref.shape[1]
    tile = total_of(back())
    tile_out.ref[...] = tile
    norms1, norms, prm = norms1(), norms(), prm()
    half = tile.shape[0] // 2
    base = (layer + 1) * PARAMS
    over = 1.0 / rowcat(prm, base + GAIN)
    shift = rowcat(prm, base + SHIFT)
    factor = norms1[0:1, :] * (1.0 / total_tokens)
    m_one, m_two = factor * lanes(tile[:half]), factor * over * lanes(tile[half:])
    m_one = m_one - shift * m_two
    sums = [0.0, 0.0, 0.0]
    for i, at in enumerate(chunks(rows, 2)):
        g = cat(u(), at) - m_one - slow1.part(i)[at, :].astype(F32) * m_two
        if i == 0:
            begin((slope, 0))
            ready.update(fetch_maps(copies, far_maps, maps, (0,)))
            begin((slow, 0), (slow1, 1), (sig, 1), (part, 1), (slope, 1), (slow, 1))
        put(g_out.ref, at, g)
        g_out.flush(i, 2)
        low = lambda x: x.part(i)[at, :].astype(F32)
        sums = back_chunk(i, at, g, low(sig), low(part), lambda: low(slow), lambda: low(slope),
                          ready, (dv, dg, dml, ds), sums)
    sums_rows(sums_out, sums)
    adjoint_start(layer, start, table()[layer], ds.ref, out, ends_out)


def back_second(layer, copies, begin, start, gathered, mom, table, ends, norms, prm, ds, states_low, g, dml, h,
                weight, *refs):
    if layer == 0:
        back, prods, dlow, u0, u1, u2, u3, adj, maps, u_ref = refs
    else:
        back, u_out, prods, dlow, adj, maps = refs
        u_ref = u_out.ref
        begin(g)
    begin(states_low)
    weight = Later(copies, [(weight.at[layer], maps)], maps)
    begin((dml, 0), (h, 0))
    if layer == 0:
        begin((g, 0), (g, 1))
    begin((dml, 1), (h, 1))
    rows = adj.shape[1]
    reverse = layer % 2 == 0
    tab = table()[layer]
    init, reset = resume(start, rows, gathered(), mom(), tab, ends(), reverse, True)
    sweep(ds(), adj, tab, init, reset, reverse, True)
    half = adj.shape[0] // 2 * LANES
    prod_re = prod_im = jnp.zeros((SUB, half), F32)
    for at in chunks(rows, 16):
        a, s = cat(adj, at), states_low()[at, :].astype(F32)
        a_re, a_im, s_re, s_im = a[:, :half], a[:, half:], s[:, :half], s[:, half:]
        re, im = a_re * s_re + a_im * s_im, a_im * s_re - a_re * s_im
        for top in range(0, re.shape[0], SUB):
            prod_re = prod_re + re[top : top + SUB, :]
            prod_im = prod_im + im[top : top + SUB, :]
    flat = [jnp.sum(x, axis=0, keepdims=True) for x in (prod_re, prod_im)]
    flat = [x[:, h_ * LANES : (h_ + 1) * LANES] for h_ in range(2) for x in flat]
    prods.ref[...] = jnp.concatenate(flat + [jnp.zeros((8 - len(flat), LANES), F32)], axis=0)
    prods.flush()
    gamma = lanes(tab[12:14, :])
    gamma = jnp.concatenate([gamma, gamma], axis=1)
    base = layer * PARAMS
    prm, norms = prm(), norms()
    skip = rowcat(prm, base + SKIP)
    factor, bias, inverse, mean = (norms[i : i + 1, :] for i in range(4))
    one = two = 0.0
    for i, at in enumerate(chunks(rows, 2)):
        low = (cat(adj, at) * gamma).astype(BF16)
        dlow.ref[at, :] = low
        dlow.flush(i, 2)
        dscaled = dot_nt(low, weight()[...]) + dml.part(i)[at, :].astype(F32) * skip
        normed = (cat(h.part(i), at) - mean) * inverse
        own = g()[at, :].astype(F32) if layer == 1 else cat(g.part(i), at)
        put(u_ref, at, own + factor * dscaled)
        one = one + jnp.sum(dscaled, axis=0, keepdims=True)
        two = two + jnp.sum(dscaled * normed, axis=0, keepdims=True)
    if layer == 0:
        back.ref[...] = jnp.concatenate([one, two] + [jnp.zeros_like(one)] * 6, axis=0)
        mp, _ = place()
        for k, piece in enumerate((u0, u1, u2, u3)):
            piece.ref[...] = u_ref[mp ^ k, :, :].astype(piece.ref.dtype)
            piece.flush()
    else:
        add_chunk(back, one, two)


def result_kernel(copies, begin, r0, r1, r2, r3, result):
    begin()
    mp, _ = place()
    rows = r0.dst.shape[0]
    for k, r in ((1, r1), (2, r2), (3, r3), (0, r0)):
        at = pl.ds(pl.multiple_of((mp ^ k) * rows, SUB), rows)
        result.ref[at, :] = r()[...].astype(F32)
        copies.flush(result.ref.at[at], result.dst.at[at])
    result.sent = True


def last_kernel(total_tokens, in_piece, copies, begin, norms, back, tile1, u0, u1, u2, u3, stream,
                out, gain_out, shift_out, held):
    begin()
    mp, _ = place()
    rows = u0.dst.shape[0]
    streams = [Later(copies, [(own_rows(stream, rows, k), held.at[k])], held.at[k]) for k in range(4)]
    tile1, norms = tile1(), norms()
    width = norms.shape[1]
    ((_, _, sums),) = unpieced(back(), 0, in_piece, width, 16)
    sums = sums.astype(F32)
    one, two = sums[6:7, :], sums[7:8, :]
    half = tile1.shape[0] // 2
    zero = jnp.zeros((1, LANES), F32)
    factor, inverse, mean, later_one, later_two = [zero] * 5
    for j in range(half):
        mine = jnp.where(mp == j, 1.0, 0.0)
        cols = slice(j * LANES, (j + 1) * LANES)
        later_one = later_one + mine * tile1[j : j + 1, :]
        later_two = later_two + mine * tile1[half + j : half + j + 1, :]
        factor = factor + mine * norms[0:1, cols]
        inverse = inverse + mine * norms[2:3, cols]
        mean = mean + mine * norms[3:4, cols]
    scaled = factor * (1.0 / total_tokens)
    m_one, m_two = scaled * one, scaled * two
    for k, u in enumerate((u0, u1, u2, u3)):
        at = pl.ds(pl.multiple_of((mp ^ k) * rows, SUB), rows)
        normed = (streams[k]()[...] - mean) * inverse
        out.ref[at, :] = u()[...].astype(F32) - m_one - normed * m_two
        copies.flush(out.ref.at[at], out.dst.at[at])
    out.sent = True
    gain_out.ref[...] = jnp.concatenate([two, later_two], axis=0)
    shift_out.ref[...] = jnp.concatenate([one, later_one], axis=0)


def pair_sum(copies, begin, keep, got, mine, other):
    keep, got = keep(), got()
    size = keep.shape[1]
    for at in chunks(size, size // 16):
        other.ref[at, :] = (keep[1, at, :].astype(F32) + got[1, at, :].astype(F32)).astype(other.ref.dtype)
        mine.ref[at, :] = (keep[0, at, :].astype(F32) + got[0, at, :].astype(F32)).astype(mine.ref.dtype)


def four_sum(order, copies, begin, *refs):
    *ins, out = refs
    out = out.ref
    for mine, got, spans in zip(ins[::2], ins[1::2], order, strict=True):
        mine, got = mine(), got()
        row = 0
        for rows, size, base, first, last in spans:
            for i in range(0, out.shape[0] * size - first if last else rows, 16):
                d, top = (first + i) // size, base + (first + i) % size
                if i < rows:
                    at = slice(row + i, row + i + 16)
                    total = (mine[at, :].astype(F32) + got[at, :].astype(F32)).astype(out.dtype)
                else:
                    total = jnp.zeros((16, out.shape[2]), out.dtype)
                out[d, top : top + 16, :] = total
            row += rows


def piece_total(pieces, at):
    total = pieces[0, at, :].astype(F32)
    for d in range(1, pieces.shape[0]):
        total = total + pieces[d, at, :].astype(F32)
    return total.astype(BF16)


def piece_sum(copies, begin, pieces, out):
    for at in chunks(out.ref.shape[0], out.ref.shape[0] // 16):
        out.ref[at, :] = piece_total(pieces(), at)


def piece_sums(sizes, copies, begin, pieces, other, first, rest):
    in_piece, vgo_piece = sizes
    rows = pieces().shape[1]
    for at in chunks(rows, rows // 16):
        low = piece_total(pieces(), at)
        inputs = at.start < in_piece
        out, top = (first.ref, at.start) if inputs else (rest.ref, at.start - in_piece)
        for d in range(out.shape[0]):
            out[d, top : top + 16, :] = low
    for at in chunks(vgo_piece, vgo_piece // 16):
        low = other()[at, :]
        for d in range(rest.ref.shape[0]):
            rest.ref[d, vgo_piece + at.start : vgo_piece + at.stop, :] = low


def unpieced(pieces, offset, size, first, rows):
    at = first
    while at < first + rows:
        piece, inside = at // size, at % size
        count = min(size - inside, first + rows - at)
        yield at - first, count, pieces[piece, offset + inside : offset + inside + count, :]
        at += count


def hand_out(features, sizes, copies, begin, decay, phase, full_in, full,
             o_grad, skip_grad, v_grad, g_grad, vb, gb, d_grad, p_grad, s_grad):
    begin()
    full, full_in = full(), full_in()
    in_piece, vgo_piece = sizes
    in_rows = features + 16
    for layer in range(2):
        base = layer * vgo_piece
        for i, out in enumerate((v_grad, g_grad, o_grad)):
            for at, count, rows in unpieced(full, base, vgo_piece, i * features, features):
                out.ref[layer, at : at + count, :] = rows.astype(F32)
            copies.flush(out.ref.at[layer], out.dst.at[layer])
            out.sent = True
    decay, phase = decay(), phase()
    for layer in range(2):
        base = layer * vgo_piece
        row = slice(layer, layer + 1)
        ((_, _, vecs),) = unpieced(full, base, vgo_piece, 3 * features, 16)
        vecs = vecs.astype(F32)
        vb.ref[row, :] = vecs[0:1, :]
        gb.ref[row, :] = vecs[1:2, :]
        skip_grad.ref[row, :] = vecs[2:3, :]
        ((_, _, tile),) = unpieced(full_in, 0, in_piece, layer * in_rows + features, 16)
        tile = tile.astype(F32)
        for h in range(2):
            cols = slice(h * LANES, (h + 1) * LANES)
            d_grad.ref[row, cols] = -jnp.exp(decay[row, cols]) * tile[3 * h : 3 * h + 1, :]
            p_grad.ref[row, cols] = jnp.exp(phase[row, cols]) * tile[3 * h + 1 : 3 * h + 2, :]
            s_grad.ref[row, cols] = tile[3 * h + 2 : 3 * h + 3, :]


def input_kernel(features, size, copies, begin, p0, p1, p2, p3, out):
    begin()
    mp, _ = place()
    for k, pieces in enumerate((p0, p1, p2, p3)):
        cols = pl.ds(pl.multiple_of((mp ^ k) * LANES, LANES), LANES)
        for layer in range(out.ref.shape[0]):
            for at, count, rows in unpieced(pieces(), 0, size, layer * (features + 16), features):
                out.ref[layer, at : at + count, cols] = rows.astype(F32)


def shape(dims, dtype=F32):
    return jax.ShapeDtypeStruct(tuple(dims), dtype)


def every(x):
    return lax.all_to_all(x, AXES, 0, 0)


def hop(x, k):
    count = lax.axis_size("mp")
    return lax.ppermute(x, "mp", [(i, i ^ k) for i in range(count)])


def spread(x, then=None):
    far = hop(x, 2)
    held = far if then is None else after(far, then)
    return hop(x, 1), far, hop(held, 1)


def swap(sends):
    return [hop(x, k + 1) for k, x in enumerate(sends)]


def after(x, *ys):
    return lax.optimization_barrier((x, *ys))[0]


def on_device(
    stream,
    cotangent,
    start_offsets,
    norm_gain,
    norm_shift,
    input_map,
    decay_log,
    phase_log,
    scale_log,
    output_map,
    skip_gain,
    value_weight,
    gate_weight,
    value_bias,
    gate_bias,
):
    block, width = stream.shape
    layers = input_map.shape[0]
    count_dp, parts = lax.axis_size("dp"), lax.axis_size("mp")
    devices = count_dp * parts
    tokens = block * count_dp
    rows = block // parts
    features = width * parts
    assert width == LANES and features == 4 * LANES and layers == 2 and parts == 4

    plist = (norm_gain, norm_shift, skip_gain, value_bias, gate_bias)
    blocks = shape((parts, rows, width))
    v_blocks = pltpu.VMEM(blocks.shape, F32)
    one_block = (rows, width)
    low_block = shape(one_block, BF16)
    wide_low = shape((rows, features), BF16)
    near_blocks = Near(blocks)
    near_ends = Near(shape((4, SUB, LANES)))
    near_every = Near(shape((devices, 4, LANES)))
    near_sums = Near(shape((devices, 2 * parts, LANES)))
    near_norms = Near(shape((8, features)))
    near_low = Near(low_block)
    packed_w = shape((3 * features, width), BF16)
    one_map = pltpu.VMEM((features, features), BF16)
    maps = pltpu.VMEM((3, features, features), BF16)
    all_maps = shape((3, features, features), BF16)
    near_map = Near(shape((features, features), BF16))

    mom_out, table, *sends = call(
        functools.partial(first_kernel, rows),
        [near_every, Near(shape((layers, 16, LANES)))] + [Near(shape((rows + 32, width), BF16))] * 3,
        [pltpu.VMEM((block, width), F32)],
        start_offsets, Raw(stream), *plist, decay_log, phase_log, scale_log,
        scalars=1,
    )
    table = Near(table)
    got_h = [Near(x) for x in swap(sends)]
    mom0 = every(after(mom_out, *[g.array for g in got_h]))
    h0, prm = call(
        gather_block,
        [near_blocks, Near(shape((parts, 16, width)))],
        [pltpu.VMEM(one_block, F32)],
        *got_h, *plist, Raw(stream),
    )
    h0, prm, mom0 = Near(h0), Near(prm), Near(after(mom0, h0))
    *packs, near_in = call(
        functools.partial(pack_maps, layers), [packed_w] * layers + [near_map], [],
        output_map, value_weight, gate_weight, Raw(input_map),
    )
    w0 = after(packs[0], got_h[1].array, got_h[2].array)
    (full0,) = call(assemble, [all_maps], [], w0, *[Near(w) for w in spread(w0, mom0.array)])

    drive0, norms0, ends_all, ends0, slow0 = call(
        functools.partial(drive_first, tokens),
        [near_blocks, near_norms, near_every, near_ends, wide_low],
        [],
        start_offsets, mom0, table, h0, prm, Near(near_in),
        scalars=1,
    )
    got = Near(after(every(ends_all), full0))
    norms0 = Near(norms0)
    h1, mom_out, h0, states0, sent0, slope0, sig0, part0 = call(
        functools.partial(mix_first, 0),
        [near_blocks, near_sums, Raw(blocks)] + [wide_low] * 5,
        [v_blocks, maps],
        start_offsets, got, mom0, table, Near(ends0), norms0, prm, Near(drive0), h0, Raw(full0),
        scalars=1,
    )
    h1 = Near(h1)
    near_in, *sends = call(
        pack_block, [near_map] + [low_block] * 3, [], after(cotangent, got.array), Raw(input_map)
    )
    mom1 = Near(after(every(mom_out), *sends))
    w1 = after(packs[1], got.array)
    (full1,) = call(assemble, [all_maps], [], w1, *[Near(w) for w in spread(w1, mom1.array)])
    drive1, norms1, ends_all, ends1, slow1 = call(
        functools.partial(drive_next, 1, tokens),
        [near_blocks, near_norms, near_every, near_ends, wide_low],
        [],
        start_offsets, mom1, prm, table, h1, Near(near_in),
        scalars=1,
    )
    got_cot = [Near(x) for x in swap([after(s, norms1) for s in sends])]
    (cot,) = call(gather_cotangent, [wide_low], [], *got_cot, after(cotangent, full1))
    got = Near(after(every(ends_all), full1, cot))
    norms1 = Near(norms1)
    vgo_rows, in_rows = 3 * features + 16, features + 16

    def pair_share(keep, send):
        size = Near(shape(keep.shape[1:], BF16))
        return call(pair_sum, [size, size], [], Near(keep), Near(hop(send, 1)))

    vgo_half = Near(shape((2, vgo_rows, width), BF16))
    in_half = Near(shape((2, in_rows, width), BF16))
    vgo_pack = pltpu.VMEM((parts, vgo_rows, width), BF16)
    both_half = Near(shape((2, vgo_rows + in_rows, width), BF16))
    both_pack = pltpu.VMEM((parts, vgo_rows + in_rows, width), BF16)
    in_pack = pltpu.VMEM((parts, in_rows, width), BF16)
    in_room = [in_pack, pltpu.VMEM((features, features), F32), one_map]
    ds1, ends_all, back_ends1, h1, states1, sent1, dv, dg, dml1, sums, *res = call(
        functools.partial(turn, 1),
        [near_blocks, near_every, near_ends, Raw(blocks)] + [wide_low] * 5 + [near_norms.array, shape(one_block)]
        + [low_block] * 3,
        [maps, v_blocks, v_blocks],
        start_offsets, got, mom0, table, Near(ends1), norms1, prm, Near(drive1), h1, Raw(full1), Halves(cot),
        scalars=1,
    )
    got = Near(every(ends_all))
    keep1, send1 = call(
        weight_grads, [vgo_half, vgo_half], [vgo_pack], sent1, dv, dg, states1, dml1, sums
    )
    got = Near(after(got.array, keep1))
    send1 = after(send1, got.array)
    got = Near(after(got.array, keep1))
    back_out, u1, prods, dlow = call(
        functools.partial(back_second, 1),
        [near_sums, near_blocks, shape((8, LANES)), wide_low],
        [v_blocks, one_map],
        start_offsets, got, mom0, table, Near(back_ends1), norms1, prm, Near(ds1), states1, cot, Halves(dml1),
        Halves(h1), Raw(input_map),
        scalars=1,
    )
    back1 = Near(every(back_out))
    late1 = (slow1, dlow, prods)
    mine1, other1 = pair_share(after(keep1, back_out), send1)
    back1 = Near(after(back1.array, mine1))
    far1 = hop(other1, 2)
    g0, ds0, ends_all, back_ends0, tile1, dv, dg, dml0, sums = call(
        functools.partial(back_first, 0, tokens),
        [blocks, near_blocks, near_every, near_ends, Near(shape((2 * parts, LANES)))] + [wide_low] * 3
        + [near_norms.array],
        [maps],
        start_offsets, back1, norms1, table, prm, Near(u1), norms0,
        Halves(slow1), Halves(sig0), Halves(part0), Halves(slope0), Halves(slow0), Raw(full0),
        scalars=1,
    )
    unit = 16 * count_dp
    in_piece, vgo_piece = (-(-n // unit) * 16 for n in (2 * in_rows, vgo_rows))

    def joined(order, *operands):
        piece = max(base + size for spans in order for _, size, base, _, _ in spans)
        out = Near(shape((count_dp, piece, width), BF16))
        return call(functools.partial(four_sum, order), [out], [], *map(Near, operands))[0]

    own1 = joined((((vgo_rows, vgo_piece, 0, 0, True),),), mine1, far1)
    got = Near(every(after(ends_all, far1)))
    keep0, send0 = call(
        functools.partial(both_grads, 0), [both_half, both_half], [both_pack] + in_room[1:],
        sent0, dv, dg, states0, dml0, sums, *late1, Raw(input_map),
    )
    pieces = lax.all_to_all(after(own1, got.array), "dp", 0, 0)
    (summed1,) = call(piece_sum, [Near(shape((vgo_piece, width), BF16))], [], Near(pieces))
    send0 = after(send0, got.array)
    got = Near(after(got.array, keep0))
    back_out, prods, dlow, *us = call(
        functools.partial(back_second, 0),
        [near_norms, Near(shape((8, LANES))), Near(wide_low), Near(shape(one_block))] + [near_low] * 3,
        [v_blocks, one_map, v_blocks],
        start_offsets, got, mom0, table, Near(back_ends0), norms0, prm, Near(ds0), states0, Halves(g0), Halves(dml0),
        Halves(h0), Raw(input_map),
        scalars=1,
    )
    mine0, other0 = pair_share(keep0, send0)
    far0 = hop(other0, 2)
    prods = after(prods, mine0)
    in_keep0, in_send0 = call(
        functools.partial(input_grads, 0), [in_half, in_half], in_room, slow0, Near(dlow), Near(prods), Near(back_out), Raw(input_map)
    )
    us = (us[0], *swap([after(u, in_send0) for u in us[1:]]))
    in_mine0, in_other0 = pair_share(in_keep0, in_send0)
    in_far0 = hop(in_other0, 2)

    order = (
        ((in_rows, in_piece, 0, 0, False),),
        ((vgo_rows, vgo_piece, in_piece, 0, True), (in_rows, in_piece, 0, in_rows, True)),
    )
    own0 = joined(order, in_mine0, in_far0, mine0, far0)
    pieces = lax.all_to_all(after(own0, summed1), "dp", 0, 0)
    first, rest = call(
        functools.partial(piece_sums, (in_piece, vgo_piece)),
        [Near(shape((count_dp, n, width), BF16)) for n in (in_piece, 2 * vgo_piece)],
        [],
        Near(pieces), Near(summed1),
    )
    result = [res[0], *swap([after(r, own0) for r in res[1:]])]
    (result,) = call(result_kernel, [shape((block, width))], [], res[0], *[Near(r) for r in result[1:]])
    full_in = lax.all_to_all(after(first, result, *us[1:]), "dp", 0, 0)
    stream_grad, gain_grad, shift_grad = call(
        functools.partial(last_kernel, tokens, in_piece),
        [shape((block, width)), shape((layers, width)), shape((layers, width))],
        [pltpu.VMEM((4,) + one_block, F32)],
        norms0, Near(full_in), Near(tile1), *[Near(u) for u in us], Raw(stream),
    )
    rest = after(rest, full_in)
    (input_grad,) = call(
        functools.partial(input_kernel, features, in_piece), [shape((layers, features, features))], [],
        Near(full_in), *[Near(x) for x in spread(full_in)],
    )
    full = lax.all_to_all(rest, "dp", 0, 0)
    full = after(full, input_grad, stream_grad)
    mat, vec, state = shape((layers, features, width)), shape((layers, width)), shape(decay_log.shape)
    o_grad, skip_grad, v_grad, g_grad, vb, gb, d_grad, p_grad, s_grad = call(
        functools.partial(hand_out, features, (in_piece, vgo_piece)),
        [mat, vec, mat, mat, vec, vec, state, state, state],
        [],
        decay_log, phase_log, Near(full_in), Near(full),
    )
    return (
        result, stream_grad, gain_grad, shift_grad, input_grad, d_grad, p_grad, s_grad,
        o_grad, skip_grad, v_grad, g_grad, vb, gb,
    )


def solution(mesh):
    split = P("dp", "mp")
    cols = P(None, "mp")
    wide = P(None, None, "mp")
    placed = (
        split, split, P("dp"), cols, cols, P(), P(), P(), P(), wide, cols, wide, wide, cols, cols,
    )
    return jax.shard_map(
        on_device,
        mesh=mesh,
        in_specs=placed,
        out_specs=(
            split, split, cols, cols, P(), P(), P(), P(), wide, cols, wide, wide, cols, cols,
        ),
        check_vma=False,
    )
```

```python
import functools

import jax
import jax.numpy as jnp
from jax import lax
from jax.experimental import pallas as pl
from jax.experimental.pallas import tpu as pltpu
from jax.sharding import PartitionSpec as P

epsilon = 1e-05
LANES = 128
SUB = 8
ROOT = 0.7978845608028654
CUBE = 0.044715
AXES = ("dp", "mp")
F32 = jnp.float32
BF16 = jnp.bfloat16
NT = (((1,), (1,)), ((), ()))
TN = (((0,), (0,)), ((), ()))
GAIN, SHIFT, SKIP, VBIAS, GBIAS = range(5)
PARAMS = 5


class Copies:
    def __init__(self, sems):
        self.sems, self.used, self.open = sems, 0, []

    def start(self, src, dst):
        copy = pltpu.make_async_copy(src, dst, self.sems.at[self.used])
        self.used += 1
        copy.start()
        return copy

    def flush(self, src, dst):
        self.open.append(self.start(src, dst))

    def finish(self):
        for copy in self.open:
            copy.wait()
        self.open = []


def along(ref, part, parts):
    if parts == 1:
        return ref
    axis = len(ref.shape) - 2
    size = ref.shape[axis] // parts
    at = pl.ds(part * size, size)
    return ref.at[at] if axis == 0 else ref.at[:, at]


class Arrival:
    def __init__(self, copies, src, dst, parts):
        self.copies, self.src, self.dst, self.parts = copies, src, dst, parts
        self.waits = [None] * parts

    def begin(self, part):
        src, dst = (along(r, part, self.parts) for r in (self.src, self.dst))
        self.waits[part] = self.copies.start(src, dst)

    def part(self, part):
        if self.waits[part] is not None:
            self.waits[part].wait()
            self.waits[part] = None
        return self.dst

    def __call__(self):
        for part in range(self.parts):
            self.part(part)
        return self.dst


class Result:
    def __init__(self, copies, ref, dst):
        self.copies, self.ref, self.dst, self.sent = copies, ref, dst, False

    def flush(self, part=0, parts=1):
        self.sent = True
        self.copies.flush(along(self.ref, part, parts), along(self.dst, part, parts))


class Raw:
    def __init__(self, array):
        self.array = array


class Halves:
    def __init__(self, array):
        self.array = array


class Near:
    def __init__(self, array):
        self.array = array


class Here:
    def __init__(self, ref):
        self.ref = self.dst = ref

    def part(self, part):
        return self.ref

    def __call__(self):
        return self.ref

    def flush(self, part=0, parts=1):
        pass


def call(body, outs, scratch, *args, scalars=0):
    wraps = (Raw, Halves, Near)
    plain = [a.array if isinstance(a, wraps) else a for a in args]
    out_shapes = [o.array if isinstance(o, wraps) else o for o in outs]
    autos = [i for i, a in enumerate(args) if i >= scalars and not isinstance(a, (Raw, Near))]
    made = [i for i, o in enumerate(outs) if not isinstance(o, (Raw, Near))]
    rooms = [pltpu.VMEM(plain[i].shape, plain[i].dtype) for i in autos]
    rooms += [pltpu.VMEM(out_shapes[i].shape, out_shapes[i].dtype) for i in made]

    def kernel(*refs):
        ins, refs = refs[: len(args)], refs[len(args) :]
        dsts, refs = refs[: len(outs)], refs[len(outs) :]
        sems, refs = refs[0], refs[1:]
        vin, refs = refs[: len(autos)], refs[len(autos) :]
        vout, rest = refs[: len(made)], refs[len(made) :]
        copies = Copies(sems)
        operands = [Here(r) if isinstance(a, Near) else r for a, r in zip(args, ins, strict=True)]
        for i, room in zip(autos, vin, strict=True):
            parts = 2 if isinstance(args[i], Halves) else 1
            operands[i] = Arrival(copies, ins[i], room, parts)
        results = [Here(r) if isinstance(o, Near) else r for o, r in zip(outs, dsts, strict=True)]
        for i, room in zip(made, vout, strict=True):
            results[i] = Result(copies, room, dsts[i])

        def begin(*some):
            for one in some or [operands[i] for i in autos]:
                operand, parts = one if isinstance(one, tuple) else (one, None)
                for part in range(operand.parts) if parts is None else (parts,):
                    operand.begin(part)

        body(copies, begin, *operands, *results, *rest)
        for r in results:
            if isinstance(r, Result) and not r.sent:
                r.flush()
        copies.finish()
        used.append(copies.used)

    near = pl.BlockSpec(memory_space=pltpu.VMEM)
    far = pl.BlockSpec(memory_space=pltpu.HBM)
    plain[scalars:] = [
        a if isinstance(w, Near) else pltpu.with_memory_space_constraint(a, pltpu.HBM)
        for w, a in zip(args[scalars:], plain[scalars:], strict=True)
    ]
    used = []

    def made_call(count):
        return pl.pallas_call(
            kernel,
            out_shape=[
                s if isinstance(o, Near) else pltpu.HBM(s.shape, s.dtype)
                for o, s in zip(outs, out_shapes, strict=True)
            ],
            in_specs=[pl.BlockSpec(memory_space=pltpu.SMEM)] * scalars
            + [near if isinstance(a, Near) else far for a in args[scalars:]],
            out_specs=[near if isinstance(o, Near) else far for o in outs],
            scratch_shapes=[pltpu.SemaphoreType.DMA((count,))] + rooms + list(scratch),
            compiler_params=pltpu.CompilerParams(vmem_limit_bytes=32 * 1024 * 1024),
        )

    jax.eval_shape(made_call(128), *plain)
    return made_call(max(used[0], 1))(*plain)


def cat(ref, rows):
    return jnp.concatenate([ref[j, rows, :] for j in range(ref.shape[0])], axis=1)


def put(ref, rows, val):
    for j in range(ref.shape[0]):
        ref[j, rows, :] = val[:, j * LANES : (j + 1) * LANES].astype(ref.dtype)


def rowcat(ref, r):
    return jnp.concatenate([ref[j, r : r + 1, :] for j in range(ref.shape[0])], axis=1)


def lanes(rows):
    return jnp.concatenate([rows[j : j + 1, :] for j in range(rows.shape[0])], axis=1)


def dot(a, b):
    return jnp.dot(a, b, preferred_element_type=F32)


def dot_nt(a, b):
    return lax.dot_general(a, b, NT, preferred_element_type=F32)


def dot_tn(a, b):
    return lax.dot_general(a, b, TN, preferred_element_type=F32)


def chunks(rows, count):
    size = rows // count
    return [slice(i * size, (i + 1) * size) for i in range(count)]


def sweep(src, dst, table, init, reset, reverse, conj):
    halves = src.shape[0] // 2
    span = src.shape[1] // SUB
    rate_re = [jnp.broadcast_to(table[h : h + 1, :], (SUB, LANES)) for h in range(halves)]
    rate_im = [
        jnp.broadcast_to(table[halves + h : halves + h + 1, :], (SUB, LANES))
        for h in range(halves)
    ]
    if conj:
        rate_im = [-r for r in rate_im]
    base = lax.broadcasted_iota(jnp.int32, (SUB, LANES), 0) * span - reset

    def body(step, state):
        j = span - 1 - step if reverse else step
        drop = base == -j
        at = pl.ds(j, SUB, stride=span)
        new_re, new_im = [], []
        for h in range(halves):
            a = jnp.where(drop, 0.0, rate_re[h])
            b = jnp.where(drop, 0.0, rate_im[h])
            re, im = state[h], state[halves + h]
            new_re.append((src[h, at, :] + a * re) - b * im)
            new_im.append((src[halves + h, at, :] + a * im) + b * re)
        state = tuple(new_re + new_im)
        if dst is not None:
            for k in range(2 * halves):
                dst[k, at, :] = state[k]
        return state

    return lax.fori_loop(0, span, body, init, unroll=8)


def zeros_state(halves):
    return tuple(jnp.zeros((SUB, LANES), F32) for _ in range(2 * halves))


def chain_segments(ends, first, table, reset, span, reverse, conj):
    halves = len(ends) // 2
    power_re = [table[4 + h : 5 + h, :] for h in range(halves)]
    power_im = [table[6 + h : 7 + h, :] for h in range(halves)]
    if conj:
        power_im = [-r for r in power_im]
    state = list(first)
    incoming = [[None] * SUB for _ in ends]
    order = range(SUB - 1, -1, -1) if reverse else range(SUB)
    for k in order:
        inside = (reset >= k * span) & (reset < (k + 1) * span)
        keep = jnp.where(inside, 0.0, 1.0)
        new = [None] * len(ends)
        for h in range(halves):
            re, im = state[h], state[halves + h]
            incoming[h][k], incoming[halves + h][k] = re, im
            new[h] = keep * (power_re[h] * re - power_im[h] * im) + ends[h][k : k + 1, :]
            new[halves + h] = (
                keep * (power_re[h] * im + power_im[h] * re) + ends[halves + h][k : k + 1, :]
            )
        state = new
    return [jnp.concatenate(rows, axis=0) for rows in incoming], state


def zero_rows(halves):
    return [jnp.zeros((1, LANES), F32) for _ in range(2 * halves)]


def emit_ends(out, ends_out, ends, table, reset, span, reverse, conj):
    halves = len(ends) // 2
    _, last = chain_segments(ends, zero_rows(halves), table, reset, span, reverse, conj)
    tile = jnp.concatenate(last, axis=0)
    out.ref[...] = jnp.broadcast_to(tile[None], out.ref.shape)
    out.flush()
    for k in range(2 * halves):
        ends_out.ref[k, :, :] = ends[k]
    ends_out.flush()


def carried_in(gathered, moments, table, me, reverse, conj):
    count = gathered.shape[0]
    power_re = table[8:10, :]
    power_im = table[10:12, :]
    if conj:
        power_im = -power_im
    flag = 3 if reverse else 2

    def body(i, state):
        d = count - 1 - i if reverse else i
        re, im = state
        keep = moments[d, flag : flag + 1, :]
        tile = gathered[d]
        return (
            keep * (power_re * re - power_im * im) + tile[0:2, :],
            keep * (power_re * im + power_im * re) + tile[2:4, :],
        )

    zero = jnp.zeros((2, LANES), F32)
    re, im = lax.fori_loop(0, count - 1 - me if reverse else me, body, (zero, zero))
    return [re[0:1, :], re[1:2, :], im[0:1, :], im[1:2, :]]


def place():
    mp = lax.axis_index("mp")
    return mp, lax.axis_index("dp") * lax.axis_size("mp") + mp


def local_resets(start, rows):
    offset = start[0]
    shift = jnp.where(offset > 0, offset - lax.axis_index("mp") * rows, -(1 << 20))
    return shift, shift - 1


def first_kernel(rows, copies, begin, start, stream, gain, shift, skip, vbias, gbias, decay, phase, scale,
                 moments, table_out, send1, send2, send3, held):
    mp, _ = place()
    total, width = held.shape
    parts = total // rows
    arrive = [copies.start(along(stream, i, parts), along(held, i, parts)) for i in range(parts)]
    begin()
    size = 128
    one = two = jnp.zeros((SUB, LANES), F32)

    def body(i, carry):
        one, two = carry
        x = held[pl.ds(i * size, size), :]
        for g in range(0, size, SUB):
            piece = x[g : g + SUB, :]
            one = one + piece
            two = two + piece * piece
        return one, two

    for i in range(parts):
        arrive[i].wait()
        one, two = lax.fori_loop(i * rows // size, (i + 1) * rows // size, body, (one, two))
    fwd, bwd = local_resets(start, rows)
    keep_f = jnp.where((fwd >= 0) & (fwd < rows), 0.0, 1.0)
    keep_b = jnp.where((bwd >= 0) & (bwd < rows), 0.0, 1.0)
    tile = jnp.concatenate(
        [
            jnp.sum(one, axis=0, keepdims=True),
            jnp.sum(two, axis=0, keepdims=True),
            jnp.full((1, LANES), keep_f, F32),
            jnp.full((1, LANES), keep_b, F32),
        ],
        axis=0,
    )
    moments.ref[...] = jnp.broadcast_to(tile[None], moments.ref.shape)
    moments.flush()
    gain, shift, skip, vbias, gbias = (a() for a in (gain, shift, skip, vbias, gbias))
    decay, phase, scale = decay(), phase(), scale()
    layers = decay.shape[0]
    plist = jnp.concatenate(
        [a[l : l + 1, :] for l in range(layers) for a in (gain, shift, skip, vbias, gbias)]
        + [jnp.zeros((16 - PARAMS * layers, width), F32)],
        axis=0,
    )
    high = plist.astype(BF16)
    rest = (plist - high.astype(F32)).astype(BF16)
    for k, send in ((1, send1), (2, send2), (3, send3)):
        base = (mp ^ k) * rows
        send.ref[0:rows, :] = held[pl.ds(pl.multiple_of(base, SUB), rows), :].astype(BF16)
        send.ref[rows : rows + 16, :] = high
        send.ref[rows + 16 : rows + 32, :] = rest
        send.flush()
    span = rows // SUB
    table = table_out.ref
    for layer in range(layers):
        for h in range(2):
            cols = slice(h * LANES, (h + 1) * LANES)
            radius = jnp.exp(-jnp.exp(decay[layer : layer + 1, cols]))
            angle = jnp.exp(phase[layer : layer + 1, cols])
            re, im = radius * jnp.cos(angle), radius * jnp.sin(angle)
            table[layer, h : h + 1, :] = re
            table[layer, 2 + h : 3 + h, :] = im
            length = 1
            while length < rows:
                re, im = re * re - im * im, 2.0 * re * im
                length *= 2
                if length == span:
                    table[layer, 4 + h : 5 + h, :] = re
                    table[layer, 6 + h : 7 + h, :] = im
            table[layer, 8 + h : 9 + h, :] = re
            table[layer, 10 + h : 11 + h, :] = im
            table[layer, 12 + h : 13 + h, :] = jnp.exp(scale[layer : layer + 1, cols])
            table[layer, 14 + h : 15 + h, :] = jnp.zeros((1, LANES), F32)


def pack_maps(layers, copies, begin, c_own, v_own, g_own, weight, *packs):
    begin()
    *packs, near = packs
    copies.flush(weight.at[0], near.ref)
    for layer in range(layers):
        for i, own in enumerate((c_own, v_own, g_own)):
            deep = own().shape[1]
            packs[layer].ref[i * deep : (i + 1) * deep, :] = own()[layer]
        packs[layer].flush()


def pack_block(copies, begin, x, weight, near, *sends):
    mp, _ = place()
    rows = sends[0].ref.shape[0]
    begin()
    copies.flush(weight.at[1], near.ref)
    whole = x()
    for k, send in enumerate(sends):
        base = pl.multiple_of((mp ^ (k + 1)) * rows, SUB)
        send.ref[...] = whole[pl.ds(base, rows), :].astype(BF16)
        send.flush()


def gather_block(copies, begin, got1, got2, got3, gain, shift, skip, vbias, gbias, stream, h, prm, held):
    mp, _ = place()
    rows = h.ref.shape[1]
    own = Later(copies, [(own_rows(stream, rows), held)], held)
    begin()
    plist = [a() for a in (gain, shift, skip, vbias, gbias)]
    layers = plist[0].shape[0]
    for k, got in ((1, got1), (2, got2), (3, got3)):
        got = got()
        h.ref[mp ^ k, :, :] = got[0:rows, :].astype(F32)
        pair = got[rows : rows + 16, :].astype(F32) + got[rows + 16 : rows + 32, :].astype(F32)
        prm.ref[mp ^ k, :, :] = pair
    mine = [a[l : l + 1, :] for l in range(layers) for a in plist]
    prm.ref[mp, 0 : PARAMS * layers, :] = jnp.concatenate(mine, axis=0)
    prm.ref[mp, PARAMS * layers :, :] = jnp.zeros((16 - PARAMS * layers, LANES), F32)
    h.ref[mp, :, :] = own()[...]


def norm_rows(mean, second, gain, shift):
    inverse = lax.rsqrt(second - mean * mean + epsilon)
    factor = inverse * gain
    return inverse, factor, shift - mean * factor


def drive_body(layer, mean, second, start, h, prm, table, weight, drive, norms, out, ends_out, slow):
    rows = drive.ref.shape[1]
    reverse = layer % 2 == 1
    base = layer * PARAMS
    inverse, factor, bias = norm_rows(
        mean, second, rowcat(prm, base + GAIN), rowcat(prm, base + SHIFT)
    )
    norms.ref[...] = jnp.concatenate(
        [factor, bias, inverse, mean] + [jnp.zeros_like(mean)] * 4, axis=0
    )
    norms.flush()
    gamma = lanes(table[layer, 12:14, :])
    gamma = jnp.concatenate([gamma, gamma], axis=1)
    for i, at in enumerate(chunks(rows, 2)):
        low = (cat(h, at) * factor + bias).astype(BF16)
        slow.ref[at, :] = low
        slow.flush(i, 2)
        put(drive.ref, at, dot(low, weight()[...]) * gamma)
        drive.flush(i, 2)
    fwd, bwd = local_resets(start, rows)
    reset = bwd if reverse else fwd
    ends = sweep(drive.ref, None, table[layer], zeros_state(2), reset, reverse, False)
    emit_ends(out, ends_out, ends, table[layer], reset, rows // SUB, reverse, False)


class Later:
    def __init__(self, copies, pairs, dst):
        self.waits, self.dst = [copies.start(src, to) for src, to in pairs], dst

    def __call__(self):
        for copy in self.waits:
            copy.wait()
        self.waits = []
        return self.dst


def own_rows(ref, rows, k=0):
    mp, _ = place()
    return ref.at[pl.ds(pl.multiple_of((mp ^ k) * rows, SUB), rows)]


def total_of(gathered):
    tile = gathered[0]
    for d in range(1, gathered.shape[0]):
        tile = tile + gathered[d]
    return tile


def drive_first(total_tokens, copies, begin, start, mom, table, h, prm, weight, drive, norms, out, ends, slow):
    mom = mom()
    groups = h.ref.shape[0]
    sums = [mom[j, 0:2, :] for j in range(groups)]
    for d in range(groups, mom.shape[0]):
        sums[d % groups] = sums[d % groups] + mom[d, 0:2, :]
    both = jnp.concatenate(sums, axis=1) * (1.0 / total_tokens)
    drive_body(0, both[0:1, :], both[1:2, :], start, h(), prm(), table(), weight, drive, norms, out, ends, slow)


def drive_next(layer, total_tokens, copies, begin, start, mom, prm, table, h, weight, drive, norms, out, ends, slow):
    tile = total_of(mom()) * (1.0 / total_tokens)
    half = tile.shape[0] // 2
    mean, second = lanes(tile[:half]), lanes(tile[half:])
    drive_body(layer, mean, second, start, h(), prm(), table(), weight, drive, norms, out, ends, slow)


def resume(start, rows, gathered, mom, tab, ends, reverse, conj):
    fwd, bwd = local_resets(start, rows)
    reset = bwd if reverse else fwd
    first = carried_in(gathered, mom, tab, place()[1], reverse, conj)
    incoming, _ = chain_segments(
        [ends[k] for k in range(4)], first, tab, reset, rows // SUB, reverse, conj
    )
    return tuple(incoming), reset


def assemble(copies, begin, p0, p1, p2, p3, maps):
    begin()
    mp, _ = place()
    count, deep = maps.ref.shape[0], maps.ref.shape[1]
    for k, piece in enumerate((p0, p1, p2, p3)):
        cols = pl.ds(pl.multiple_of((mp ^ k) * LANES, LANES), LANES)
        for i in range(count):
            maps.ref[i, :, cols] = piece()[i * deep : (i + 1) * deep, :]


def gather_cotangent(copies, begin, got1, got2, got3, cot, full):
    begin()
    mp, _ = place()
    rows = full.ref.shape[0]
    own = cot()[pl.ds(pl.multiple_of(mp * rows, SUB), rows), :].astype(BF16)
    for k, block in enumerate((own, got1()[...], got2()[...], got3()[...])):
        full.ref[:, pl.ds(pl.multiple_of((mp ^ k) * LANES, LANES), LANES)] = block


def fetch_maps(copies, far, near, order=(0, 1, 2)):
    return {i: Later(copies, [(far.at[i], near.at[i])], near.at[i]) for i in order}


def mix_chunk(layer, at, h, norms, states, maps, prm):
    base = layer * PARAMS
    x = cat(h, at)
    scaled = x * norms[0:1, :] + norms[1:2, :]
    states_low = cat(states, at).astype(BF16)
    mixed = dot(states_low, maps[0]()[...]) + rowcat(prm, base + SKIP) * scaled
    square = mixed * mixed
    wave = jnp.tanh(ROOT * mixed * (1.0 + CUBE * square))
    half = 0.5 * (1.0 + wave)
    sent_low = (mixed * half).astype(BF16)
    slope = half + 0.5 * mixed * (1.0 - wave * wave) * (ROOT * (1.0 + 3.0 * CUBE * square))
    value = dot(sent_low, maps[1]()[...]) + rowcat(prm, base + VBIAS)
    gate = dot(sent_low, maps[2]()[...]) + rowcat(prm, base + GBIAS)
    sig = 0.5 + 0.5 * jnp.tanh(0.5 * gate)
    gated = value * sig
    return x, scaled, states_low, sent_low, slope, sig, gated


def back_chunk(i, at, g, sig, gain_part, scaled, slope, maps, outs, sums):
    dv, dg, dml, ds = outs
    dvalue = g * sig
    dgate = g * gain_part
    dv_low, dg_low = dvalue.astype(BF16), dgate.astype(BF16)
    dmixed = (dot_nt(dv_low, maps[1]()[...]) + dot_nt(dg_low, maps[2]()[...])) * slope()
    dm_low = dmixed.astype(BF16)
    put(ds.ref, at, dot_nt(dm_low, maps[0]()[...]))
    dv.ref[at, :] = dv_low
    dg.ref[at, :] = dg_low
    dml.ref[at, :] = dm_low
    for o in outs:
        o.flush(i, 2)
    add = lambda v: jnp.sum(v, axis=0, keepdims=True)
    return [
        s + n for s, n in zip(sums, [add(dvalue), add(dgate), add(dmixed * scaled())], strict=True)
    ]


def sums_rows(sums_out, sums):
    rows = sums + [jnp.zeros_like(sums[0])] * (8 - len(sums))
    sums_out.ref[...] = jnp.concatenate(rows, axis=0)
    sums_out.flush()


def share_out(keep, send, pack, copies):
    mp, _ = place()
    for ref, i, k in ((send, 0, 1), (send, 1, 3), (keep, 0, 0), (keep, 1, 2)):
        ref.ref[i, :, :] = pack[mp ^ k, :, :]


def weight_share(sent, dv, dg, states, dml, sums, pack):
    width = sent.dst.shape[1]
    parts = pack.shape[0]
    both = jnp.concatenate([dv()[...], dg()[...]], axis=1)
    both = dot_tn(sent()[...], both)
    put(pack, slice(0, width), both[:, :width])
    put(pack, slice(width, 2 * width), both[:, width:])
    put(pack, slice(2 * width, 3 * width), dot_tn(states()[...], dml()[...]))
    sums = sums()
    for j in range(parts):
        cols = slice(j * LANES, (j + 1) * LANES)
        rows = jnp.concatenate([sums[:, cols], jnp.zeros((8, LANES), F32)], axis=0)
        pack[j, 3 * width : 3 * width + 16, :] = rows.astype(pack.dtype)


def weight_grads(copies, begin, sent, dv, dg, states, dml, sums, keep, send, pack):
    begin()
    weight_share(sent, dv, dg, states, dml, sums, pack)
    share_out(keep, send, pack, copies)


def input_share(base, copies, slow, dlow, prods, weight, pack, held, sums=None):
    width = slow.dst.shape[1]
    held[...] = dot_tn(slow()[...], dlow()[...])
    half = width // 2
    y_re = y_im = jnp.zeros((1, half), F32)
    size = 64
    for top in range(0, width, size):
        rows = slice(top, top + size)
        grad = held[rows, :]
        put(pack, slice(base + top, base + top + size), grad)
        grad_re, grad_im = grad[:, :half], grad[:, half:]
        w = weight()[rows, :].astype(F32)
        w_re, w_im = w[:, :half], w[:, half:]
        y_re = y_re + jnp.sum(grad_re * w_re + grad_im * w_im, axis=0, keepdims=True)
        y_im = y_im + jnp.sum(grad_im * w_re - grad_re * w_im, axis=0, keepdims=True)
    prods = prods()
    rows = []
    for h in range(2):
        cols = slice(h * LANES, (h + 1) * LANES)
        rows += [prods[2 * h : 2 * h + 1, :] - y_re[:, cols], prods[2 * h + 1 : 2 * h + 2, :] - y_im[:, cols]]
        rows += [y_re[:, cols]]
    for j in range(pack.shape[0]):
        cols = slice(j * LANES, (j + 1) * LANES)
        more = [] if sums is None else [sums()[0:2, cols]]
        tile = rows + more + [jnp.zeros((10 - 2 * len(more), LANES), F32)]
        pack[j, base + width : base + width + 16, :] = jnp.concatenate(tile, axis=0).astype(pack.dtype)


def input_grads(layer, copies, begin, slow, dlow, prods, sums, weight, keep, send, pack, held, maps):
    begin()
    weight = Later(copies, [(weight.at[layer], maps)], maps)
    input_share(0, copies, slow, dlow, prods, weight, pack, held, sums)
    share_out(keep, send, pack, copies)


def both_grads(layer, copies, begin, sent, dv, dg, states, dml, sums, slow, dlow, prods, weight, keep, send,
               pack, held, maps):
    begin()
    weight = Later(copies, [(weight.at[layer + 1], maps)], maps)
    weight_share(sent, dv, dg, states, dml, sums, pack)
    input_share(3 * sent.dst.shape[1] + 16, copies, slow, dlow, prods, weight, pack, held)
    share_out(keep, send, pack, copies)


def add_chunk(mom, one, two):
    tile = jnp.concatenate(
        [one[:, j * LANES : (j + 1) * LANES] for j in range(one.shape[1] // LANES)]
        + [two[:, j * LANES : (j + 1) * LANES] for j in range(two.shape[1] // LANES)],
        axis=0,
    )
    mom.ref[...] = jnp.broadcast_to(tile[None], mom.ref.shape)
    mom.flush()


def mix_first(layer, copies, begin, start, gathered, mom, table, ends, norms, prm, drive, h, far_maps,
              new_h, new_mom, h_far, states_low_out, sent, slope_out, sig_out, part_out, states, maps):
    rows = states.shape[1]
    ready = fetch_maps(copies, far_maps, maps)
    copies.flush(h.ref, h_far)
    reverse = layer % 2 == 1
    tab = table()[layer]
    init, reset = resume(start, rows, gathered(), mom(), tab, ends(), reverse, False)
    sweep(drive(), states, tab, init, reset, reverse, False)
    norms, prm = norms(), prm()
    one = two = 0.0
    for i, at in enumerate(chunks(rows, 2)):
        x, scaled, states_low, sent_low, slope, sig, gated = mix_chunk(
            layer, at, h(), norms, states, ready, prm
        )
        states_low_out.ref[at, :] = states_low
        sent.ref[at, :] = sent_low
        slope_out.ref[at, :] = slope.astype(BF16)
        sig_out.ref[at, :] = sig.astype(BF16)
        part_out.ref[at, :] = (gated * (1.0 - sig)).astype(BF16)
        new = x + gated
        put(new_h.ref, at, new)
        one = one + jnp.sum(new, axis=0, keepdims=True)
        two = two + jnp.sum(new * new, axis=0, keepdims=True)
        for o in (states_low_out, sent, slope_out, sig_out, part_out):
            o.flush(i, 2)
    add_chunk(new_mom, one, two)


def turn(layer, copies, begin, start, gathered, mom, table, ends, norms, prm, drive, h, far_maps, cot,
         ds, out, ends_out, h_far, states_low_out, sent, dv, dg, dml, sums_out, r0, r1, r2, r3,
         maps, states, new_h):
    mp, _ = place()
    rows = states.shape[1]
    ready = fetch_maps(copies, far_maps, maps)
    begin()
    copies.flush(h.ref, h_far)
    reverse = layer % 2 == 1
    tab = table()[layer]
    init, reset = resume(start, rows, gathered(), mom(), tab, ends(), reverse, False)
    sweep(drive(), states, tab, init, reset, reverse, False)
    norms, prm = norms(), prm()
    sums = [0.0, 0.0, 0.0]
    for i, at in enumerate(chunks(rows, 2)):
        x, scaled, states_low, sent_low, slope, sig, gated = mix_chunk(
            layer, at, h(), norms, states, ready, prm
        )
        states_low_out.ref[at, :] = states_low
        sent.ref[at, :] = sent_low
        put(new_h, at, x + gated)
        g = cot.part(i)[at, :].astype(F32)
        for o in (states_low_out, sent):
            o.flush(i, 2)
        sums = back_chunk(i, at, g, sig, gated * (1.0 - sig), lambda: scaled, lambda: slope,
                          ready, (dv, dg, dml, ds), sums)
    sums_rows(sums_out, sums)
    for k, r in enumerate((r0, r1, r2, r3)):
        r.ref[...] = new_h[mp ^ k, :, :].astype(r.ref.dtype)
        r.flush()
    adjoint_start(layer, start, tab, ds.ref, out, ends_out)


def adjoint_start(layer, start, tab, ds, out, ends_out):
    rows = ds.shape[1]
    reverse = layer % 2 == 0
    fwd, bwd = local_resets(start, rows)
    reset = bwd if reverse else fwd
    ends = sweep(ds, None, tab, zeros_state(2), reset, reverse, True)
    emit_ends(out, ends_out, ends, tab, reset, rows // SUB, reverse, True)


def back_first(layer, total_tokens, copies, begin, start, back, norms1, table, prm, u, norms,
               slow1, sig, part, slope, slow, far_maps, g_out, ds, out, ends_out, tile_out, dv, dg, dml, sums_out,
               maps):
    begin((slow1, 0), (sig, 0), (part, 0))
    ready = fetch_maps(copies, far_maps, maps, (1, 2))
    rows = ds.ref.shape[1]
    tile = total_of(back())
    tile_out.ref[...] = tile
    norms1, norms, prm = norms1(), norms(), prm()
    half = tile.shape[0] // 2
    base = (layer + 1) * PARAMS
    over = 1.0 / rowcat(prm, base + GAIN)
    shift = rowcat(prm, base + SHIFT)
    factor = norms1[0:1, :] * (1.0 / total_tokens)
    m_one, m_two = factor * lanes(tile[:half]), factor * over * lanes(tile[half:])
    m_one = m_one - shift * m_two
    sums = [0.0, 0.0, 0.0]
    for i, at in enumerate(chunks(rows, 2)):
        g = cat(u(), at) - m_one - slow1.part(i)[at, :].astype(F32) * m_two
        if i == 0:
            begin((slope, 0))
            ready.update(fetch_maps(copies, far_maps, maps, (0,)))
            begin((slow, 0), (slow1, 1), (sig, 1), (part, 1), (slope, 1), (slow, 1))
        put(g_out.ref, at, g)
        g_out.flush(i, 2)
        low = lambda x: x.part(i)[at, :].astype(F32)
        sums = back_chunk(i, at, g, low(sig), low(part), lambda: low(slow), lambda: low(slope),
                          ready, (dv, dg, dml, ds), sums)
    sums_rows(sums_out, sums)
    adjoint_start(layer, start, table()[layer], ds.ref, out, ends_out)


def back_second(layer, copies, begin, start, gathered, mom, table, ends, norms, prm, ds, states_low, g, dml, h,
                weight, *refs):
    if layer == 0:
        back, prods, dlow, u0, u1, u2, u3, adj, maps, u_ref = refs
    else:
        back, u_out, prods, dlow, adj, maps = refs
        u_ref = u_out.ref
        begin(g)
    begin(states_low)
    weight = Later(copies, [(weight.at[layer], maps)], maps)
    begin((dml, 0), (h, 0))
    if layer == 0:
        begin((g, 0), (g, 1))
    begin((dml, 1), (h, 1))
    rows = adj.shape[1]
    reverse = layer % 2 == 0
    tab = table()[layer]
    init, reset = resume(start, rows, gathered(), mom(), tab, ends(), reverse, True)
    sweep(ds(), adj, tab, init, reset, reverse, True)
    half = adj.shape[0] // 2 * LANES
    prod_re = prod_im = jnp.zeros((SUB, half), F32)
    for at in chunks(rows, 16):
        a, s = cat(adj, at), states_low()[at, :].astype(F32)
        a_re, a_im, s_re, s_im = a[:, :half], a[:, half:], s[:, :half], s[:, half:]
        re, im = a_re * s_re + a_im * s_im, a_im * s_re - a_re * s_im
        for top in range(0, re.shape[0], SUB):
            prod_re = prod_re + re[top : top + SUB, :]
            prod_im = prod_im + im[top : top + SUB, :]
    flat = [jnp.sum(x, axis=0, keepdims=True) for x in (prod_re, prod_im)]
    flat = [x[:, h_ * LANES : (h_ + 1) * LANES] for h_ in range(2) for x in flat]
    prods.ref[...] = jnp.concatenate(flat + [jnp.zeros((8 - len(flat), LANES), F32)], axis=0)
    prods.flush()
    gamma = lanes(tab[12:14, :])
    gamma = jnp.concatenate([gamma, gamma], axis=1)
    base = layer * PARAMS
    prm, norms = prm(), norms()
    skip = rowcat(prm, base + SKIP)
    factor, bias, inverse, mean = (norms[i : i + 1, :] for i in range(4))
    one = two = 0.0
    for i, at in enumerate(chunks(rows, 2)):
        dlow.ref[at, :] = (cat(adj, at) * gamma).astype(BF16)
        dlow.flush(i, 2)
    for i, at in enumerate(chunks(rows, 2)):
        dscaled = dot_nt(dlow.ref[at, :], weight()[...]) + dml.part(i)[at, :].astype(F32) * skip
        normed = (cat(h.part(i), at) - mean) * inverse
        own = g()[at, :].astype(F32) if layer == 1 else cat(g.part(i), at)
        put(u_ref, at, own + factor * dscaled)
        one = one + jnp.sum(dscaled, axis=0, keepdims=True)
        two = two + jnp.sum(dscaled * normed, axis=0, keepdims=True)
    if layer == 0:
        back.ref[...] = jnp.concatenate([one, two] + [jnp.zeros_like(one)] * 6, axis=0)
        mp, _ = place()
        for k, piece in enumerate((u0, u1, u2, u3)):
            piece.ref[...] = u_ref[mp ^ k, :, :].astype(piece.ref.dtype)
            piece.flush()
    else:
        add_chunk(back, one, two)


def result_kernel(copies, begin, r0, r1, r2, r3, result):
    begin()
    mp, _ = place()
    rows = r0.dst.shape[0]
    for k, r in ((1, r1), (2, r2), (3, r3), (0, r0)):
        at = pl.ds(pl.multiple_of((mp ^ k) * rows, SUB), rows)
        result.ref[at, :] = r()[...].astype(F32)
        copies.flush(result.ref.at[at], result.dst.at[at])
    result.sent = True


def last_kernel(total_tokens, in_piece, copies, begin, norms, back, tile1, u0, u1, u2, u3, stream,
                out, gain_out, shift_out, held):
    begin()
    mp, _ = place()
    rows = u0.dst.shape[0]
    streams = [Later(copies, [(own_rows(stream, rows, k), held.at[k])], held.at[k]) for k in range(4)]
    tile1, norms = tile1(), norms()
    width = norms.shape[1]
    ((_, _, sums),) = unpieced(back(), 0, in_piece, width, 16)
    sums = sums.astype(F32)
    one, two = sums[6:7, :], sums[7:8, :]
    half = tile1.shape[0] // 2
    zero = jnp.zeros((1, LANES), F32)
    factor, inverse, mean, later_one, later_two = [zero] * 5
    for j in range(half):
        mine = jnp.where(mp == j, 1.0, 0.0)
        cols = slice(j * LANES, (j + 1) * LANES)
        later_one = later_one + mine * tile1[j : j + 1, :]
        later_two = later_two + mine * tile1[half + j : half + j + 1, :]
        factor = factor + mine * norms[0:1, cols]
        inverse = inverse + mine * norms[2:3, cols]
        mean = mean + mine * norms[3:4, cols]
    scaled = factor * (1.0 / total_tokens)
    m_one, m_two = scaled * one, scaled * two
    for k, u in enumerate((u0, u1, u2, u3)):
        at = pl.ds(pl.multiple_of((mp ^ k) * rows, SUB), rows)
        normed = (streams[k]()[...] - mean) * inverse
        out.ref[at, :] = u()[...].astype(F32) - m_one - normed * m_two
        copies.flush(out.ref.at[at], out.dst.at[at])
    out.sent = True
    gain_out.ref[...] = jnp.concatenate([two, later_two], axis=0)
    shift_out.ref[...] = jnp.concatenate([one, later_one], axis=0)


def pair_sum(copies, begin, keep, got, mine, other):
    keep, got = keep(), got()
    size = keep.shape[1]
    for at in chunks(size, size // 16):
        other.ref[at, :] = (keep[1, at, :].astype(F32) + got[1, at, :].astype(F32)).astype(other.ref.dtype)
        mine.ref[at, :] = (keep[0, at, :].astype(F32) + got[0, at, :].astype(F32)).astype(mine.ref.dtype)


def four_sum(order, copies, begin, *refs):
    *ins, out = refs
    out = out.ref
    for mine, got, spans in zip(ins[::2], ins[1::2], order, strict=True):
        mine, got = mine(), got()
        row = 0
        for rows, size, base, first, last in spans:
            for i in range(0, out.shape[0] * size - first if last else rows, 16):
                d, top = (first + i) // size, base + (first + i) % size
                if i < rows:
                    at = slice(row + i, row + i + 16)
                    total = (mine[at, :].astype(F32) + got[at, :].astype(F32)).astype(out.dtype)
                else:
                    total = jnp.zeros((16, out.shape[2]), out.dtype)
                out[d, top : top + 16, :] = total
            row += rows


def piece_total(pieces, at):
    total = pieces[0, at, :].astype(F32)
    for d in range(1, pieces.shape[0]):
        total = total + pieces[d, at, :].astype(F32)
    return total.astype(BF16)


def piece_sum(copies, begin, pieces, out):
    for at in chunks(out.ref.shape[0], out.ref.shape[0] // 16):
        out.ref[at, :] = piece_total(pieces(), at)


def piece_sums(sizes, copies, begin, pieces, other, first, rest):
    in_piece, vgo_piece = sizes
    rows = pieces().shape[1]
    for at in chunks(rows, rows // 16):
        low = piece_total(pieces(), at)
        inputs = at.start < in_piece
        out, top = (first.ref, at.start) if inputs else (rest.ref, at.start - in_piece)
        for d in range(out.shape[0]):
            out[d, top : top + 16, :] = low
    for at in chunks(vgo_piece, vgo_piece // 16):
        low = other()[at, :]
        for d in range(rest.ref.shape[0]):
            rest.ref[d, vgo_piece + at.start : vgo_piece + at.stop, :] = low


def unpieced(pieces, offset, size, first, rows):
    at = first
    while at < first + rows:
        piece, inside = at // size, at % size
        count = min(size - inside, first + rows - at)
        yield at - first, count, pieces[piece, offset + inside : offset + inside + count, :]
        at += count


def hand_out(features, sizes, copies, begin, decay, phase, full_in, full,
             o_grad, skip_grad, v_grad, g_grad, vb, gb, d_grad, p_grad, s_grad):
    begin()
    full, full_in = full(), full_in()
    in_piece, vgo_piece = sizes
    in_rows = features + 16
    for layer in range(2):
        base = layer * vgo_piece
        for i, out in enumerate((v_grad, g_grad, o_grad)):
            for at, count, rows in unpieced(full, base, vgo_piece, i * features, features):
                out.ref[layer, at : at + count, :] = rows.astype(F32)
            copies.flush(out.ref.at[layer], out.dst.at[layer])
            out.sent = True
    decay, phase = decay(), phase()
    for layer in range(2):
        base = layer * vgo_piece
        row = slice(layer, layer + 1)
        ((_, _, vecs),) = unpieced(full, base, vgo_piece, 3 * features, 16)
        vecs = vecs.astype(F32)
        vb.ref[row, :] = vecs[0:1, :]
        gb.ref[row, :] = vecs[1:2, :]
        skip_grad.ref[row, :] = vecs[2:3, :]
        ((_, _, tile),) = unpieced(full_in, 0, in_piece, layer * in_rows + features, 16)
        tile = tile.astype(F32)
        for h in range(2):
            cols = slice(h * LANES, (h + 1) * LANES)
            d_grad.ref[row, cols] = -jnp.exp(decay[row, cols]) * tile[3 * h : 3 * h + 1, :]
            p_grad.ref[row, cols] = jnp.exp(phase[row, cols]) * tile[3 * h + 1 : 3 * h + 2, :]
            s_grad.ref[row, cols] = tile[3 * h + 2 : 3 * h + 3, :]


def input_kernel(features, size, copies, begin, p0, p1, p2, p3, out):
    begin()
    mp, _ = place()
    for k, pieces in enumerate((p0, p1, p2, p3)):
        cols = pl.ds(pl.multiple_of((mp ^ k) * LANES, LANES), LANES)
        for layer in range(out.ref.shape[0]):
            for at, count, rows in unpieced(pieces(), 0, size, layer * (features + 16), features):
                out.ref[layer, at : at + count, cols] = rows.astype(F32)


def shape(dims, dtype=F32):
    return jax.ShapeDtypeStruct(tuple(dims), dtype)


def every(x):
    return lax.all_to_all(x, AXES, 0, 0)


def hop(x, k):
    count = lax.axis_size("mp")
    return lax.ppermute(x, "mp", [(i, i ^ k) for i in range(count)])


def spread(x, then=None):
    far = hop(x, 2)
    held = far if then is None else after(far, then)
    return hop(x, 1), far, hop(held, 1)


def swap(sends):
    return [hop(x, k + 1) for k, x in enumerate(sends)]


def after(x, *ys):
    return lax.optimization_barrier((x, *ys))[0]


def on_device(
    stream,
    cotangent,
    start_offsets,
    norm_gain,
    norm_shift,
    input_map,
    decay_log,
    phase_log,
    scale_log,
    output_map,
    skip_gain,
    value_weight,
    gate_weight,
    value_bias,
    gate_bias,
):
    block, width = stream.shape
    layers = input_map.shape[0]
    count_dp, parts = lax.axis_size("dp"), lax.axis_size("mp")
    devices = count_dp * parts
    tokens = block * count_dp
    rows = block // parts
    features = width * parts
    assert width == LANES and features == 4 * LANES and layers == 2 and parts == 4

    plist = (norm_gain, norm_shift, skip_gain, value_bias, gate_bias)
    blocks = shape((parts, rows, width))
    v_blocks = pltpu.VMEM(blocks.shape, F32)
    one_block = (rows, width)
    low_block = shape(one_block, BF16)
    wide_low = shape((rows, features), BF16)
    near_blocks = Near(blocks)
    near_ends = Near(shape((4, SUB, LANES)))
    near_every = Near(shape((devices, 4, LANES)))
    near_sums = Near(shape((devices, 2 * parts, LANES)))
    near_norms = Near(shape((8, features)))
    near_low = Near(low_block)
    packed_w = shape((3 * features, width), BF16)
    one_map = pltpu.VMEM((features, features), BF16)
    maps = pltpu.VMEM((3, features, features), BF16)
    all_maps = shape((3, features, features), BF16)
    near_map = Near(shape((features, features), BF16))

    mom_out, table, *sends = call(
        functools.partial(first_kernel, rows),
        [near_every, Near(shape((layers, 16, LANES)))] + [Near(shape((rows + 32, width), BF16))] * 3,
        [pltpu.VMEM((block, width), F32)],
        start_offsets, Raw(stream), *plist, decay_log, phase_log, scale_log,
        scalars=1,
    )
    table = Near(table)
    got_h = [Near(x) for x in swap(sends)]
    mom0 = every(after(mom_out, got_h[0].array, got_h[1].array))
    h0, prm = call(
        gather_block,
        [near_blocks, Near(shape((parts, 16, width)))],
        [pltpu.VMEM(one_block, F32)],
        *got_h, *plist, Raw(stream),
    )
    h0, prm, mom0 = Near(h0), Near(prm), Near(after(mom0, h0))
    *packs, near_in = call(
        functools.partial(pack_maps, layers), [packed_w] * layers + [near_map], [],
        output_map, value_weight, gate_weight, Raw(input_map),
    )
    w0 = after(packs[0], got_h[1].array, got_h[2].array)
    (full0,) = call(assemble, [all_maps], [], w0, *[Near(w) for w in spread(w0, mom0.array)])

    drive0, norms0, ends_all, ends0, slow0 = call(
        functools.partial(drive_first, tokens),
        [near_blocks, near_norms, near_every, near_ends, wide_low],
        [],
        start_offsets, mom0, table, h0, prm, Near(near_in),
        scalars=1,
    )
    got = Near(after(every(ends_all), full0))
    norms0 = Near(norms0)
    h1, mom_out, h0, states0, sent0, slope0, sig0, part0 = call(
        functools.partial(mix_first, 0),
        [near_blocks, near_sums, Raw(blocks)] + [wide_low] * 5,
        [v_blocks, maps],
        start_offsets, got, mom0, table, Near(ends0), norms0, prm, Near(drive0), h0, Raw(full0),
        scalars=1,
    )
    h1 = Near(h1)
    near_in, *sends = call(
        pack_block, [near_map] + [low_block] * 3, [], after(cotangent, got.array), Raw(input_map)
    )
    mom1 = Near(after(every(mom_out), *sends))
    w1 = after(packs[1], got.array)
    (full1,) = call(assemble, [all_maps], [], w1, *[Near(w) for w in spread(w1, mom1.array)])
    drive1, norms1, ends_all, ends1, slow1 = call(
        functools.partial(drive_next, 1, tokens),
        [near_blocks, near_norms, near_every, near_ends, wide_low],
        [],
        start_offsets, mom1, prm, table, h1, Near(near_in),
        scalars=1,
    )
    got_cot = [Near(x) for x in swap([after(s, norms1) for s in sends])]
    (cot,) = call(gather_cotangent, [wide_low], [], *got_cot, after(cotangent, full1))
    got = Near(after(every(ends_all), full1, cot))
    norms1 = Near(norms1)
    vgo_rows, in_rows = 3 * features + 16, features + 16

    def pair_share(keep, send):
        size = Near(shape(keep.shape[1:], BF16))
        return call(pair_sum, [size, size], [], Near(keep), Near(hop(send, 1)))

    vgo_half = Near(shape((2, vgo_rows, width), BF16))
    in_half = Near(shape((2, in_rows, width), BF16))
    vgo_pack = pltpu.VMEM((parts, vgo_rows, width), BF16)
    both_half = Near(shape((2, vgo_rows + in_rows, width), BF16))
    both_pack = pltpu.VMEM((parts, vgo_rows + in_rows, width), BF16)
    in_pack = pltpu.VMEM((parts, in_rows, width), BF16)
    in_room = [in_pack, pltpu.VMEM((features, features), F32), one_map]
    ds1, ends_all, back_ends1, h1, states1, sent1, dv, dg, dml1, sums, *res = call(
        functools.partial(turn, 1),
        [near_blocks, near_every, near_ends, Raw(blocks)] + [wide_low] * 5 + [near_norms.array, shape(one_block)]
        + [low_block] * 3,
        [maps, v_blocks, v_blocks],
        start_offsets, got, mom0, table, Near(ends1), norms1, prm, Near(drive1), h1, Raw(full1), Halves(cot),
        scalars=1,
    )
    got = Near(every(ends_all))
    keep1, send1 = call(
        weight_grads, [vgo_half, vgo_half], [vgo_pack], sent1, dv, dg, states1, dml1, sums
    )
    got = Near(after(got.array, keep1))
    send1 = after(send1, got.array)
    got = Near(after(got.array, keep1))
    back_out, u1, prods, dlow = call(
        functools.partial(back_second, 1),
        [near_sums, near_blocks, shape((8, LANES)), wide_low],
        [v_blocks, one_map],
        start_offsets, got, mom0, table, Near(back_ends1), norms1, prm, Near(ds1), states1, cot, Halves(dml1),
        Halves(h1), Raw(input_map),
        scalars=1,
    )
    back1 = Near(every(back_out))
    late1 = (slow1, dlow, prods)
    mine1, other1 = pair_share(after(keep1, back_out), send1)
    back1 = Near(after(back1.array, mine1))
    far1 = hop(other1, 2)
    g0, ds0, ends_all, back_ends0, tile1, dv, dg, dml0, sums = call(
        functools.partial(back_first, 0, tokens),
        [blocks, near_blocks, near_every, near_ends, Near(shape((2 * parts, LANES)))] + [wide_low] * 3
        + [near_norms.array],
        [maps],
        start_offsets, back1, norms1, table, prm, Near(u1), norms0,
        Halves(slow1), Halves(sig0), Halves(part0), Halves(slope0), Halves(slow0), Raw(full0),
        scalars=1,
    )
    unit = 16 * count_dp
    in_piece, vgo_piece = (-(-n // unit) * 16 for n in (2 * in_rows, vgo_rows))

    def joined(order, *operands):
        piece = max(base + size for spans in order for _, size, base, _, _ in spans)
        out = Near(shape((count_dp, piece, width), BF16))
        return call(functools.partial(four_sum, order), [out], [], *map(Near, operands))[0]

    own1 = joined((((vgo_rows, vgo_piece, 0, 0, True),),), mine1, far1)
    got = Near(every(after(ends_all, far1)))
    keep0, send0 = call(
        functools.partial(both_grads, 0), [both_half, both_half], [both_pack] + in_room[1:],
        sent0, dv, dg, states0, dml0, sums, *late1, Raw(input_map),
    )
    pieces = lax.all_to_all(after(own1, got.array), "dp", 0, 0)
    (summed1,) = call(piece_sum, [Near(shape((vgo_piece, width), BF16))], [], Near(pieces))
    send0 = after(send0, got.array)
    got = Near(after(got.array, keep0))
    back_out, prods, dlow, *us = call(
        functools.partial(back_second, 0),
        [near_norms, Near(shape((8, LANES))), Near(wide_low), Near(shape(one_block))] + [near_low] * 3,
        [v_blocks, one_map, v_blocks],
        start_offsets, got, mom0, table, Near(back_ends0), norms0, prm, Near(ds0), states0, Halves(g0), Halves(dml0),
        Halves(h0), Raw(input_map),
        scalars=1,
    )
    mine0, other0 = pair_share(keep0, send0)
    far0 = hop(other0, 2)
    prods = after(prods, mine0)
    in_keep0, in_send0 = call(
        functools.partial(input_grads, 0), [in_half, in_half], in_room, slow0, Near(dlow), Near(prods), Near(back_out), Raw(input_map)
    )
    us = (us[0], *swap([after(u, in_send0) for u in us[1:]]))
    in_mine0, in_other0 = pair_share(in_keep0, in_send0)
    in_far0 = hop(in_other0, 2)

    order = (
        ((in_rows, in_piece, 0, 0, False),),
        ((vgo_rows, vgo_piece, in_piece, 0, True), (in_rows, in_piece, 0, in_rows, True)),
    )
    own0 = joined(order, in_mine0, in_far0, mine0, far0)
    pieces = lax.all_to_all(after(own0, summed1), "dp", 0, 0)
    first, rest = call(
        functools.partial(piece_sums, (in_piece, vgo_piece)),
        [Near(shape((count_dp, n, width), BF16)) for n in (in_piece, 2 * vgo_piece)],
        [],
        Near(pieces), Near(summed1),
    )
    result = [res[0], *swap([after(r, own0) for r in res[1:]])]
    (result,) = call(result_kernel, [shape((block, width))], [], res[0], *[Near(r) for r in result[1:]])
    full_in = lax.all_to_all(after(first, result, *us[1:]), "dp", 0, 0)
    stream_grad, gain_grad, shift_grad = call(
        functools.partial(last_kernel, tokens, in_piece),
        [shape((block, width)), shape((layers, width)), shape((layers, width))],
        [pltpu.VMEM((4,) + one_block, F32)],
        norms0, Near(full_in), Near(tile1), *[Near(u) for u in us], Raw(stream),
    )
    rest = after(rest, full_in)
    (input_grad,) = call(
        functools.partial(input_kernel, features, in_piece), [shape((layers, features, features))], [],
        Near(full_in), *[Near(x) for x in spread(full_in)],
    )
    full = lax.all_to_all(rest, "dp", 0, 0)
    full = after(full, input_grad, stream_grad)
    mat, vec, state = shape((layers, features, width)), shape((layers, width)), shape(decay_log.shape)
    o_grad, skip_grad, v_grad, g_grad, vb, gb, d_grad, p_grad, s_grad = call(
        functools.partial(hand_out, features, (in_piece, vgo_piece)),
        [mat, vec, mat, mat, vec, vec, state, state, state],
        [],
        decay_log, phase_log, Near(full_in), Near(full),
    )
    return (
        result, stream_grad, gain_grad, shift_grad, input_grad, d_grad, p_grad, s_grad,
        o_grad, skip_grad, v_grad, g_grad, vb, gb,
    )


def solution(mesh):
    split = P("dp", "mp")
    cols = P(None, "mp")
    wide = P(None, None, "mp")
    placed = (
        split, split, P("dp"), cols, cols, P(), P(), P(), P(), wide, cols, wide, wide, cols, cols,
    )
    return jax.shard_map(
        on_device,
        mesh=mesh,
        in_specs=placed,
        out_specs=(
            split, split, cols, cols, P(), P(), P(), P(), wide, cols, wide, wide, cols, cols,
        ),
        check_vma=False,
    )
```
